256 devices in a mesh: rep: 8 (over x, core), dom: 32 (over y, z).
Axes of the slice: x: 4, y: 4, z: 8, core: 2. Of those that a mesh axis runs over, the one named last changes fastest.
Arguments:
- coords: float32 [8, 3, 131072], P('rep', None, 'dom'), may hold values from -6 to 6
- atom_var: float32 [131072], P('dom'), may hold values from 0.2 to 1
- atom_weight: float32 [131072], P('dom'), may hold values from 0.5 to 2
- atoms_live: int32 [1024], P('dom'), may hold values from 1 to 128, 98304 in all
- block_list: int32 [1024, 16], P('dom'), may hold values from 0 to 2047, as said below
- owner_map: int32 [2048], replicated, may hold values from 0 to 2047, as said below
- comp_means: float32 [3, 262144], replicated, may hold values from -6 to 6
- comp_var: float32 [262144], replicated, may hold values from 0.3 to 1.5
- comp_weight: float32 [262144], replicated, may hold values from 0.1 to 1
- target: float32 [262144], P('dom'), may hold values from 0 to 2
- noise_sigma: float32 [262144], P('dom'), may hold values from 0.05 to 0.5
Outputs:
- intersection_avg: float32 [262144], P('dom')
- forces: float32 [8, 3, 131072], P('rep', None, 'dom')
The draws below stay inside these ranges and needn't reach their ends.
Inputs may be any that keep to these rules, and one draw needn't show every extreme that they name: `atoms_live`: entry a is the number of live atoms of atom block a, held in the first slots of the block. `owner_map`: A permutation of the component blocks. Storage position p lies on dom index p // 64. `block_list`: of the 32 x 16 entries of one dom index's atom blocks, at most 64 name blocks whose storage position lies on any one dom index, and in every draw some dom index receives exactly 64 entries from every dom index. An atom block may list a component block more than once; each entry counts.
All inputs are finite; a program needn't handle non-finite values.
Results may differ from the reference program's by a relative error of at most 0.0003.
Values sent between devices are 32-bit elements; how exact they have to be, the bound alone decides.
No kernel may reach another device: no remote copies, remote signals or barrier semaphores. Data moves between devices by JAX's collectives and lax.ppermute only.
A program may use at most 128 MiB of HBM per device.

```python
import math
import jax
import jax.numpy as jnp
import numpy as np
from jax import lax

NCOMP = 262144
ATOM_BLK = 128
COMP_BLK = 128
LISTED = 16
REPLICAS = 8
ATOMS = 131072
BLK_DEV = 32
ATOM_BLOCKS = 1024
COMP_BLOCKS = 2048
CAPACITY = 64
N_DOM = 32


def owner_table(key):
    return jax.random.permutation(jax.random.fold_in(key, 11), COMP_BLOCKS).astype(jnp.int32)


def draw_owner_map(key, part):
    return owner_table(key)


def draw_block_list(key, part):
    perm = owner_table(key)
    inverse = jnp.zeros((COMP_BLOCKS,), jnp.int32).at[perm].set(jnp.arange(COMP_BLOCKS, dtype=jnp.int32))
    per_owner = COMP_BLOCKS // N_DOM
    entries = BLK_DEV * LISTED
    base = jax.random.fold_in(key, 23)
    hottest = jax.random.randint(jax.random.fold_in(base, 1), (), 0, N_DOM).astype(jnp.int32)

    def one_domain(domain_key):
        first, second, third = jax.random.split(domain_key, 3)
        pool = jax.random.permutation(first, (N_DOM - 1) * CAPACITY)[:entries - CAPACITY].astype(jnp.int32)
        others = (hottest + 1 + pool // CAPACITY) % N_DOM
        chosen = jnp.concatenate([jnp.full((CAPACITY,), hottest, jnp.int32), others])
        chosen = jax.random.permutation(second, chosen)
        inside = jax.random.randint(third, (entries,), 0, per_owner).astype(jnp.int32)
        return inverse[chosen * per_owner + inside].reshape(BLK_DEV, LISTED)
    domain_keys = jax.random.split(jax.random.fold_in(base, 2), N_DOM)
    return jax.vmap(one_domain)(domain_keys).reshape(BLK_DEV * N_DOM, LISTED).astype(jnp.int32)


def shard_levels(stream_key, dims, shards, low, high):
    def one(axis_at, blocks):
        draws = jax.random.uniform(jax.random.fold_in(jax.random.fold_in(stream_key, 6), axis_at), (blocks,), jnp.float32, low / len(shards), high / len(shards))
        return jnp.repeat(jnp.exp(draws), dims[axis_at] // blocks).reshape((-1,) + (1,) * (len(dims) - axis_at - 1))

    level = one(*shards[0])
    for cut in shards[1:]:
        level = level * one(*cut)
    return level


def split_up(count, total, reach, lean):
    loads = [(1 << 20) // math.isqrt(grade ** lean) + 1 for grade in range(2, count + 1)]
    spare, given = total - reach - (count - 1), [1] * (count - 1)
    while spare > 0:
        free = [i for i in range(count - 1) if given[i] < reach]
        mass, left = sum([loads[i] for i in free]), spare
        for i in free:
            more = min(reach - given[i], max(1, left * loads[i] // mass), spare)
            given[i] = given[i] + more
            spare = spare - more
    return np.array([reach] + given)


def uneven_parts(rng, number_of, total, limit, skew):
    if number_of == 2:
        one = jax.random.randint(rng, (), max(1, total - limit), min(limit, total - 1) + 1)
        return jnp.stack([one, total - one])
    tallies = jnp.asarray(split_up(number_of, total, limit, skew), jnp.int32)
    pairs = (number_of - 1) // 2
    source_of, receiver = tallies[1:1 + 2 * pairs:2], tallies[2:2 + 2 * pairs:2]
    room = jnp.minimum(source_of - 1, limit - receiver)
    passed = jax.random.randint(jax.random.fold_in(rng, 1), (pairs,), 0, 1 << 20) % (room + 1)
    tallies = tallies.at[1:1 + 2 * pairs:2].set(source_of - passed).at[2:2 + 2 * pairs:2].set(receiver + passed)
    return tallies[jax.random.permutation(jax.random.fold_in(rng, 2), number_of)]


def normal_values(key, dims, deviation, bound, pieces=(), held_as=jnp.bfloat16):
    drawn = deviation * jax.random.normal(key, dims, jnp.float32)
    if pieces:
        drawn = drawn * shard_levels(key, dims, pieces, -0.22, 0.18)
    return jnp.clip(drawn, -bound, bound).astype(held_as)


def setup_inputs(seed: int = 0) -> dict:
    key_list = jax.random.split(jax.random.key(seed), 12)
    return {
        "coords": normal_values(key_list[0], (REPLICAS, 3, ATOMS), 1.0, 6.0, ((0, 8), (2, 32)), jnp.float32),
        "atom_var": jnp.clip(jnp.exp(math.log(1.0) - 1.609438 * jax.random.uniform(key_list[1], (ATOMS,), jnp.float32) ** shard_levels(key_list[1], (ATOMS,), ((0, 32),), -0.2, 0.2)), 0.2, 1.0),
        "atom_weight": jnp.clip(0.5 + 1.5 * jax.random.uniform(key_list[2], (ATOMS,), jnp.float32) ** shard_levels(key_list[2], (ATOMS,), ((0, 32),), -0.2, 0.2), 0.5, 2.0),
        "atoms_live": uneven_parts(key_list[3], ATOM_BLOCKS, ATOM_BLOCKS * ATOM_BLK * 3 // 4, ATOM_BLK, 0).astype(jnp.int32),
        "block_list": draw_block_list(jax.random.fold_in(key_list[11], 71), 0),
        "owner_map": draw_owner_map(jax.random.fold_in(key_list[11], 71), 0),
        "comp_means": normal_values(key_list[6], (3, NCOMP), 1.0, 6.0, (), jnp.float32),
        "comp_var": jnp.clip(jnp.exp(jax.random.uniform(key_list[7], (NCOMP,), jnp.float32, math.log(0.3), math.log(1.5))), 0.3, 1.5),
        "comp_weight": jnp.clip(jnp.exp(jax.random.uniform(key_list[8], (NCOMP,), jnp.float32, math.log(0.1), math.log(1.0))), 0.1, 1.0),
        "target": jnp.clip(2.0 * jax.random.uniform(key_list[9], (NCOMP,), jnp.float32) ** shard_levels(key_list[9], (NCOMP,), ((0, 32),), -0.2, 0.2), 0.0, 2.0),
        "noise_sigma": jnp.clip(jnp.exp(math.log(0.5) - 2.3025851 * jax.random.uniform(key_list[10], (NCOMP,), jnp.float32) ** shard_levels(key_list[10], (NCOMP,), ((0, 32),), -0.2, 0.2)), 0.05, 0.5),
    }


full_turn = 2.0 * math.pi
energy_unit = 2.494


def intersection_tile(positions, variances, weights, centers, center_var, center_weight):
    offsets = positions[:, None, :, None] - centers[:, :, None, :]
    squared = jnp.sum(offsets * offsets, axis=0)
    widths = variances[None, :, None] + center_var[:, None, :]
    prefactor = weights[None, :, None] * center_weight[:, None, :]
    intersection = prefactor * (full_turn * widths) ** -1.5 * jnp.exp(-0.5 * squared / widths)
    return offsets, widths, intersection


def reference(coords, atom_var, atom_weight, atoms_live, block_list, owner_map, comp_means, comp_var, comp_weight, target, noise_sigma):
    blocks = block_list.shape[0]
    replicas = coords.shape[0]
    slot_index = jnp.arange(ATOM_BLK, dtype=jnp.int32)
    live_mask = (slot_index[None, :] < atoms_live[:, None]).astype(atom_weight.dtype)
    positions = coords.reshape(replicas, 3, blocks, ATOM_BLK).transpose(2, 0, 1, 3)
    variances = atom_var.reshape(blocks, ATOM_BLK)
    weights = atom_weight.reshape(blocks, ATOM_BLK) * live_mask
    centers = comp_means.reshape(3, COMP_BLOCKS, COMP_BLK)
    center_var = comp_var.reshape(COMP_BLOCKS, COMP_BLK)
    center_weight = comp_weight.reshape(COMP_BLOCKS, COMP_BLK)
    tiled = jax.vmap(intersection_tile, in_axes=(0, None, None, None, None, None))

    def partial_of(inputs):
        coord_tile, var_tile, weight_tile, blocks_of = inputs
        offsets, widths, intersection = tiled(coord_tile, var_tile, weight_tile, centers[:, blocks_of], center_var[blocks_of], center_weight[blocks_of])
        return jnp.sum(intersection, axis=2)

    inputs = (positions, variances, weights, block_list)
    partials = lax.map(partial_of, inputs)
    flattened = partials.transpose(0, 2, 1, 3).reshape(blocks * LISTED, replicas, COMP_BLK)
    summed = jax.ops.segment_sum(flattened, block_list.reshape(-1), num_segments=COMP_BLOCKS)
    mean_logical = jnp.sum(summed, axis=1) / replicas
    intersection_avg = jnp.zeros_like(mean_logical).at[owner_map].set(mean_logical).reshape(-1)
    wanted = target.reshape(COMP_BLOCKS, COMP_BLK)[owner_map]
    sigmas = noise_sigma.reshape(COMP_BLOCKS, COMP_BLK)[owner_map]
    misfit = mean_logical - wanted
    adjoint = misfit / (sigmas * sigmas + 0.5 * misfit * misfit) / replicas

    def force_of(inputs):
        coord_tile, var_tile, weight_tile, blocks_of = inputs
        offsets, widths, intersection = tiled(coord_tile, var_tile, weight_tile, centers[:, blocks_of], center_var[blocks_of], center_weight[blocks_of])
        weight = adjoint[blocks_of][None, :, None, :] * (intersection / widths)
        return energy_unit * jnp.sum(weight[:, None] * offsets, axis=(2, 4))

    forces = lax.map(force_of, inputs)
    forces = forces.transpose(1, 2, 0, 3).reshape(replicas, 3, blocks * ATOM_BLK)
    return intersection_avg, forces
```

```python
import functools
import math

import jax
import jax.numpy as jnp
from jax import lax
from jax.experimental import pallas as pl
from jax.experimental.pallas import tpu as pltpu
from jax.sharding import PartitionSpec as P

ATOM_BLK = 128
COMP_BLK = 128
LISTED = 16
BLK_DEV = 32
COMP_BLOCKS = 2048
CHUNK = 32
FEATS = 48

ENERGY_UNIT = 2.494
EXP_SCALE = -0.5 / math.log(2.0)
NORM = (2.0 * math.pi) ** -1.5


def split3(v):
    hi = v.astype(jnp.bfloat16).astype(jnp.float32)
    rest = v - hi
    mid = rest.astype(jnp.bfloat16).astype(jnp.float32)
    low = (rest - mid).astype(jnp.bfloat16).astype(jnp.float32)
    return hi, mid, low


def choose(row, parts, shape):
    out = jnp.zeros(shape, jnp.float32)
    for k, part in enumerate(parts):
        out = jnp.where(row == k, part, out)
    return out


def overlap_kernel(
    live_ref, list_ref, owner_ref, coords_ref, var_ref, weight_ref, means_ref, cvar_ref, cweight_ref,
    model_ref, ratio_ref,
    left_ref, right_ref, var_lane, weight_lane, comp_rows,
):
    shape = (8, 128)
    row = lax.broadcasted_iota(jnp.int32, shape, 0)
    lane = lax.broadcasted_iota(jnp.int32, (1, 128), 1)
    model_ref[...] = jnp.zeros_like(model_ref)

    def block(a, _):
        at = pl.ds(pl.multiple_of(a * 128, 128), 128)
        live = live_ref[a]
        x, y, z = (coords_ref[0, d : d + 1, at] for d in range(3))
        norm2 = EXP_SCALE * (x * x + y * y + z * z)
        feats = choose(row, (x, y, z, jnp.float32(1.0), norm2), shape)
        hi, mid, low = split3(feats)
        weight = jnp.where(lane < live, weight_ref[pl.ds(a, 1), :], 0.0)
        extra = choose(row, (var_ref[pl.ds(a, 1), :], weight), shape)
        turned = jnp.concatenate([hi, mid, low, hi, mid, hi, extra], axis=0).T
        left_ref[...] = turned[:, :FEATS].astype(jnp.bfloat16)
        var_lane[...] = jnp.broadcast_to(turned[:, FEATS : FEATS + 1], (128, 128))
        weight_lane[...] = jnp.broadcast_to(turned[:, FEATS + 1 : FEATS + 2], (128, 128))

        for k in range(LISTED):
            b = list_ref[a, k]
            cols = pl.ds(pl.multiple_of(b * 128, 128), 128)
            cx, cy, cz = (means_ref[d : d + 1, cols] for d in range(3))
            cnorm = EXP_SCALE * (cx * cx + cy * cy + cz * cz)
            t = -2.0 * EXP_SCALE
            comp = choose(row, (t * cx, t * cy, t * cz, cnorm, jnp.float32(1.0)), shape)
            hi, mid, low = split3(comp)
            right_ref[:, k * 128 : (k + 1) * 128] = jnp.concatenate([hi, hi, hi, mid, mid, low], axis=0).astype(jnp.bfloat16)
            comp_rows[k] = jnp.broadcast_to(cvar_ref[pl.ds(b, 1), :], shape)

        def chunk(c, sums):
            rows = pl.ds(pl.multiple_of(c * CHUNK, CHUNK), CHUNK)
            left = left_ref[rows, :]
            va = var_lane[rows, :]
            wa = weight_lane[rows, :]
            out = []
            for k in range(LISTED):
                scaled = jnp.dot(left, right_ref[:, k * 128 : (k + 1) * 128], preferred_element_type=jnp.float32)
                vc = comp_rows[k]
                v = va.reshape(CHUNK // 8, 8, 128) + vc[None]
                r = lax.rsqrt(v)
                q = r * r
                p = jnp.exp2(scaled.reshape(CHUNK // 8, 8, 128) * q)
                t = (q * r) * p
                ratio_ref[a, rows, k * 128 : (k + 1) * 128] = (t * q).reshape(CHUNK, 128)
                out.append(sums[k] + jnp.sum(t * wa.reshape(CHUNK // 8, 8, 128), axis=0))
            return tuple(out)

        zero = jnp.zeros(shape, jnp.float32)
        sums = lax.fori_loop(0, (live + CHUNK - 1) // CHUNK, chunk, (zero,) * LISTED)
        for k in range(LISTED):
            b = list_ref[a, k]
            place = owner_ref[b]
            target = ((place & 56) << 5) + ((place >> 6) << 3) + (place & 7)
            total = NORM * jnp.sum(sums[k], axis=0, keepdims=True) * cweight_ref[pl.ds(b, 1), :]
            model_ref[pl.ds(target, 1), :] += total
        return 0

    lax.fori_loop(0, BLK_DEV, block, 0)


def force_kernel(
    live_ref, list_ref, owner_ref, coords_ref, weight_ref, means_ref, cweight_ref, adjoint_ref, ratio_ref,
    force_ref,
    right_ref, sums_ref,
):
    shape = (8, 128)
    row = lax.broadcasted_iota(jnp.int32, shape, 0)
    lane = lax.broadcasted_iota(jnp.int32, (1, 128), 1)
    sums_ref[...] = jnp.zeros_like(sums_ref)

    def block(a, _):
        at = pl.ds(pl.multiple_of(a * 128, 128), 128)
        live = live_ref[a]
        for k in range(LISTED):
            b = list_ref[a, k]
            place = owner_ref[b]
            target = (place & 56) * 33 + ((place >> 6) << 3) + (place & 7)
            cols = pl.ds(pl.multiple_of(b * 128, 128), 128)
            cx, cy, cz = (means_ref[d : d + 1, cols] for d in range(3))
            pull = (ENERGY_UNIT * NORM) * adjoint_ref[pl.ds(target, 1), :] * cweight_ref[pl.ds(b, 1), :]
            comp = choose(row, (pull * cx, pull * cy, pull * cz, pull), shape)
            hi, mid, low = split3(comp)
            right_ref[:, k * 128 : (k + 1) * 128] = jnp.concatenate([hi, mid, low, jnp.zeros_like(hi)], axis=0).astype(jnp.bfloat16)

        def chunk(c, _):
            rows = pl.ds(pl.multiple_of(c * CHUNK, CHUNK), CHUNK)
            ratio = ratio_ref[a, rows, :]
            hi = ratio.astype(jnp.bfloat16)
            low = (ratio - hi.astype(jnp.float32)).astype(jnp.bfloat16)
            right = right_ref[...]
            dims = (((1,), (1,)), ((), ()))
            sums_ref[rows, 0:32] = lax.dot_general(
                hi, right, dims, preferred_element_type=jnp.float32
            ) + lax.dot_general(low, right, dims, preferred_element_type=jnp.float32)
            return 0

        lax.fori_loop(0, (live + CHUNK - 1) // CHUNK, chunk, 0)
        turned = sums_ref[...].T
        got = turned[0:8] + turned[8:16] + turned[16:24]
        weight = jnp.where(lane < live, weight_ref[pl.ds(a, 1), :], 0.0)
        for d in range(3):
            force_ref[0, d : d + 1, at] = weight * (coords_ref[0, d : d + 1, at] * got[3:4] - got[d : d + 1])
        return 0

    lax.fori_loop(0, BLK_DEV, block, 0)


def shards(
    coords, atom_var, atom_weight, atoms_live, block_list, owner_map, comp_means, comp_var, comp_weight, target, noise_sigma,
):
    replicas = lax.axis_size("rep")
    domains = lax.axis_size("dom")
    share = COMP_BLOCKS // domains // replicas
    smem = pl.BlockSpec(memory_space=pltpu.SMEM)
    vmem = pl.BlockSpec(memory_space=pltpu.VMEM)
    variances = atom_var.reshape(BLK_DEV, ATOM_BLK)
    weights = atom_weight.reshape(BLK_DEV, ATOM_BLK)
    cvar = comp_var.reshape(COMP_BLOCKS, COMP_BLK)
    cweight = comp_weight.reshape(COMP_BLOCKS, COMP_BLK)
    model, ratio = pl.pallas_call(
        overlap_kernel,
        out_shape=(
            jax.ShapeDtypeStruct((COMP_BLOCKS, COMP_BLK), jnp.float32),
            pltpu.VMEM((BLK_DEV, ATOM_BLK, LISTED * COMP_BLK), jnp.float32),
        ),
        in_specs=[smem] * 3 + [vmem] * 6,
        out_specs=(vmem, vmem),
        scratch_shapes=[
            pltpu.VMEM((ATOM_BLK, FEATS), jnp.bfloat16),
            pltpu.VMEM((FEATS, LISTED * COMP_BLK), jnp.bfloat16),
            pltpu.VMEM((128, 128), jnp.float32),
            pltpu.VMEM((128, 128), jnp.float32),
            pltpu.VMEM((LISTED, 8, 128), jnp.float32),
        ],
        compiler_params=pltpu.CompilerParams(vmem_limit_bytes=16 << 20),
        name="overlap",
    )(atoms_live, block_list, owner_map, coords, variances, weights, comp_means, cvar, cweight)

    parts = lax.all_to_all(model.reshape(replicas, domains * share, COMP_BLK), "rep", 0, 0, tiled=True)
    over_rep = jnp.sum(parts, axis=0)
    parts = lax.all_to_all(over_rep.reshape(domains, share, COMP_BLK), "dom", 0, 0, tiled=True)
    mean = jnp.sum(parts, axis=0) / replicas
    first = lax.axis_index("rep") * share
    wanted = lax.dynamic_slice(target.reshape(-1, COMP_BLK), (first, 0), (share, COMP_BLK))
    sigmas = lax.dynamic_slice(noise_sigma.reshape(-1, COMP_BLK), (first, 0), (share, COMP_BLK))
    misfit = mean - wanted
    adjoint = misfit / (sigmas * sigmas + 0.5 * misfit * misfit) / replicas
    spread = jnp.broadcast_to(adjoint[None], (domains, share, COMP_BLK))
    over_dom = lax.all_to_all(spread, "dom", 0, 0, tiled=True).reshape(domains * share, COMP_BLK)
    back = jnp.concatenate([over_dom, mean], axis=0)
    spread = jnp.broadcast_to(back[None], (replicas,) + back.shape)
    returned = lax.all_to_all(spread, "rep", 0, 0, tiled=True)
    average = returned[:, domains * share :].reshape(-1)
    returned = returned.reshape(-1, COMP_BLK)

    forces = pl.pallas_call(
        force_kernel,
        out_shape=jax.ShapeDtypeStruct(coords.shape, jnp.float32),
        in_specs=[smem] * 3 + [vmem] * 6,
        out_specs=vmem,
        scratch_shapes=[
            pltpu.VMEM((32, LISTED * COMP_BLK), jnp.bfloat16),
            pltpu.VMEM((128, 128), jnp.float32),
        ],
        compiler_params=pltpu.CompilerParams(vmem_limit_bytes=16 << 20),
        name="force",
    )(
        atoms_live, block_list, owner_map, coords, weights, comp_means, cweight, returned,
        pltpu.with_memory_space_constraint(ratio, pltpu.VMEM),
    )
    return average, forces


def solution(mesh):
    return jax.shard_map(
        shards,
        mesh=mesh,
        in_specs=(
            P("rep", None, "dom"), P("dom"), P("dom"), P("dom"), P("dom", None), P(), P(), P(), P(), P("dom"), P("dom"),
        ),
        out_specs=(P("dom"), P("rep", None, "dom")),
        check_vma=False,
    )
```

```python
import functools
import math

import jax
import jax.numpy as jnp
from jax import lax
from jax.experimental import pallas as pl
from jax.experimental.pallas import tpu as pltpu
from jax.sharding import PartitionSpec as P

ATOM_BLK = 128
COMP_BLK = 128
LISTED = 16
BLK_DEV = 32
COMP_BLOCKS = 2048
REPLICAS = 8
DEAD = 1e30

ENERGY_UNIT = 2.494
EXP_SCALE = -0.5 / math.log(2.0)
NORM = (2.0 * math.pi) ** -1.5


def split3(v):
    hi = v.astype(jnp.bfloat16).astype(jnp.float32)
    rest = v - hi
    mid = rest.astype(jnp.bfloat16).astype(jnp.float32)
    return hi, mid, rest - mid


def atom_scale(weight, live, dead):
    return jnp.where(live, jnp.exp2(jnp.log(weight) * (-2.0 / (3.0 * math.log(2.0)))), dead)


def choose(row, parts, shape, other=0.0):
    out = jnp.full(shape, other, jnp.float32)
    for k, part in enumerate(parts):
        out = jnp.where(row == k, part, out)
    return out


def overlap_kernel(
    live_any, list_any, owner_any, coords_any, var_any, weight_any, means_any, cvar_any, cweight_any,
    model_ref, ratio_ref,
    live_ref, list_ref, owner_ref, coords_ref, var_ref, weight_ref, means_ref, cvar_ref, cweight_ref, sems,
    ratio_buf, ratio_sems,
):
    pairs = (
        (live_any, live_ref), (list_any, list_ref), (owner_any, owner_ref), (coords_any, coords_ref),
        (var_any, var_ref), (weight_any, weight_ref), (means_any, means_ref), (cvar_any, cvar_ref),
        (cweight_any, cweight_ref),
    )
    copies = [pltpu.make_async_copy(src, dst, sems.at[n]) for n, (src, dst) in enumerate(pairs)]
    for copy in copies:
        copy.start()
    shape = (8, 128)
    row = lax.broadcasted_iota(jnp.int32, shape, 0)
    lane = lax.broadcasted_iota(jnp.int32, (1, 128), 1)
    for_distance = ((row < 4) | (row == 5)).astype(jnp.float32)
    for_variance = ((row == 4) | (row == 6)).astype(jnp.float32)
    model_ref[...] = jnp.zeros_like(model_ref)
    for copy in copies:
        copy.wait()

    def store(a):
        slot = a & 1
        return pltpu.make_async_copy(ratio_buf.at[slot], ratio_ref.at[a], ratio_sems.at[slot])

    def block(a, _):
        live = live_ref[a]
        slot = a & 1

        @pl.when(a >= 2)
        def _():
            store(a - 2).wait()

        x, y, z = (coords_ref[pl.ds(d * BLK_DEV + a, 1), :] for d in range(3))
        scale = atom_scale(weight_ref[pl.ds(a, 1), :], lane < live, DEAD)
        norm2 = EXP_SCALE * (x * x + y * y + z * z)
        t = -2.0 * EXP_SCALE
        feats = scale * choose(row, (t * x, t * y, t * z, EXP_SCALE, 1.0, norm2, var_ref[pl.ds(a, 1), :]), shape)
        hi, mid, low = split3(feats)
        left = jnp.concatenate([hi, mid, low, hi, mid, hi], axis=0).T.astype(jnp.bfloat16)

        for k in range(LISTED):
            b = list_ref[k, a]
            cols = pl.ds(pl.multiple_of(b * 128, 128), 128)
            cx, cy, cz = (means_ref[d : d + 1, cols] for d in range(3))
            cnorm = cx * cx + cy * cy + cz * cz
            comp = choose(row, (cx, cy, cz, cnorm, cvar_ref[pl.ds(b, 1), :]), shape, 1.0)
            sides = []
            hi, mid, low = split3(comp)
            for mask in (for_distance, for_variance):
                h, m, w = hi * mask, mid * mask, low * mask
                sides.append(jnp.concatenate([h, h, h, m, m, w], axis=0).astype(jnp.bfloat16))
            right = jnp.concatenate(sides, axis=1)
            both = jnp.dot(left, right, preferred_element_type=jnp.float32).reshape(16, 8, 256)
            r = lax.rsqrt(both[:, :, 128:])
            q = r * r
            t = (q * r) * jnp.exp2(both[:, :, :128] * q)
            ratio_buf[slot, :, k * 128 : (k + 1) * 128] = (t * q).reshape(128, 128)
            total = jnp.sum(jnp.sum(t, axis=0), axis=0, keepdims=True)
            place = owner_ref[b]
            target = ((place & 56) << 5) + ((place >> 6) << 3) + (place & 7)
            model_ref[pl.ds(target, 1), :] += NORM * total * cweight_ref[pl.ds(b, 1), :]
        store(a).start()
        return 0

    lax.fori_loop(0, BLK_DEV, block, 0)
    store(BLK_DEV - 2).wait()
    store(BLK_DEV - 1).wait()


def in_hbm(array):
    return pltpu.with_memory_space_constraint(array, pltpu.HBM)


def rep_sum_kernel(parts_ref, out_ref):
    out_ref[...] = jnp.sum(parts_ref[...], axis=0)


def adjoint_kernel(parts_ref, target_ref, sigma_ref, spread_ref, mean_ref):
    share = mean_ref.shape[0]
    mean = jnp.sum(parts_ref[...], axis=0) / REPLICAS
    first = pl.ds(pl.multiple_of(lax.axis_index("rep") * share, share), share)
    sigma = sigma_ref[first, :]
    misfit = mean - target_ref[first, :]
    adjoint = misfit / (sigma * sigma + 0.5 * misfit * misfit) / REPLICAS
    mean_ref[...] = mean
    spread_ref[...] = jnp.broadcast_to(adjoint[None], spread_ref.shape)


def spread_kernel(adjoint_ref, mean_ref, out_ref):
    rows = adjoint_ref.shape[0]
    for r in range(REPLICAS):
        out_ref[r, :rows] = adjoint_ref[...]
        out_ref[r, rows:] = mean_ref[...]


def force_kernel(
    live_ref, list_ref, owner_ref, coords_ref, weight_ref, means_ref, cweight_ref, adjoint_ref, ratio_any,
    force_ref,
    ratio_ref, ratio_sems,
):
    depth = ratio_ref.shape[0]

    def load(a):
        slot = lax.rem(a, depth)
        return pltpu.make_async_copy(ratio_any.at[a], ratio_ref.at[slot], ratio_sems.at[slot])

    for first in range(depth - 1):
        load(jnp.int32(first)).start()

    shape = (8, 128)
    row = lax.broadcasted_iota(jnp.int32, shape, 0)
    upper = row < 4
    lane = lax.broadcasted_iota(jnp.int32, (1, 128), 1)

    def block(a, _):
        @pl.when(a + depth - 1 < BLK_DEV)
        def _():
            load(a + depth - 1).start()

        live = live_ref[a]
        rights = []
        for k in range(LISTED):
            b = list_ref[k, a]
            place = owner_ref[b]
            target = (place & 56) * 33 + ((place >> 6) << 3) + (place & 7)
            cols = pl.ds(pl.multiple_of(b * 128, 128), 128)
            cx, cy, cz = (means_ref[d : d + 1, cols] for d in range(3))
            pull = (ENERGY_UNIT * NORM) * adjoint_ref[pl.ds(target, 1), :] * cweight_ref[pl.ds(b, 1), :]
            hi, mid, low = split3(pull * choose(row & 3, (cx, cy, cz, 1.0), shape))
            rights.append(
                jnp.concatenate([jnp.where(upper, hi, mid), jnp.where(upper, low, 0.0)], axis=0).astype(jnp.bfloat16)
            )
        load(a).wait()
        slot = lax.rem(a, depth)
        total = jnp.zeros((128, 16), jnp.float32)
        dims = (((1,), (1,)), ((), ()))
        for k in range(0, LISTED, 2):
            right = jnp.concatenate(rights[k : k + 2], axis=1)
            ratio = ratio_ref[slot, :, k * 128 : (k + 2) * 128]
            hi = ratio.astype(jnp.bfloat16)
            low = (ratio - hi.astype(jnp.float32)).astype(jnp.bfloat16)
            total += lax.dot_general(hi, right, dims, preferred_element_type=jnp.float32)
            total += lax.dot_general(low, right, dims, preferred_element_type=jnp.float32)
        turned = total.T
        got = turned[0:8] + turned[8:16]
        got = got[0:4] + got[4:8]
        scale = atom_scale(weight_ref[pl.ds(a, 1), :], lane < live, 0.0)
        for d in range(3):
            at = pl.ds(d * BLK_DEV + a, 1)
            force_ref[at, :] = scale * (coords_ref[at, :] * got[3:4] - got[d : d + 1])
        return 0

    lax.fori_loop(0, BLK_DEV, block, 0)


def shards(
    coords, atom_var, atom_weight, atoms_live, block_list, owner_map, comp_means, comp_var, comp_weight, target, noise_sigma,
):
    replicas = lax.axis_size("rep")
    domains = lax.axis_size("dom")
    share = COMP_BLOCKS // domains // replicas
    smem = pl.BlockSpec(memory_space=pltpu.SMEM)
    vmem = pl.BlockSpec(memory_space=pltpu.VMEM)
    hbm = pl.BlockSpec(memory_space=pltpu.HBM)
    small = pltpu.CompilerParams(vmem_limit_bytes=6 << 20)
    f32 = jnp.float32
    positions = coords.reshape(3 * BLK_DEV, ATOM_BLK)
    listed = block_list.T
    variances = atom_var.reshape(BLK_DEV, ATOM_BLK)
    weights = atom_weight.reshape(BLK_DEV, ATOM_BLK)
    cvar = comp_var.reshape(COMP_BLOCKS, COMP_BLK)
    cweight = comp_weight.reshape(COMP_BLOCKS, COMP_BLK)
    model, ratio = pl.pallas_call(
        overlap_kernel,
        out_shape=(
            jax.ShapeDtypeStruct((COMP_BLOCKS, COMP_BLK), f32),
            pltpu.HBM((BLK_DEV, ATOM_BLK, LISTED * COMP_BLK), f32),
        ),
        in_specs=[hbm] * 9,
        out_specs=(vmem, hbm),
        scratch_shapes=[
            pltpu.SMEM((BLK_DEV,), jnp.int32),
            pltpu.SMEM((LISTED, BLK_DEV), jnp.int32),
            pltpu.SMEM((COMP_BLOCKS,), jnp.int32),
            pltpu.VMEM((3 * BLK_DEV, ATOM_BLK), f32),
            pltpu.VMEM((BLK_DEV, ATOM_BLK), f32),
            pltpu.VMEM((BLK_DEV, ATOM_BLK), f32),
            pltpu.VMEM((3, COMP_BLOCKS * COMP_BLK), f32),
            pltpu.VMEM((COMP_BLOCKS, COMP_BLK), f32),
            pltpu.VMEM((COMP_BLOCKS, COMP_BLK), f32),
            pltpu.SemaphoreType.DMA((9,)),
            pltpu.VMEM((2, ATOM_BLK, LISTED * COMP_BLK), f32),
            pltpu.SemaphoreType.DMA((2,)),
        ],
        compiler_params=pltpu.CompilerParams(vmem_limit_bytes=16 << 20),
        name="overlap",
    )(*(in_hbm(v) for v in (atoms_live, listed, owner_map, positions, variances, weights, comp_means, cvar, cweight)))

    parts = lax.all_to_all(model.reshape(replicas, domains * share, COMP_BLK), "rep", 0, 0, tiled=True)
    over_rep = pl.pallas_call(
        rep_sum_kernel,
        out_shape=jax.ShapeDtypeStruct((domains * share, COMP_BLK), f32),
        in_specs=[vmem], out_specs=vmem, compiler_params=small, name="rep_sum",
    )(parts)
    parts = lax.all_to_all(over_rep.reshape(domains, share, COMP_BLK), "dom", 0, 0, tiled=True)
    spread, mean = pl.pallas_call(
        adjoint_kernel,
        out_shape=(
            jax.ShapeDtypeStruct((domains, share, COMP_BLK), f32), jax.ShapeDtypeStruct((share, COMP_BLK), f32),
        ),
        in_specs=[vmem] * 3, out_specs=(vmem, vmem), compiler_params=small, name="adjoint",
    )(parts, target.reshape(-1, COMP_BLK), noise_sigma.reshape(-1, COMP_BLK))
    over_dom = lax.all_to_all(spread, "dom", 0, 0, tiled=True).reshape(domains * share, COMP_BLK)
    spread = pl.pallas_call(
        spread_kernel,
        out_shape=jax.ShapeDtypeStruct((replicas, (domains + 1) * share, COMP_BLK), f32),
        in_specs=[vmem] * 2, out_specs=vmem, compiler_params=small, name="spread",
    )(over_dom, mean)
    returned = lax.all_to_all(spread, "rep", 0, 0, tiled=True)
    average = returned[:, domains * share :].reshape(-1)
    returned = returned.reshape(-1, COMP_BLK)

    forces = pl.pallas_call(
        force_kernel,
        out_shape=jax.ShapeDtypeStruct(positions.shape, f32),
        in_specs=[smem] * 3 + [vmem] * 5 + [hbm],
        out_specs=vmem,
        scratch_shapes=[
            pltpu.VMEM((4, ATOM_BLK, LISTED * COMP_BLK), f32),
            pltpu.SemaphoreType.DMA((4,)),
        ],
        compiler_params=pltpu.CompilerParams(vmem_limit_bytes=16 << 20),
        name="force",
    )(
        atoms_live, listed, owner_map, positions, weights, comp_means, cweight, returned,
        in_hbm(ratio),
    )
    return average, forces.reshape(coords.shape)


def solution(mesh):
    return jax.shard_map(
        shards,
        mesh=mesh,
        in_specs=(
            P("rep", None, "dom"), P("dom"), P("dom"), P("dom"), P("dom", None), P(), P(), P(), P(), P("dom"), P("dom"),
        ),
        out_specs=(P("dom"), P("rep", None, "dom")),
        check_vma=False,
    )
```

```python
import functools
import math

import jax
import jax.numpy as jnp
from jax import lax
from jax.experimental import pallas as pl
from jax.experimental.pallas import tpu as pltpu
from jax.sharding import PartitionSpec as P

ATOM_BLK = 128
COMP_BLK = 128
LISTED = 16
BLK_DEV = 32
COMP_BLOCKS = 2048
REPLICAS = 8
FEATS = 48
PART = 8

ENERGY_UNIT = 2.494
EXP_SCALE = -0.5 / math.log(2.0)
NORM = (2.0 * math.pi) ** -1.5


def split3(v):
    hi = v.astype(jnp.bfloat16).astype(jnp.float32)
    rest = v - hi
    mid = rest.astype(jnp.bfloat16).astype(jnp.float32)
    return hi, mid, rest - mid


def choose(row, parts, shape, other=0.0):
    out = jnp.full(shape, other, jnp.float32)
    for k, part in enumerate(parts):
        out = jnp.where(row == k, part, out)
    return out


def right_side(comp):
    hi, mid, low = split3(comp)
    return jnp.concatenate([hi, hi, hi, mid, mid, low], axis=0).astype(jnp.bfloat16)


def spread_lanes(atoms, column):
    return jnp.broadcast_to(atoms[:, column : column + 1], (128, 128)).reshape(16, 8, 128)


def pair_terms(left, spread_var, comp_of):
    for k in range(0, LISTED, 2):
        comps = [comp_of(k), comp_of(k + 1)]
        right = jnp.concatenate([right_side(comp) for comp in comps], axis=1)
        scaled = jnp.dot(left, right, preferred_element_type=jnp.float32).reshape(16, 8, 256)
        for n in range(2):
            r = lax.rsqrt(spread_var + comps[n][5:6].reshape(1, 1, 128))
            q = r * r
            yield k + n, q, (q * r) * jnp.exp2(scaled[:, :, n * 128 : (n + 1) * 128] * q)


def overlap_kernel(
    live_any, list_any, owner_any, coords_any, var_any, weight_any, means_any, cvar_any, cweight_any,
    model_ref, comps_ref, atoms_ref,
    live_ref, list_ref, owner_ref, coords_ref, var_ref, weight_ref, means_ref, cvar_ref, cweight_ref, sems,
):
    pairs = (
        (live_any, live_ref), (list_any, list_ref), (owner_any, owner_ref), (coords_any, coords_ref),
        (var_any, var_ref), (weight_any, weight_ref), (means_any, means_ref), (cvar_any, cvar_ref),
        (cweight_any, cweight_ref),
    )
    copies = [pltpu.make_async_copy(src, dst, sems.at[n]) for n, (src, dst) in enumerate(pairs)]
    for copy in copies:
        copy.start()
    shape = (8, 128)
    row = lax.broadcasted_iota(jnp.int32, shape, 0)
    lane = lax.broadcasted_iota(jnp.int32, (1, 128), 1)
    model_ref[...] = jnp.zeros_like(model_ref)
    for copy in copies:
        copy.wait()

    def block(a, _):
        x, y, z = (coords_ref[pl.ds(d * BLK_DEV + a, 1), :] for d in range(3))
        norm2 = EXP_SCALE * (x * x + y * y + z * z)
        t = -2.0 * EXP_SCALE
        hi, mid, low = split3(choose(row, (t * x, t * y, t * z, EXP_SCALE, norm2), shape))
        weight = jnp.where(lane < live_ref[a], weight_ref[pl.ds(a, 1), :], 0.0)
        extra = choose(row, (var_ref[pl.ds(a, 1), :], weight), shape)
        feats = jnp.concatenate([hi, mid, low, hi, mid, hi, extra], axis=0)
        atoms_ref[a] = feats
        atoms = feats.T
        left = atoms[:, :FEATS].astype(jnp.bfloat16)
        spread_var = spread_lanes(atoms, FEATS)
        spread_weight = spread_lanes(atoms, FEATS + 1)

        def comp_of(k):
            b = list_ref[k, a]
            cols = pl.ds(pl.multiple_of(b * 128, 128), 128)
            cx, cy, cz = (means_ref[d : d + 1, cols] for d in range(3))
            norm = cx * cx + cy * cy + cz * cz
            comp = choose(row, (cx, cy, cz, norm, 1.0, cvar_ref[pl.ds(b, 1), :], cweight_ref[pl.ds(b, 1), :]), shape)
            comps_ref[a, k] = comp
            return comp

        for k, _, t in pair_terms(left, spread_var, comp_of):
            total = jnp.sum(jnp.sum(t * spread_weight, axis=0), axis=0, keepdims=True)
            place = owner_ref[list_ref[k, a]]
            target = ((place & 56) << 5) + ((place >> 6) << 3) + (place & 7)
            model_ref[pl.ds(target, 1), :] += NORM * total * comps_ref[a, k, 6:7, :]
        return 0

    lax.fori_loop(0, BLK_DEV, block, 0)


def ratio_kernel(atoms_ref, comps_ref, ratio_any, ratio_buf, sems):
    blocks = ratio_any.shape[0]

    def store(a):
        return pltpu.make_async_copy(ratio_buf.at[a & 1], ratio_any.at[a], sems.at[a & 1])

    def block(a, _):
        @pl.when(a >= 2)
        def _():
            store(a - 2).wait()

        atoms = atoms_ref[a].T
        left = atoms[:, :FEATS].astype(jnp.bfloat16)
        spread_var = spread_lanes(atoms, FEATS)
        slot = a & 1
        for k, q, t in pair_terms(left, spread_var, lambda k: comps_ref[a, k]):
            ratio_buf[slot, :, k * 128 : (k + 1) * 128] = (t * q).reshape(128, 128)
        store(a).start()
        return 0

    lax.fori_loop(0, blocks, block, 0)
    store(blocks - 2).wait()
    store(blocks - 1).wait()


def in_hbm(array):
    return pltpu.with_memory_space_constraint(array, pltpu.HBM)


def rep_sum_kernel(parts_ref, out_ref):
    out_ref[...] = jnp.sum(parts_ref[...], axis=0)


def adjoint_kernel(parts_ref, target_ref, sigma_ref, spread_ref, mean_ref):
    share = mean_ref.shape[0]
    mean = jnp.sum(parts_ref[...], axis=0) / REPLICAS
    first = pl.ds(pl.multiple_of(lax.axis_index("rep") * share, share), share)
    sigma = sigma_ref[first, :]
    misfit = mean - target_ref[first, :]
    adjoint = misfit / (sigma * sigma + 0.5 * misfit * misfit) / REPLICAS
    mean_ref[...] = mean
    spread_ref[...] = jnp.broadcast_to(adjoint[None], spread_ref.shape)


def spread_kernel(adjoint_ref, mean_ref, out_ref):
    rows = adjoint_ref.shape[0]
    for r in range(REPLICAS):
        out_ref[r, :rows] = adjoint_ref[...]
        out_ref[r, rows:] = mean_ref[...]


def force_kernel(
    live_ref, list_ref, owner_ref, coords_ref, weight_ref, comps_ref, adjoint_ref, *refs,
):
    parts = BLK_DEV // PART
    ratio_any, (force_ref, ratio_ref, ratio_sems) = refs[:parts], refs[parts:]
    depth = ratio_ref.shape[0]
    shape = (8, 128)
    row = lax.broadcasted_iota(jnp.int32, shape, 0)
    upper = row < 4
    lane = lax.broadcasted_iota(jnp.int32, (1, 128), 1)

    def load(part, n):
        slot = (part * PART + n) % depth
        return pltpu.make_async_copy(ratio_any[part].at[n], ratio_ref.at[slot], ratio_sems.at[slot])

    def ahead(part, n):
        if n >= PART:
            part, n = part + 1, n - PART
        if part < parts:
            load(part, n).start()

    def block(part, n):
        a = part * PART + n
        load(part, n).wait()
        slot = a % depth
        rights = []
        for k in range(LISTED):
            place = owner_ref[list_ref[k, a]]
            target = (place & 56) * 33 + ((place >> 6) << 3) + (place & 7)
            cx, cy, cz, cw = (comps_ref[a, k, d : d + 1, :] for d in (0, 1, 2, 6))
            pull = (ENERGY_UNIT * NORM) * adjoint_ref[pl.ds(target, 1), :] * cw
            hi, mid, low = split3(pull * choose(row & 3, (cx, cy, cz, 1.0), shape))
            rights.append(
                jnp.concatenate([jnp.where(upper, hi, mid), jnp.where(upper, low, 0.0)], axis=0).astype(jnp.bfloat16)
            )
        total = jnp.zeros((128, 16), jnp.float32)
        dims = (((1,), (1,)), ((), ()))
        for k in range(0, LISTED, 2):
            right = jnp.concatenate(rights[k : k + 2], axis=1)
            ratio = ratio_ref[slot, :, k * 128 : (k + 2) * 128]
            hi = ratio.astype(jnp.bfloat16)
            low = (ratio - hi.astype(jnp.float32)).astype(jnp.bfloat16)
            total += lax.dot_general(hi, right, dims, preferred_element_type=jnp.float32)
            total += lax.dot_general(low, right, dims, preferred_element_type=jnp.float32)
        turned = total.T
        got = turned[0:8] + turned[8:16]
        got = got[0:4] + got[4:8]
        weight = jnp.where(lane < live_ref[a], weight_ref[pl.ds(a, 1), :], 0.0)
        for d in range(3):
            at = pl.ds(d * BLK_DEV + a, 1)
            force_ref[at, :] = weight * (coords_ref[at, :] * got[3:4] - got[d : d + 1])

    for n in range(depth - 1):
        ahead(0, n)
    for part in range(parts):
        def step(n, _, part=part):
            @pl.when(n + depth - 1 < PART)
            def _():
                load(part, n + depth - 1).start()

            if part + 1 < parts:
                @pl.when(n + depth - 1 >= PART)
                def _():
                    load(part + 1, n + depth - 1 - PART).start()

            block(part, n)
            return 0

        lax.fori_loop(0, PART, step, 0)


SMEM_SPEC = pl.BlockSpec(memory_space=pltpu.SMEM)
VMEM_SPEC = pl.BlockSpec(memory_space=pltpu.VMEM)
HBM_SPEC = pl.BlockSpec(memory_space=pltpu.HBM)


def call_overlap(*arrays):
    f32 = jnp.float32
    vmem, hbm = VMEM_SPEC, HBM_SPEC
    return pl.pallas_call(
        overlap_kernel,
        out_shape=(
            jax.ShapeDtypeStruct((COMP_BLOCKS, COMP_BLK), f32),
            jax.ShapeDtypeStruct((BLK_DEV, LISTED, 8, COMP_BLK), f32),
            jax.ShapeDtypeStruct((BLK_DEV, FEATS + 8, ATOM_BLK), f32),
        ),
        in_specs=[hbm] * 9,
        out_specs=(vmem,) * 3,
        scratch_shapes=[
            pltpu.SMEM((BLK_DEV,), jnp.int32),
            pltpu.SMEM((LISTED, BLK_DEV), jnp.int32),
            pltpu.SMEM((COMP_BLOCKS,), jnp.int32),
            pltpu.VMEM((3 * BLK_DEV, ATOM_BLK), f32),
            pltpu.VMEM((BLK_DEV, ATOM_BLK), f32),
            pltpu.VMEM((BLK_DEV, ATOM_BLK), f32),
            pltpu.VMEM((3, COMP_BLOCKS * COMP_BLK), f32),
            pltpu.VMEM((COMP_BLOCKS, COMP_BLK), f32),
            pltpu.VMEM((COMP_BLOCKS, COMP_BLK), f32),
            pltpu.SemaphoreType.DMA((9,)),
        ],
        compiler_params=pltpu.CompilerParams(vmem_limit_bytes=20 << 20),
        name="overlap",
    )(*(in_hbm(v) for v in arrays))


def call_ratio(atoms, comps, part):
    f32 = jnp.float32
    specs = [
        pl.BlockSpec((PART,) + a.shape[1:], lambda i, n=a.ndim: (part,) + (0,) * (n - 1)) for a in (atoms, comps)
    ]
    return pl.pallas_call(
        ratio_kernel,
        grid=(1,),
        out_shape=pltpu.HBM((PART, ATOM_BLK, LISTED * COMP_BLK), f32),
        in_specs=specs,
        out_specs=HBM_SPEC,
        scratch_shapes=[
            pltpu.VMEM((2, ATOM_BLK, LISTED * COMP_BLK), f32),
            pltpu.SemaphoreType.DMA((2,)),
        ],
        compiler_params=pltpu.CompilerParams(vmem_limit_bytes=12 << 20),
        cost_estimate=pl.CostEstimate(flops=PART << 24, bytes_accessed=PART << 20, transcendentals=PART << 19),
        name="ratio",
    )(atoms, comps)


def call_force(*arrays):
    f32 = jnp.float32
    smem, vmem, hbm = SMEM_SPEC, VMEM_SPEC, HBM_SPEC
    *arrays, ratios = arrays
    return pl.pallas_call(
        force_kernel,
        out_shape=jax.ShapeDtypeStruct((3 * BLK_DEV, ATOM_BLK), f32),
        in_specs=[smem] * 3 + [vmem] * 4 + [hbm] * len(ratios),
        out_specs=vmem,
        scratch_shapes=[
            pltpu.VMEM((4, ATOM_BLK, LISTED * COMP_BLK), f32),
            pltpu.SemaphoreType.DMA((4,)),
        ],
        compiler_params=pltpu.CompilerParams(vmem_limit_bytes=16 << 20),
        name="force",
    )(*arrays, *(in_hbm(ratio) for ratio in ratios))


def shards(
    coords, atom_var, atom_weight, atoms_live, block_list, owner_map, comp_means, comp_var, comp_weight, target, noise_sigma,
):
    replicas = lax.axis_size("rep")
    domains = lax.axis_size("dom")
    share = COMP_BLOCKS // domains // replicas
    vmem = VMEM_SPEC
    small = pltpu.CompilerParams(vmem_limit_bytes=6 << 20)
    f32 = jnp.float32
    positions = coords.reshape(3 * BLK_DEV, ATOM_BLK)
    listed = block_list.T
    variances = atom_var.reshape(BLK_DEV, ATOM_BLK)
    weights = atom_weight.reshape(BLK_DEV, ATOM_BLK)
    cvar = comp_var.reshape(COMP_BLOCKS, COMP_BLK)
    cweight = comp_weight.reshape(COMP_BLOCKS, COMP_BLK)
    model, comps, atoms = call_overlap(
        atoms_live, listed, owner_map, positions, variances, weights, comp_means, cvar, cweight
    )
    tie = lax.optimization_barrier
    ratios = [call_ratio(atoms, comps, 0)]
    parts = lax.all_to_all(model.reshape(replicas, domains * share, COMP_BLK), "rep", 0, 0, tiled=True)
    parts, ratios[0] = tie((parts, ratios[0]))
    over_rep = pl.pallas_call(
        rep_sum_kernel,
        out_shape=jax.ShapeDtypeStruct((domains * share, COMP_BLK), f32),
        in_specs=[vmem], out_specs=vmem, compiler_params=small, name="rep_sum",
    )(parts)
    over_rep, atoms = tie((over_rep, atoms))
    ratios.append(call_ratio(atoms, comps, 1))
    parts = lax.all_to_all(over_rep.reshape(domains, share, COMP_BLK), "dom", 0, 0, tiled=True)
    parts, ratios[1] = tie((parts, ratios[1]))
    spread, mean = pl.pallas_call(
        adjoint_kernel,
        out_shape=(
            jax.ShapeDtypeStruct((domains, share, COMP_BLK), f32), jax.ShapeDtypeStruct((share, COMP_BLK), f32),
        ),
        in_specs=[vmem] * 3, out_specs=(vmem, vmem), compiler_params=small, name="adjoint",
    )(parts, target.reshape(-1, COMP_BLK), noise_sigma.reshape(-1, COMP_BLK))
    spread, atoms = tie((spread, atoms))
    ratios.append(call_ratio(atoms, comps, 2))
    over_dom = lax.all_to_all(spread, "dom", 0, 0, tiled=True).reshape(domains * share, COMP_BLK)
    over_dom, ratios[2] = tie((over_dom, ratios[2]))
    spread = pl.pallas_call(
        spread_kernel,
        out_shape=jax.ShapeDtypeStruct((replicas, (domains + 1) * share, COMP_BLK), f32),
        in_specs=[vmem] * 2, out_specs=vmem, compiler_params=small, name="spread",
    )(over_dom, mean)
    spread, atoms = tie((spread, atoms))
    ratios.append(call_ratio(atoms, comps, 3))
    returned = lax.all_to_all(spread, "rep", 0, 0, tiled=True)
    average = returned[:, domains * share :].reshape(-1)
    returned = returned.reshape(-1, COMP_BLK)

    forces = call_force(atoms_live, listed, owner_map, positions, weights, comps, returned, ratios)
    return average, forces.reshape(coords.shape)


def solution(mesh):
    return jax.shard_map(
        shards,
        mesh=mesh,
        in_specs=(
            P("rep", None, "dom"), P("dom"), P("dom"), P("dom"), P("dom", None), P(), P(), P(), P(), P("dom"), P("dom"),
        ),
        out_specs=(P("dom"), P("rep", None, "dom")),
        check_vma=False,
    )
```

```python
import functools
import math

import jax
import jax.numpy as jnp
from jax import lax
from jax.experimental import pallas as pl
from jax.experimental.pallas import tpu as pltpu
from jax.sharding import PartitionSpec as P

ATOM_BLK = 128
COMP_BLK = 128
LISTED = 16
BLK_DEV = 32
COMP_BLOCKS = 2048
REPLICAS = 8
FEATS = 48
ROOM = 96
SHARE = 8
OWNED = 256
PART = 8

ENERGY_UNIT = 2.494
EXP_SCALE = -0.5 / math.log(2.0)
NORM = (2.0 * math.pi) ** -1.5


def split3(v):
    hi = v.astype(jnp.bfloat16).astype(jnp.float32)
    rest = v - hi
    mid = rest.astype(jnp.bfloat16).astype(jnp.float32)
    return hi, mid, rest - mid


def choose(row, parts, shape, other=0.0):
    out = jnp.full(shape, other, jnp.float32)
    for k, part in enumerate(parts):
        out = jnp.where(row == k, part, out)
    return out


def right_side(comp):
    hi, mid, low = split3(comp)
    return jnp.concatenate([hi, hi, hi, mid, mid, low], axis=0).astype(jnp.bfloat16)


def spread_lanes(atoms, column):
    return jnp.broadcast_to(atoms[:, column : column + 1], (128, 128)).reshape(16, 8, 128)


def pair_terms(left, spread_var, comp_of):
    for k in range(0, LISTED, 2):
        comps = [comp_of(k), comp_of(k + 1)]
        right = jnp.concatenate([right_side(comp) for comp in comps], axis=1)
        scaled = jnp.dot(left, right, preferred_element_type=jnp.float32).reshape(16, 8, 256)
        for n in range(2):
            r = lax.rsqrt(spread_var + comps[n][5:6].reshape(1, 1, 128))
            q = r * r
            yield k + n, q, (q * r) * jnp.exp2(scaled[:, :, n * 128 : (n + 1) * 128] * q)


def overlap_kernel(
    live_any, list_any, owner_any, coords_any, var_any, weight_any, means_any, cvar_any, cweight_any,
    model_ref, over_ref, rows_ref, slots_ref, counts_ref, comps_ref, atoms_ref,
    sums_ref, live_ref, list_ref, owner_ref, coords_ref, var_ref, weight_ref, means_ref, cvar_ref, cweight_ref, sems,
):
    pairs = (
        (live_any, live_ref), (list_any, list_ref), (owner_any, owner_ref), (coords_any, coords_ref),
        (var_any, var_ref), (weight_any, weight_ref), (means_any, means_ref), (cvar_any, cvar_ref),
        (cweight_any, cweight_ref),
    )
    copies = [pltpu.make_async_copy(src, dst, sems.at[n]) for n, (src, dst) in enumerate(pairs)]
    for copy in copies:
        copy.start()
    shape = (8, 128)
    row = lax.broadcasted_iota(jnp.int32, shape, 0)
    lane = lax.broadcasted_iota(jnp.int32, (1, 128), 1)
    sums_ref[...] = jnp.zeros_like(sums_ref)
    for r in range(REPLICAS + 1):
        counts_ref[r] = 0

    def unused(n, _):
        slots_ref[n] = OWNED
        return 0

    lax.fori_loop(0, REPLICAS * ROOM, unused, 0, unroll=8)
    for copy in copies:
        copy.wait()

    def block(a, _):
        x, y, z = (coords_ref[pl.ds(d * BLK_DEV + a, 1), :] for d in range(3))
        norm2 = EXP_SCALE * (x * x + y * y + z * z)
        t = -2.0 * EXP_SCALE
        hi, mid, low = split3(choose(row, (t * x, t * y, t * z, EXP_SCALE, norm2), shape))
        weight = jnp.where(lane < live_ref[a], weight_ref[pl.ds(a, 1), :], 0.0)
        extra = choose(row, (var_ref[pl.ds(a, 1), :], weight), shape)
        feats = jnp.concatenate([hi, mid, low, hi, mid, hi, extra], axis=0)
        atoms_ref[a] = feats
        atoms = feats.T
        left = atoms[:, :FEATS].astype(jnp.bfloat16)
        spread_var = spread_lanes(atoms, FEATS)
        spread_weight = spread_lanes(atoms, FEATS + 1)

        def comp_of(k):
            b = list_ref[k, a]
            cols = pl.ds(pl.multiple_of(b * 128, 128), 128)
            cx, cy, cz = (means_ref[d : d + 1, cols] for d in range(3))
            norm = cx * cx + cy * cy + cz * cz
            comp = choose(row, (cx, cy, cz, norm, 1.0, cvar_ref[pl.ds(b, 1), :], cweight_ref[pl.ds(b, 1), :]), shape)
            comps_ref[a, k] = comp
            return comp

        for k, _, t in pair_terms(left, spread_var, comp_of):
            total = jnp.sum(jnp.sum(t * spread_weight, axis=0), axis=0, keepdims=True)
            place = owner_ref[list_ref[k, a]]
            rank = (place >> 3) & 7
            owned = ((place >> 6) << 3) + (place & 7)
            count = counts_ref[rank]
            counts_ref[rank] = count + 1
            fits = count < ROOM
            counts_ref[REPLICAS] = jnp.where(fits, counts_ref[REPLICAS], 1)
            slots_ref[jnp.where(fits, rank * ROOM + count, REPLICAS * ROOM)] = owned
            dense = rank * OWNED + owned
            rows_ref[k, a] = jnp.where(fits, rank * (ROOM + SHARE) + count, REPLICAS * (ROOM + SHARE) + dense)
            target = jnp.where(fits, rank * ROOM + count, REPLICAS * ROOM + dense)
            sums_ref[pl.ds(target, 1), :] += NORM * total * comps_ref[a, k, 6:7, :]
        return 0

    lax.fori_loop(0, BLK_DEV, block, 0)
    model_ref[...] = sums_ref[: REPLICAS * ROOM]
    over_ref[...] = sums_ref[REPLICAS * ROOM :]


def ratio_kernel(atoms_ref, comps_ref, ratio_any, ratio_buf, sems):
    blocks = ratio_any.shape[0]

    def store(a):
        return pltpu.make_async_copy(ratio_buf.at[a & 1], ratio_any.at[a], sems.at[a & 1])

    def block(a, _):
        @pl.when(a >= 2)
        def _():
            store(a - 2).wait()

        atoms = atoms_ref[a].T
        left = atoms[:, :FEATS].astype(jnp.bfloat16)
        spread_var = spread_lanes(atoms, FEATS)
        slot = a & 1
        for k, q, t in pair_terms(left, spread_var, lambda k: comps_ref[a, k]):
            ratio_buf[slot, :, k * 128 : (k + 1) * 128] = (t * q).reshape(128, 128)
        store(a).start()
        return 0

    lax.fori_loop(0, blocks, block, 0)
    store(blocks - 2).wait()
    store(blocks - 1).wait()


def in_hbm(array):
    return pltpu.with_memory_space_constraint(array, pltpu.HBM)


def rep_sum_kernel(slots_ref, parts_ref, over_ref, out_ref, sum_ref, dense_ref):
    sum_ref[...] = jnp.sum(parts_ref[...], axis=0)
    dense_ref[:OWNED] = over_ref[...]
    first = lax.axis_index("rep") * ROOM
    for n in range(ROOM):
        dense_ref[pl.ds(slots_ref[first + n], 1), :] += sum_ref[n : n + 1, :]
    out_ref[...] = dense_ref[:OWNED]


def adjoint_kernel(parts_ref, target_ref, sigma_ref, spread_ref, mean_ref):
    share = mean_ref.shape[0]
    mean = jnp.sum(parts_ref[...], axis=0) / REPLICAS
    first = pl.ds(pl.multiple_of(lax.axis_index("rep") * share, share), share)
    sigma = sigma_ref[first, :]
    misfit = mean - target_ref[first, :]
    adjoint = misfit / (sigma * sigma + 0.5 * misfit * misfit) / REPLICAS
    mean_ref[...] = mean
    spread_ref[...] = jnp.broadcast_to(adjoint[None], spread_ref.shape)


def spread_kernel(slots_ref, adjoint_ref, mean_ref, out_ref, rows_ref):
    first = lax.axis_index("rep") * ROOM
    for n in range(ROOM):
        rows_ref[n : n + 1, :] = adjoint_ref[pl.ds(jnp.minimum(slots_ref[first + n], OWNED - 1), 1), :]
    rows_ref[ROOM:] = mean_ref[...]
    for r in range(REPLICAS):
        out_ref[r] = rows_ref[...]


def force_kernel(
    live_ref, rows_ref, coords_ref, weight_ref, comps_ref, adjoint_ref, over_ref, *refs,
):
    parts = BLK_DEV // PART
    ratio_any, (force_ref, ratio_ref, ratio_sems) = refs[:parts], refs[parts:]
    depth = ratio_ref.shape[0]
    shape = (8, 128)
    row = lax.broadcasted_iota(jnp.int32, shape, 0)
    upper = row < 4
    lane = lax.broadcasted_iota(jnp.int32, (1, 128), 1)

    def load(part, n):
        slot = (part * PART + n) % depth
        return pltpu.make_async_copy(ratio_any[part].at[n], ratio_ref.at[slot], ratio_sems.at[slot])

    def ahead(part, n):
        if n >= PART:
            part, n = part + 1, n - PART
        if part < parts:
            load(part, n).start()

    def block(part, n):
        a = part * PART + n
        load(part, n).wait()
        slot = a % depth
        rights = []
        for k in range(LISTED):
            target = rows_ref[k, a]
            beyond = target - REPLICAS * (ROOM + SHARE)
            near = adjoint_ref[pl.ds(jnp.minimum(target, REPLICAS * (ROOM + SHARE) - 1), 1), :]
            far = over_ref[pl.ds(jnp.maximum(beyond, 0), 1), :]
            cx, cy, cz, cw = (comps_ref[a, k, d : d + 1, :] for d in (0, 1, 2, 6))
            pull = (ENERGY_UNIT * NORM) * jnp.where(beyond < 0, near, far) * cw
            hi, mid, low = split3(pull * choose(row & 3, (cx, cy, cz, 1.0), shape))
            rights.append(
                jnp.concatenate([jnp.where(upper, hi, mid), jnp.where(upper, low, 0.0)], axis=0).astype(jnp.bfloat16)
            )
        total = jnp.zeros((128, 16), jnp.float32)
        dims = (((1,), (1,)), ((), ()))
        for k in range(0, LISTED, 2):
            right = jnp.concatenate(rights[k : k + 2], axis=1)
            ratio = ratio_ref[slot, :, k * 128 : (k + 2) * 128]
            hi = ratio.astype(jnp.bfloat16)
            low = (ratio - hi.astype(jnp.float32)).astype(jnp.bfloat16)
            total += lax.dot_general(hi, right, dims, preferred_element_type=jnp.float32)
            total += lax.dot_general(low, right, dims, preferred_element_type=jnp.float32)
        turned = total.T
        got = turned[0:8] + turned[8:16]
        got = got[0:4] + got[4:8]
        weight = jnp.where(lane < live_ref[a], weight_ref[pl.ds(a, 1), :], 0.0)
        for d in range(3):
            at = pl.ds(d * BLK_DEV + a, 1)
            force_ref[at, :] = weight * (coords_ref[at, :] * got[3:4] - got[d : d + 1])

    for n in range(depth - 1):
        ahead(0, n)
    for part in range(parts):
        def step(n, _, part=part):
            @pl.when(n + depth - 1 < PART)
            def _():
                load(part, n + depth - 1).start()

            if part + 1 < parts:
                @pl.when(n + depth - 1 >= PART)
                def _():
                    load(part + 1, n + depth - 1 - PART).start()

            block(part, n)
            return 0

        lax.fori_loop(0, PART, step, 0)


SMEM_SPEC = pl.BlockSpec(memory_space=pltpu.SMEM)
VMEM_SPEC = pl.BlockSpec(memory_space=pltpu.VMEM)
HBM_SPEC = pl.BlockSpec(memory_space=pltpu.HBM)


def call_overlap(*arrays):
    f32 = jnp.float32
    vmem, hbm = VMEM_SPEC, HBM_SPEC
    return pl.pallas_call(
        overlap_kernel,
        out_shape=(
            jax.ShapeDtypeStruct((REPLICAS * ROOM, COMP_BLK), f32),
            jax.ShapeDtypeStruct((COMP_BLOCKS, COMP_BLK), f32),
            jax.ShapeDtypeStruct((LISTED, BLK_DEV), jnp.int32),
            jax.ShapeDtypeStruct((REPLICAS * ROOM + 128,), jnp.int32),
            jax.ShapeDtypeStruct((128,), jnp.int32),
            jax.ShapeDtypeStruct((BLK_DEV, LISTED, 8, COMP_BLK), f32),
            jax.ShapeDtypeStruct((BLK_DEV, FEATS + 8, ATOM_BLK), f32),
        ),
        in_specs=[hbm] * 9,
        out_specs=(vmem, vmem, SMEM_SPEC, SMEM_SPEC, SMEM_SPEC, vmem, vmem),
        scratch_shapes=[
            pltpu.VMEM((REPLICAS * ROOM + COMP_BLOCKS, COMP_BLK), f32),
            pltpu.SMEM((BLK_DEV,), jnp.int32),
            pltpu.SMEM((LISTED, BLK_DEV), jnp.int32),
            pltpu.SMEM((COMP_BLOCKS,), jnp.int32),
            pltpu.VMEM((3 * BLK_DEV, ATOM_BLK), f32),
            pltpu.VMEM((BLK_DEV, ATOM_BLK), f32),
            pltpu.VMEM((BLK_DEV, ATOM_BLK), f32),
            pltpu.VMEM((3, COMP_BLOCKS * COMP_BLK), f32),
            pltpu.VMEM((COMP_BLOCKS, COMP_BLK), f32),
            pltpu.VMEM((COMP_BLOCKS, COMP_BLK), f32),
            pltpu.SemaphoreType.DMA((9,)),
        ],
        compiler_params=pltpu.CompilerParams(vmem_limit_bytes=20 << 20),
        name="overlap",
    )(*(in_hbm(v) for v in arrays))


def call_ratio(atoms, comps, part):
    f32 = jnp.float32
    specs = [
        pl.BlockSpec((PART,) + a.shape[1:], lambda i, n=a.ndim: (part,) + (0,) * (n - 1)) for a in (atoms, comps)
    ]
    return pl.pallas_call(
        ratio_kernel,
        grid=(1,),
        out_shape=pltpu.HBM((PART, ATOM_BLK, LISTED * COMP_BLK), f32),
        in_specs=specs,
        out_specs=HBM_SPEC,
        scratch_shapes=[
            pltpu.VMEM((2, ATOM_BLK, LISTED * COMP_BLK), f32),
            pltpu.SemaphoreType.DMA((2,)),
        ],
        compiler_params=pltpu.CompilerParams(vmem_limit_bytes=12 << 20),
        cost_estimate=pl.CostEstimate(flops=PART << 24, bytes_accessed=PART << 20, transcendentals=PART << 19),
        name="ratio",
    )(atoms, comps)


def call_force(*arrays):
    f32 = jnp.float32
    smem, vmem, hbm = SMEM_SPEC, VMEM_SPEC, HBM_SPEC
    *arrays, ratios = arrays
    return pl.pallas_call(
        force_kernel,
        out_shape=jax.ShapeDtypeStruct((3 * BLK_DEV, ATOM_BLK), f32),
        in_specs=[smem] * 2 + [vmem] * 5 + [hbm] * len(ratios),
        out_specs=vmem,
        scratch_shapes=[
            pltpu.VMEM((4, ATOM_BLK, LISTED * COMP_BLK), f32),
            pltpu.SemaphoreType.DMA((4,)),
        ],
        compiler_params=pltpu.CompilerParams(vmem_limit_bytes=16 << 20),
        name="force",
    )(*arrays, *(in_hbm(ratio) for ratio in ratios))


def shards(
    coords, atom_var, atom_weight, atoms_live, block_list, owner_map, comp_means, comp_var, comp_weight, target, noise_sigma,
):
    replicas = lax.axis_size("rep")
    domains = lax.axis_size("dom")
    share = COMP_BLOCKS // domains // replicas
    vmem = VMEM_SPEC
    small = pltpu.CompilerParams(vmem_limit_bytes=6 << 20)
    f32 = jnp.float32
    positions = coords.reshape(3 * BLK_DEV, ATOM_BLK)
    listed = block_list.T
    variances = atom_var.reshape(BLK_DEV, ATOM_BLK)
    weights = atom_weight.reshape(BLK_DEV, ATOM_BLK)
    cvar = comp_var.reshape(COMP_BLOCKS, COMP_BLK)
    cweight = comp_weight.reshape(COMP_BLOCKS, COMP_BLK)
    model, over, rows, slots, counts, comps, atoms = call_overlap(
        atoms_live, listed, owner_map, positions, variances, weights, comp_means, cvar, cweight
    )
    crowded = counts[REPLICAS] > 0
    tie = lax.optimization_barrier
    ratios = [call_ratio(atoms, comps, 0)]
    parts = lax.all_to_all(model.reshape(replicas, ROOM, COMP_BLK), "rep", 0, 0, tiled=True)
    parts, ratios[0] = tie((parts, ratios[0]))
    over_sum = lax.cond(
        crowded,
        lambda v: jnp.sum(lax.all_to_all(v.reshape(replicas, OWNED, COMP_BLK), "rep", 0, 0, tiled=True), axis=0),
        lambda v: jnp.zeros((OWNED, COMP_BLK), f32),
        over,
    )
    over_rep = pl.pallas_call(
        rep_sum_kernel,
        out_shape=jax.ShapeDtypeStruct((OWNED, COMP_BLK), f32),
        in_specs=[SMEM_SPEC, vmem, vmem], out_specs=vmem,
        scratch_shapes=[pltpu.VMEM((ROOM, COMP_BLK), f32), pltpu.VMEM((OWNED + 8, COMP_BLK), f32)],
        compiler_params=small, name="rep_sum",
    )(slots, parts, over_sum)
    over_rep, atoms = tie((over_rep, atoms))
    ratios.append(call_ratio(atoms, comps, 1))
    parts = lax.all_to_all(over_rep.reshape(domains, share, COMP_BLK), "dom", 0, 0, tiled=True)
    parts, ratios[1] = tie((parts, ratios[1]))
    spread, mean = pl.pallas_call(
        adjoint_kernel,
        out_shape=(
            jax.ShapeDtypeStruct((domains, share, COMP_BLK), f32), jax.ShapeDtypeStruct((share, COMP_BLK), f32),
        ),
        in_specs=[vmem] * 3, out_specs=(vmem, vmem), compiler_params=small, name="adjoint",
    )(parts, target.reshape(-1, COMP_BLK), noise_sigma.reshape(-1, COMP_BLK))
    spread, atoms = tie((spread, atoms))
    ratios.append(call_ratio(atoms, comps, 2))
    over_dom = lax.all_to_all(spread, "dom", 0, 0, tiled=True).reshape(domains * share, COMP_BLK)
    over_dom, ratios[2] = tie((over_dom, ratios[2]))
    over_back = lax.cond(
        crowded,
        lambda v: lax.all_to_all(jnp.broadcast_to(v[None], (replicas, OWNED, COMP_BLK)), "rep", 0, 0, tiled=True),
        lambda v: jnp.zeros((replicas, OWNED, COMP_BLK), f32),
        over_dom,
    ).reshape(-1, COMP_BLK)
    spread = pl.pallas_call(
        spread_kernel,
        out_shape=jax.ShapeDtypeStruct((replicas, ROOM + share, COMP_BLK), f32),
        in_specs=[SMEM_SPEC, vmem, vmem], out_specs=vmem,
        scratch_shapes=[pltpu.VMEM((ROOM + share, COMP_BLK), f32)],
        compiler_params=small, name="spread",
    )(slots, over_dom, mean)
    spread, atoms = tie((spread, atoms))
    ratios.append(call_ratio(atoms, comps, 3))
    returned = lax.all_to_all(spread, "rep", 0, 0, tiled=True)
    average = returned[:, ROOM:].reshape(-1)
    returned = returned.reshape(-1, COMP_BLK)

    forces = call_force(atoms_live, rows, positions, weights, comps, returned, over_back, ratios)
    return average, forces.reshape(coords.shape)


def solution(mesh):
    return jax.shard_map(
        shards,
        mesh=mesh,
        in_specs=(
            P("rep", None, "dom"), P("dom"), P("dom"), P("dom"), P("dom", None), P(), P(), P(), P(), P("dom"), P("dom"),
        ),
        out_specs=(P("dom"), P("rep", None, "dom")),
        check_vma=False,
    )
```

```python
import functools
import math

import jax
import jax.numpy as jnp
from jax import lax
from jax.experimental import pallas as pl
from jax.experimental.pallas import tpu as pltpu
from jax.sharding import PartitionSpec as P

ATOM_BLK = 128
COMP_BLK = 128
LISTED = 16
BLK_DEV = 32
COMP_BLOCKS = 2048
REPLICAS = 8
FEATS = 48
ROOM = 96
SHARE = 8
OWNED = 256
PART = 8

ENERGY_UNIT = 2.494
EXP_SCALE = -0.5 / math.log(2.0)
NORM = (2.0 * math.pi) ** -1.5


def split3(v):
    hi = v.astype(jnp.bfloat16).astype(jnp.float32)
    rest = v - hi
    mid = rest.astype(jnp.bfloat16).astype(jnp.float32)
    return hi, mid, rest - mid


def choose(row, parts, shape, other=0.0):
    out = jnp.full(shape, other, jnp.float32)
    for k, part in enumerate(parts):
        out = jnp.where(row == k, part, out)
    return out


def right_side(comp):
    hi, mid, low = split3(comp)
    return jnp.concatenate([hi, hi, hi, mid, mid, low], axis=0).astype(jnp.bfloat16)


def spread_lanes(atoms, column):
    return jnp.broadcast_to(atoms[:, column : column + 1], (128, 128)).reshape(16, 8, 128)


def pair_terms(left, spread_var, comp_of):
    for k in range(0, LISTED, 2):
        comps = [comp_of(k), comp_of(k + 1)]
        right = jnp.concatenate([right_side(comp) for comp in comps], axis=1)
        scaled = jnp.dot(left, right, preferred_element_type=jnp.float32).reshape(16, 8, 256)
        for n in range(2):
            r = lax.rsqrt(spread_var + comps[n][5:6].reshape(1, 1, 128))
            q = r * r
            yield k + n, q, (q * r) * jnp.exp2(scaled[:, :, n * 128 : (n + 1) * 128] * q)


def overlap_kernel(
    live_any, list_any, owner_any, coords_any, var_any, weight_any, means_any, cvar_any, cweight_any,
    model_ref, over_ref, rows_ref, slots_ref, counts_ref, comps_ref, atoms_ref,
    sums_ref, live_ref, list_ref, owner_ref, coords_ref, var_ref, weight_ref, means_ref, cvar_ref, cweight_ref, sems,
):
    pairs = (
        (live_any, live_ref), (list_any, list_ref), (owner_any, owner_ref), (coords_any, coords_ref),
        (var_any, var_ref), (weight_any, weight_ref), (means_any, means_ref), (cvar_any, cvar_ref),
        (cweight_any, cweight_ref),
    )
    copies = [pltpu.make_async_copy(src, dst, sems.at[n]) for n, (src, dst) in enumerate(pairs)]
    for copy in copies:
        copy.start()
    shape = (8, 128)
    row = lax.broadcasted_iota(jnp.int32, shape, 0)
    lane = lax.broadcasted_iota(jnp.int32, (1, 128), 1)
    sums_ref[...] = jnp.zeros_like(sums_ref)
    for r in range(REPLICAS + 1):
        counts_ref[r] = 0

    def unused(n, _):
        slots_ref[n] = OWNED
        return 0

    lax.fori_loop(0, REPLICAS * ROOM, unused, 0, unroll=8)
    for copy in copies:
        copy.wait()

    def block(a, _):
        x, y, z = (coords_ref[pl.ds(d * BLK_DEV + a, 1), :] for d in range(3))
        norm2 = EXP_SCALE * (x * x + y * y + z * z)
        t = -2.0 * EXP_SCALE
        hi, mid, low = split3(choose(row, (t * x, t * y, t * z, EXP_SCALE, norm2), shape))
        weight = jnp.where(lane < live_ref[a], weight_ref[pl.ds(a, 1), :], 0.0)
        extra = choose(row, (var_ref[pl.ds(a, 1), :], weight), shape)
        feats = jnp.concatenate([hi, mid, low, hi, mid, hi, extra], axis=0)
        atoms_ref[a] = feats
        atoms = feats.T
        left = atoms[:, :FEATS].astype(jnp.bfloat16)
        spread_var = spread_lanes(atoms, FEATS)
        spread_weight = spread_lanes(atoms, FEATS + 1)

        def comp_of(k):
            b = list_ref[k, a]
            cols = pl.ds(pl.multiple_of(b * 128, 128), 128)
            cx, cy, cz = (means_ref[d : d + 1, cols] for d in range(3))
            norm = cx * cx + cy * cy + cz * cz
            comp = choose(row, (cx, cy, cz, norm, 1.0, cvar_ref[pl.ds(b, 1), :], cweight_ref[pl.ds(b, 1), :]), shape)
            comps_ref[a, k] = comp
            return comp

        for k, _, t in pair_terms(left, spread_var, comp_of):
            total = jnp.sum(jnp.sum(t * spread_weight, axis=0), axis=0, keepdims=True)
            place = owner_ref[list_ref[k, a]]
            rank = (place >> 3) & 7
            owned = ((place >> 6) << 3) + (place & 7)
            count = counts_ref[rank]
            counts_ref[rank] = count + 1
            fits = count < ROOM
            counts_ref[REPLICAS] = jnp.where(fits, counts_ref[REPLICAS], 1)
            slots_ref[jnp.where(fits, rank * ROOM + count, REPLICAS * ROOM)] = owned
            dense = rank * OWNED + owned
            rows_ref[k, a] = jnp.where(fits, rank * (ROOM + SHARE) + count, REPLICAS * (ROOM + SHARE) + dense)
            target = jnp.where(fits, rank * ROOM + count, REPLICAS * ROOM + dense)
            sums_ref[pl.ds(target, 1), :] += NORM * total * comps_ref[a, k, 6:7, :]
        return 0

    lax.fori_loop(0, BLK_DEV, block, 0)
    model_ref[...] = sums_ref[: REPLICAS * ROOM]
    over_ref[...] = sums_ref[REPLICAS * ROOM :]


def ratio_kernel(atoms_ref, comps_ref, ratio_any, ratio_buf, sems):
    blocks = ratio_any.shape[0]

    def store(a):
        return pltpu.make_async_copy(ratio_buf.at[a & 1], ratio_any.at[a], sems.at[a & 1])

    def block(a, _):
        @pl.when(a >= 2)
        def _():
            store(a - 2).wait()

        slot = a & 1
        row = lax.broadcasted_iota(jnp.int32, (8, 128), 0)
        own = jnp.where(row == 5, 1.0, 0.0)
        var = jnp.where(row == 4, jnp.broadcast_to(atoms_ref[a, FEATS : FEATS + 1, :], (8, 128)), 0.0)
        hi, mid, low = split3(var)
        sums = jnp.concatenate([hi + own, mid, low, own, jnp.zeros_like(own), own], axis=0)
        right = jnp.concatenate([atoms_ref[a, :FEATS, :], sums], axis=1).astype(jnp.bfloat16)
        for k in range(LISTED):
            left = right_side(comps_ref[a, k]).T
            both = jnp.dot(left, right, preferred_element_type=jnp.float32).reshape(16, 8, 256)
            r = lax.rsqrt(both[:, :, 128:])
            q = r * r
            ratio = ((q * q) * (r * jnp.exp2(both[:, :, :128] * q))).reshape(128, 128)
            hi = ratio.astype(jnp.bfloat16)
            rows = slice(k * 128, (k + 1) * 128)
            ratio_buf[slot, rows, :128] = hi
            ratio_buf[slot, rows, 128:] = (ratio - hi.astype(jnp.float32)).astype(jnp.bfloat16)
        store(a).start()
        return 0

    lax.fori_loop(0, blocks, block, 0)
    store(blocks - 2).wait()
    store(blocks - 1).wait()


def in_hbm(array):
    return pltpu.with_memory_space_constraint(array, pltpu.HBM)


def rep_sum_kernel(slots_ref, parts_ref, over_ref, out_ref, sum_ref, dense_ref):
    sum_ref[...] = jnp.sum(parts_ref[...], axis=0)
    dense_ref[:OWNED] = over_ref[...]
    first = lax.axis_index("rep") * ROOM
    for n in range(ROOM):
        dense_ref[pl.ds(slots_ref[first + n], 1), :] += sum_ref[n : n + 1, :]
    out_ref[...] = dense_ref[:OWNED]


def adjoint_kernel(parts_ref, target_ref, sigma_ref, spread_ref, mean_ref):
    share = mean_ref.shape[0]
    mean = jnp.sum(parts_ref[...], axis=0) / REPLICAS
    first = pl.ds(pl.multiple_of(lax.axis_index("rep") * share, share), share)
    sigma = sigma_ref[first, :]
    misfit = mean - target_ref[first, :]
    adjoint = misfit / (sigma * sigma + 0.5 * misfit * misfit) / REPLICAS
    mean_ref[...] = mean
    spread_ref[...] = jnp.broadcast_to(adjoint[None], spread_ref.shape)


def spread_kernel(slots_ref, adjoint_ref, mean_ref, out_ref, rows_ref):
    first = lax.axis_index("rep") * ROOM
    for n in range(ROOM):
        rows_ref[n : n + 1, :] = adjoint_ref[pl.ds(jnp.minimum(slots_ref[first + n], OWNED - 1), 1), :]
    rows_ref[ROOM:] = mean_ref[...]
    for r in range(REPLICAS):
        out_ref[r] = rows_ref[...]


def force_kernel(
    live_ref, rows_ref, coords_ref, weight_ref, comps_ref, adjoint_ref, over_ref, *refs,
):
    parts = BLK_DEV // PART
    ratio_any, (force_ref, ratio_ref, ratio_sems) = refs[:parts], refs[parts:]
    depth = ratio_ref.shape[0]
    shape = (8, 128)
    row = lax.broadcasted_iota(jnp.int32, shape, 0)
    upper = row < 4
    lane = lax.broadcasted_iota(jnp.int32, (1, 128), 1)

    def load(part, n):
        slot = (part * PART + n) % depth
        return pltpu.make_async_copy(ratio_any[part].at[n], ratio_ref.at[slot], ratio_sems.at[slot])

    def ahead(part, n):
        if n >= PART:
            part, n = part + 1, n - PART
        if part < parts:
            load(part, n).start()

    def block(part, n):
        a = part * PART + n
        load(part, n).wait()
        slot = a % depth
        rights = []
        for k in range(LISTED):
            target = rows_ref[k, a]
            beyond = target - REPLICAS * (ROOM + SHARE)
            near = adjoint_ref[pl.ds(jnp.minimum(target, REPLICAS * (ROOM + SHARE) - 1), 1), :]
            far = over_ref[pl.ds(jnp.maximum(beyond, 0), 1), :]
            cx, cy, cz, cw = (comps_ref[a, k, d : d + 1, :] for d in (0, 1, 2, 6))
            pull = (ENERGY_UNIT * NORM) * jnp.where(beyond < 0, near, far) * cw
            hi, mid, low = split3(pull * choose(row & 3, (cx, cy, cz, 1.0), shape))
            rights.append(
                jnp.concatenate([jnp.where(upper, hi, mid), jnp.where(upper, low, 0.0)], axis=0).astype(jnp.bfloat16)
            )
        total = jnp.zeros((16, 256), jnp.float32)
        for k in range(0, LISTED, 2):
            pulls = jnp.concatenate(rights[k : k + 2], axis=1)
            total += jnp.dot(pulls, ratio_ref[slot, k * 128 : (k + 2) * 128, :], preferred_element_type=jnp.float32)
        got = total[:, :128] + total[:, 128:]
        got = got[0:8] + got[8:16]
        got = got[0:4] + got[4:8]
        weight = jnp.where(lane < live_ref[a], weight_ref[pl.ds(a, 1), :], 0.0)
        for d in range(3):
            at = pl.ds(d * BLK_DEV + a, 1)
            force_ref[at, :] = weight * (coords_ref[at, :] * got[3:4] - got[d : d + 1])

    for n in range(depth - 1):
        ahead(0, n)
    for part in range(parts):
        def step(n, _, part=part):
            @pl.when(n + depth - 1 < PART)
            def _():
                load(part, n + depth - 1).start()

            if part + 1 < parts:
                @pl.when(n + depth - 1 >= PART)
                def _():
                    load(part + 1, n + depth - 1 - PART).start()

            block(part, n)
            return 0

        lax.fori_loop(0, PART, step, 0)


SMEM_SPEC = pl.BlockSpec(memory_space=pltpu.SMEM)
VMEM_SPEC = pl.BlockSpec(memory_space=pltpu.VMEM)
HBM_SPEC = pl.BlockSpec(memory_space=pltpu.HBM)


def call_overlap(*arrays):
    f32 = jnp.float32
    vmem, hbm = VMEM_SPEC, HBM_SPEC
    return pl.pallas_call(
        overlap_kernel,
        out_shape=(
            jax.ShapeDtypeStruct((REPLICAS * ROOM, COMP_BLK), f32),
            jax.ShapeDtypeStruct((COMP_BLOCKS, COMP_BLK), f32),
            jax.ShapeDtypeStruct((LISTED, BLK_DEV), jnp.int32),
            jax.ShapeDtypeStruct((REPLICAS * ROOM + 128,), jnp.int32),
            jax.ShapeDtypeStruct((128,), jnp.int32),
            jax.ShapeDtypeStruct((BLK_DEV, LISTED, 8, COMP_BLK), f32),
            jax.ShapeDtypeStruct((BLK_DEV, FEATS + 8, ATOM_BLK), f32),
        ),
        in_specs=[hbm] * 9,
        out_specs=(vmem, vmem, SMEM_SPEC, SMEM_SPEC, SMEM_SPEC, vmem, vmem),
        scratch_shapes=[
            pltpu.VMEM((REPLICAS * ROOM + COMP_BLOCKS, COMP_BLK), f32),
            pltpu.SMEM((BLK_DEV,), jnp.int32),
            pltpu.SMEM((LISTED, BLK_DEV), jnp.int32),
            pltpu.SMEM((COMP_BLOCKS,), jnp.int32),
            pltpu.VMEM((3 * BLK_DEV, ATOM_BLK), f32),
            pltpu.VMEM((BLK_DEV, ATOM_BLK), f32),
            pltpu.VMEM((BLK_DEV, ATOM_BLK), f32),
            pltpu.VMEM((3, COMP_BLOCKS * COMP_BLK), f32),
            pltpu.VMEM((COMP_BLOCKS, COMP_BLK), f32),
            pltpu.VMEM((COMP_BLOCKS, COMP_BLK), f32),
            pltpu.SemaphoreType.DMA((9,)),
        ],
        compiler_params=pltpu.CompilerParams(vmem_limit_bytes=20 << 20),
        name="overlap",
    )(*(in_hbm(v) for v in arrays))


def call_ratio(atoms, comps, part):
    f32 = jnp.float32
    specs = [
        pl.BlockSpec((PART,) + a.shape[1:], lambda i, n=a.ndim: (part,) + (0,) * (n - 1)) for a in (atoms, comps)
    ]
    return pl.pallas_call(
        ratio_kernel,
        grid=(1,),
        out_shape=pltpu.HBM((PART, LISTED * COMP_BLK, 2 * ATOM_BLK), jnp.bfloat16),
        in_specs=specs,
        out_specs=HBM_SPEC,
        scratch_shapes=[
            pltpu.VMEM((2, LISTED * COMP_BLK, 2 * ATOM_BLK), jnp.bfloat16),
            pltpu.SemaphoreType.DMA((2,)),
        ],
        compiler_params=pltpu.CompilerParams(vmem_limit_bytes=12 << 20),
        cost_estimate=pl.CostEstimate(flops=PART << 24, bytes_accessed=PART << 20, transcendentals=PART << 19),
        name="ratio",
    )(atoms, comps)


def call_force(*arrays):
    f32 = jnp.float32
    smem, vmem, hbm = SMEM_SPEC, VMEM_SPEC, HBM_SPEC
    *arrays, ratios = arrays
    return pl.pallas_call(
        force_kernel,
        out_shape=jax.ShapeDtypeStruct((3 * BLK_DEV, ATOM_BLK), f32),
        in_specs=[smem] * 2 + [vmem] * 5 + [hbm] * len(ratios),
        out_specs=vmem,
        scratch_shapes=[
            pltpu.VMEM((4, LISTED * COMP_BLK, 2 * ATOM_BLK), jnp.bfloat16),
            pltpu.SemaphoreType.DMA((4,)),
        ],
        compiler_params=pltpu.CompilerParams(vmem_limit_bytes=16 << 20),
        name="force",
    )(*arrays, *(in_hbm(ratio) for ratio in ratios))


def shards(
    coords, atom_var, atom_weight, atoms_live, block_list, owner_map, comp_means, comp_var, comp_weight, target, noise_sigma,
):
    replicas = lax.axis_size("rep")
    domains = lax.axis_size("dom")
    share = COMP_BLOCKS // domains // replicas
    vmem = VMEM_SPEC
    small = pltpu.CompilerParams(vmem_limit_bytes=6 << 20)
    f32 = jnp.float32
    positions = coords.reshape(3 * BLK_DEV, ATOM_BLK)
    listed = block_list.T
    variances = atom_var.reshape(BLK_DEV, ATOM_BLK)
    weights = atom_weight.reshape(BLK_DEV, ATOM_BLK)
    cvar = comp_var.reshape(COMP_BLOCKS, COMP_BLK)
    cweight = comp_weight.reshape(COMP_BLOCKS, COMP_BLK)
    model, over, rows, slots, counts, comps, atoms = call_overlap(
        atoms_live, listed, owner_map, positions, variances, weights, comp_means, cvar, cweight
    )
    crowded = counts[REPLICAS] > 0
    tie = lax.optimization_barrier
    ratios = [call_ratio(atoms, comps, 0)]
    parts = lax.all_to_all(model.reshape(replicas, ROOM, COMP_BLK), "rep", 0, 0, tiled=True)
    parts, ratios[0] = tie((parts, ratios[0]))
    over_sum = lax.cond(
        crowded,
        lambda v: jnp.sum(lax.all_to_all(v.reshape(replicas, OWNED, COMP_BLK), "rep", 0, 0, tiled=True), axis=0),
        lambda v: jnp.zeros((OWNED, COMP_BLK), f32),
        over,
    )
    over_rep = pl.pallas_call(
        rep_sum_kernel,
        out_shape=jax.ShapeDtypeStruct((OWNED, COMP_BLK), f32),
        in_specs=[SMEM_SPEC, vmem, vmem], out_specs=vmem,
        scratch_shapes=[pltpu.VMEM((ROOM, COMP_BLK), f32), pltpu.VMEM((OWNED + 8, COMP_BLK), f32)],
        compiler_params=small, name="rep_sum",
    )(slots, parts, over_sum)
    over_rep, atoms = tie((over_rep, atoms))
    ratios.append(call_ratio(atoms, comps, 1))
    parts = lax.all_to_all(over_rep.reshape(domains, share, COMP_BLK), "dom", 0, 0, tiled=True)
    parts, ratios[1] = tie((parts, ratios[1]))
    spread, mean = pl.pallas_call(
        adjoint_kernel,
        out_shape=(
            jax.ShapeDtypeStruct((domains, share, COMP_BLK), f32), jax.ShapeDtypeStruct((share, COMP_BLK), f32),
        ),
        in_specs=[vmem] * 3, out_specs=(vmem, vmem), compiler_params=small, name="adjoint",
    )(parts, target.reshape(-1, COMP_BLK), noise_sigma.reshape(-1, COMP_BLK))
    spread, atoms = tie((spread, atoms))
    ratios.append(call_ratio(atoms, comps, 2))
    over_dom = lax.all_to_all(spread, "dom", 0, 0, tiled=True).reshape(domains * share, COMP_BLK)
    over_dom, ratios[2] = tie((over_dom, ratios[2]))
    over_back = lax.cond(
        crowded,
        lambda v: lax.all_to_all(jnp.broadcast_to(v[None], (replicas, OWNED, COMP_BLK)), "rep", 0, 0, tiled=True),
        lambda v: jnp.zeros((replicas, OWNED, COMP_BLK), f32),
        over_dom,
    ).reshape(-1, COMP_BLK)
    spread = pl.pallas_call(
        spread_kernel,
        out_shape=jax.ShapeDtypeStruct((replicas, ROOM + share, COMP_BLK), f32),
        in_specs=[SMEM_SPEC, vmem, vmem], out_specs=vmem,
        scratch_shapes=[pltpu.VMEM((ROOM + share, COMP_BLK), f32)],
        compiler_params=small, name="spread",
    )(slots, over_dom, mean)
    spread, atoms = tie((spread, atoms))
    ratios.append(call_ratio(atoms, comps, 3))
    returned = lax.all_to_all(spread, "rep", 0, 0, tiled=True)
    average = returned[:, ROOM:].reshape(-1)
    returned = returned.reshape(-1, COMP_BLK)

    forces = call_force(atoms_live, rows, positions, weights, comps, returned, over_back, ratios)
    return average, forces.reshape(coords.shape)


def solution(mesh):
    return jax.shard_map(
        shards,
        mesh=mesh,
        in_specs=(
            P("rep", None, "dom"), P("dom"), P("dom"), P("dom"), P("dom", None), P(), P(), P(), P(), P("dom"), P("dom"),
        ),
        out_specs=(P("dom"), P("rep", None, "dom")),
        check_vma=False,
    )
```

```python
import functools
import math

import jax
import jax.numpy as jnp
from jax import lax
from jax.experimental import pallas as pl
from jax.experimental.pallas import tpu as pltpu
from jax.sharding import PartitionSpec as P

ATOM_BLK = 128
COMP_BLK = 128
LISTED = 16
BLK_DEV = 32
COMP_BLOCKS = 2048
REPLICAS = 8
FEATS = 48
ROOM = 96
SHARE = 8
OWNED = 256
PART = 8
DEPTH = 8

ENERGY_UNIT = 2.494
EXP_SCALE = -0.5 / math.log(2.0)
NORM = (2.0 * math.pi) ** -1.5


def split3(v):
    hi = v.astype(jnp.bfloat16).astype(jnp.float32)
    rest = v - hi
    mid = rest.astype(jnp.bfloat16).astype(jnp.float32)
    return hi, mid, rest - mid


def choose(row, parts, shape, other=0.0):
    out = jnp.full(shape, other, jnp.float32)
    for k, part in enumerate(parts):
        out = jnp.where(row == k, part, out)
    return out


def right_side(comp):
    hi, mid, low = split3(comp)
    return jnp.concatenate([hi, hi, hi, mid, mid, low], axis=0).astype(jnp.bfloat16)


def spread_lanes(atoms, column):
    return jnp.broadcast_to(atoms[:, column : column + 1], (128, 128)).reshape(16, 8, 128)


def pair_terms(left, spread_var, comp_of):
    for k in range(0, LISTED, 2):
        comps = [comp_of(k), comp_of(k + 1)]
        right = jnp.concatenate([right_side(comp) for comp in comps], axis=1)
        scaled = jnp.dot(left, right, preferred_element_type=jnp.float32).reshape(16, 8, 256)
        for n in range(2):
            r = lax.rsqrt(spread_var + comps[n][5:6].reshape(1, 1, 128))
            q = r * r
            yield k + n, q, (q * r) * jnp.exp2(scaled[:, :, n * 128 : (n + 1) * 128] * q)


def overlap_kernel(
    live_any, list_any, owner_any, coords_any, var_any, weight_any, means_any, cvar_any, cweight_any,
    model_ref, over_ref, rows_ref, slots_ref, flag_ref, comps_ref, atoms_ref,
    counts_ref, sums_ref, live_ref, list_ref, owner_ref, coords_ref, var_ref, weight_ref, means_ref, cvar_ref, cweight_ref, sems,
):
    pairs = (
        (live_any, live_ref), (list_any, list_ref), (owner_any, owner_ref), (coords_any, coords_ref),
        (var_any, var_ref), (weight_any, weight_ref), (means_any, means_ref), (cvar_any, cvar_ref),
        (cweight_any, cweight_ref),
    )
    copies = [pltpu.make_async_copy(src, dst, sems.at[n]) for n, (src, dst) in enumerate(pairs)]
    for copy in copies:
        copy.start()
    shape = (8, 128)
    row = lax.broadcasted_iota(jnp.int32, shape, 0)
    lane = lax.broadcasted_iota(jnp.int32, (1, 128), 1)
    sums_ref[...] = jnp.zeros_like(sums_ref)
    for r in range(REPLICAS + 1):
        counts_ref[r] = 0

    def unused(n, _):
        slots_ref[n] = OWNED
        return 0

    lax.fori_loop(0, REPLICAS * ROOM, unused, 0, unroll=8)
    for copy in copies:
        copy.wait()

    def block(a, _):
        x, y, z = (coords_ref[pl.ds(d * BLK_DEV + a, 1), :] for d in range(3))
        norm2 = EXP_SCALE * (x * x + y * y + z * z)
        t = -2.0 * EXP_SCALE
        hi, mid, low = split3(choose(row, (t * x, t * y, t * z, EXP_SCALE, norm2), shape))
        weight = jnp.where(lane < live_ref[a], weight_ref[pl.ds(a, 1), :], 0.0)
        extra = choose(row, (var_ref[pl.ds(a, 1), :], weight), shape)
        feats = jnp.concatenate([hi, mid, low, hi, mid, hi, extra], axis=0)
        atoms_ref[a] = feats
        atoms = feats.T
        left = atoms[:, :FEATS].astype(jnp.bfloat16)
        spread_var = spread_lanes(atoms, FEATS)
        spread_weight = spread_lanes(atoms, FEATS + 1)

        def comp_of(k):
            b = list_ref[k, a]
            cols = pl.ds(pl.multiple_of(b * 128, 128), 128)
            cx, cy, cz = (means_ref[d : d + 1, cols] for d in range(3))
            norm = cx * cx + cy * cy + cz * cz
            comp = choose(row, (cx, cy, cz, norm, 1.0, cvar_ref[pl.ds(b, 1), :], cweight_ref[pl.ds(b, 1), :]), shape)
            comps_ref[a, k] = comp
            return comp

        for k, _, t in pair_terms(left, spread_var, comp_of):
            total = jnp.sum(jnp.sum(t * spread_weight, axis=0), axis=0, keepdims=True)
            place = owner_ref[list_ref[k, a]]
            rank = (place >> 3) & 7
            owned = ((place >> 6) << 3) + (place & 7)
            count = counts_ref[rank]
            counts_ref[rank] = count + 1
            fits = count < ROOM
            counts_ref[REPLICAS] = jnp.where(fits, counts_ref[REPLICAS], 1)
            slots_ref[jnp.where(fits, rank * ROOM + count, REPLICAS * ROOM)] = owned
            dense = rank * OWNED + owned
            rows_ref[k, a] = jnp.where(fits, rank * (ROOM + SHARE) + count, REPLICAS * (ROOM + SHARE) + dense)
            target = jnp.where(fits, rank * ROOM + count, REPLICAS * ROOM + dense)
            sums_ref[pl.ds(target, 1), :] += NORM * total * comps_ref[a, k, 6:7, :]
        return 0

    lax.fori_loop(0, BLK_DEV, block, 0)
    flag_ref[0] = counts_ref[REPLICAS]
    copies = [
        pltpu.make_async_copy(sums_ref.at[pl.ds(0, REPLICAS * ROOM)], model_ref, sems.at[0]),
        pltpu.make_async_copy(sums_ref.at[pl.ds(REPLICAS * ROOM, COMP_BLOCKS)], over_ref, sems.at[1]),
    ]
    for copy in copies:
        copy.start()
    for copy in copies:
        copy.wait()


def ratio_kernel(first, atoms_ref, comps_ref, ratio_any, ratio_buf, sems):
    blocks = ratio_any.shape[0]

    def store(a):
        return pltpu.make_async_copy(ratio_buf.at[a & 1], ratio_any.at[a], sems.at[a & 1])

    def block(a, _):
        @pl.when(a >= 2)
        def _():
            store(a - 2).wait()

        slot = a & 1
        row = lax.broadcasted_iota(jnp.int32, (8, 128), 0)
        own = jnp.where(row == 5, 1.0, 0.0)
        var = jnp.where(row == 4, jnp.broadcast_to(atoms_ref[first + a, FEATS : FEATS + 1, :], (8, 128)), 0.0)
        hi, mid, low = split3(var)
        sums = jnp.concatenate([hi + own, mid, low, own, jnp.zeros_like(own), own], axis=0)
        right = jnp.concatenate([atoms_ref[first + a, :FEATS, :], sums], axis=1).astype(jnp.bfloat16)
        for k in range(LISTED):
            left = right_side(comps_ref[first + a, k]).T
            both = jnp.dot(left, right, preferred_element_type=jnp.float32).reshape(16, 8, 256)
            r = lax.rsqrt(both[:, :, 128:])
            q = r * r
            ratio = ((q * q) * (r * jnp.exp2(both[:, :, :128] * q))).reshape(128, 128)
            hi = ratio.astype(jnp.bfloat16)
            rows = slice(k * 128, (k + 1) * 128)
            ratio_buf[slot, rows, :128] = hi
            ratio_buf[slot, rows, 128:] = (ratio - hi.astype(jnp.float32)).astype(jnp.bfloat16)
        store(a).start()
        return 0

    lax.fori_loop(0, blocks, block, 0)
    store(blocks - 2).wait()
    store(blocks - 1).wait()


def in_hbm(array):
    return pltpu.with_memory_space_constraint(array, pltpu.HBM)


def rep_sum_kernel(slots_ref, parts_ref, over_ref, out_ref, sum_ref, dense_ref):
    sum_ref[...] = jnp.sum(parts_ref[...], axis=0)
    dense_ref[:OWNED] = over_ref[...]
    first = lax.axis_index("rep") * ROOM
    for n in range(ROOM):
        dense_ref[pl.ds(slots_ref[first + n], 1), :] += sum_ref[n : n + 1, :]
    out_ref[...] = dense_ref[:OWNED]


def adjoint_kernel(parts_ref, target_ref, sigma_ref, spread_ref, mean_ref):
    share = mean_ref.shape[0]
    mean = jnp.sum(parts_ref[...], axis=0) / REPLICAS
    first = pl.ds(pl.multiple_of(lax.axis_index("rep") * share, share), share)
    sigma = sigma_ref[first, :]
    misfit = mean - target_ref[first, :]
    adjoint = misfit / (sigma * sigma + 0.5 * misfit * misfit) / REPLICAS
    mean_ref[...] = mean
    spread_ref[...] = jnp.broadcast_to(adjoint[None], spread_ref.shape)


def spread_kernel(slots_ref, adjoint_ref, mean_ref, out_ref, rows_ref, sems):
    first = lax.axis_index("rep") * ROOM
    for n in range(ROOM):
        rows_ref[n : n + 1, :] = adjoint_ref[pl.ds(jnp.minimum(slots_ref[first + n], OWNED - 1), 1), :]
    rows_ref[ROOM:] = mean_ref[...]
    copies = [pltpu.make_async_copy(rows_ref, out_ref.at[r], sems.at[r]) for r in range(REPLICAS)]
    for copy in copies:
        copy.start()
    for copy in copies:
        copy.wait()


def force_kernel(
    live_ref, rows_ref, coords_ref, weight_ref, comps_ref, adjoint_ref, over_ref, *refs,
):
    parts = BLK_DEV // PART
    ratio_any, (force_ref, ratio_ref, ratio_sems) = refs[:parts], refs[parts:]
    depth = ratio_ref.shape[0]
    shape = (8, 128)
    row = lax.broadcasted_iota(jnp.int32, shape, 0)
    upper = row < 4
    lane = lax.broadcasted_iota(jnp.int32, (1, 128), 1)

    def load(part, n):
        slot = (part * PART + n) % depth
        return pltpu.make_async_copy(ratio_any[part].at[n], ratio_ref.at[slot], ratio_sems.at[slot])

    def ahead(part, n):
        if n >= PART:
            part, n = part + 1, n - PART
        if part < parts:
            load(part, n).start()

    def block(part, n):
        a = part * PART + n
        load(part, n).wait()
        slot = a % depth
        rights = []
        for k in range(LISTED):
            target = rows_ref[k, a]
            beyond = target - REPLICAS * (ROOM + SHARE)
            near = adjoint_ref[pl.ds(jnp.minimum(target, REPLICAS * (ROOM + SHARE) - 1), 1), :]
            far = over_ref[pl.ds(jnp.maximum(beyond, 0), 1), :]
            cx, cy, cz, cw = (comps_ref[a, k, d : d + 1, :] for d in (0, 1, 2, 6))
            pull = (ENERGY_UNIT * NORM) * jnp.where(beyond < 0, near, far) * cw
            hi, mid, low = split3(pull * choose(row & 3, (cx, cy, cz, 1.0), shape))
            rights.append(
                jnp.concatenate([jnp.where(upper, hi, mid), jnp.where(upper, low, 0.0)], axis=0).astype(jnp.bfloat16)
            )
        total = jnp.zeros((16, 256), jnp.float32)
        for k in range(0, LISTED, 2):
            pulls = jnp.concatenate(rights[k : k + 2], axis=1)
            total += jnp.dot(pulls, ratio_ref[slot, k * 128 : (k + 2) * 128, :], preferred_element_type=jnp.float32)
        got = total[:, :128] + total[:, 128:]
        got = got[0:8] + got[8:16]
        got = got[0:4] + got[4:8]
        weight = jnp.where(lane < live_ref[a], weight_ref[pl.ds(a, 1), :], 0.0)
        for d in range(3):
            at = pl.ds(d * BLK_DEV + a, 1)
            force_ref[at, :] = weight * (coords_ref[at, :] * got[3:4] - got[d : d + 1])

    for n in range(depth - 1):
        ahead(0, n)
    for part in range(parts):
        def step(n, _, part=part):
            @pl.when(n + depth - 1 < PART)
            def _():
                load(part, n + depth - 1).start()

            if part + 1 < parts:
                @pl.when(n + depth - 1 >= PART)
                def _():
                    load(part + 1, n + depth - 1 - PART).start()

            block(part, n)
            return 0

        lax.fori_loop(0, PART, step, 0)


SMEM_SPEC = pl.BlockSpec(memory_space=pltpu.SMEM)
VMEM_SPEC = pl.BlockSpec(memory_space=pltpu.VMEM)
HBM_SPEC = pl.BlockSpec(memory_space=pltpu.HBM)


def call_overlap(*arrays):
    f32 = jnp.float32
    vmem, hbm = VMEM_SPEC, HBM_SPEC
    return pl.pallas_call(
        overlap_kernel,
        out_shape=(
            pltpu.HBM((REPLICAS * ROOM, COMP_BLK), f32),
            pltpu.HBM((COMP_BLOCKS, COMP_BLK), f32),
            jax.ShapeDtypeStruct((LISTED, BLK_DEV), jnp.int32),
            jax.ShapeDtypeStruct((REPLICAS * ROOM + 128,), jnp.int32),
            jax.ShapeDtypeStruct((1,), jnp.int32),
            jax.ShapeDtypeStruct((BLK_DEV, LISTED, 8, COMP_BLK), f32),
            jax.ShapeDtypeStruct((BLK_DEV, FEATS + 8, ATOM_BLK), f32),
        ),
        in_specs=[hbm] * 9,
        out_specs=(hbm, hbm, SMEM_SPEC, SMEM_SPEC, SMEM_SPEC, vmem, vmem),
        scratch_shapes=[
            pltpu.SMEM((REPLICAS + 1,), jnp.int32),
            pltpu.VMEM((REPLICAS * ROOM + COMP_BLOCKS, COMP_BLK), f32),
            pltpu.SMEM((BLK_DEV,), jnp.int32),
            pltpu.SMEM((LISTED, BLK_DEV), jnp.int32),
            pltpu.SMEM((COMP_BLOCKS,), jnp.int32),
            pltpu.VMEM((3 * BLK_DEV, ATOM_BLK), f32),
            pltpu.VMEM((BLK_DEV, ATOM_BLK), f32),
            pltpu.VMEM((BLK_DEV, ATOM_BLK), f32),
            pltpu.VMEM((3, COMP_BLOCKS * COMP_BLK), f32),
            pltpu.VMEM((COMP_BLOCKS, COMP_BLK), f32),
            pltpu.VMEM((COMP_BLOCKS, COMP_BLK), f32),
            pltpu.SemaphoreType.DMA((9,)),
        ],
        compiler_params=pltpu.CompilerParams(vmem_limit_bytes=20 << 20),
        name="overlap",
    )(*(in_hbm(v) for v in arrays))


def call_ratio(atoms, comps, part):
    f32 = jnp.float32
    return pl.pallas_call(
        functools.partial(ratio_kernel, part * PART),
        out_shape=pltpu.HBM((PART, LISTED * COMP_BLK, 2 * ATOM_BLK), jnp.bfloat16),
        in_specs=[VMEM_SPEC] * 2,
        out_specs=HBM_SPEC,
        scratch_shapes=[
            pltpu.VMEM((2, LISTED * COMP_BLK, 2 * ATOM_BLK), jnp.bfloat16),
            pltpu.SemaphoreType.DMA((2,)),
        ],
        compiler_params=pltpu.CompilerParams(vmem_limit_bytes=12 << 20),
        cost_estimate=pl.CostEstimate(flops=PART << 24, bytes_accessed=PART << 20, transcendentals=PART << 19),
        name="ratio",
    )(atoms, comps)


def call_force(*arrays):
    f32 = jnp.float32
    smem, vmem, hbm = SMEM_SPEC, VMEM_SPEC, HBM_SPEC
    *arrays, ratios = arrays
    return pl.pallas_call(
        force_kernel,
        out_shape=jax.ShapeDtypeStruct((3 * BLK_DEV, ATOM_BLK), f32),
        in_specs=[smem] * 2 + [vmem] * 5 + [hbm] * len(ratios),
        out_specs=vmem,
        scratch_shapes=[
            pltpu.VMEM((DEPTH, LISTED * COMP_BLK, 2 * ATOM_BLK), jnp.bfloat16),
            pltpu.SemaphoreType.DMA((DEPTH,)),
        ],
        compiler_params=pltpu.CompilerParams(vmem_limit_bytes=24 << 20),
        name="force",
    )(*arrays, *(in_hbm(ratio) for ratio in ratios))


def shards(
    coords, atom_var, atom_weight, atoms_live, block_list, owner_map, comp_means, comp_var, comp_weight, target, noise_sigma,
):
    replicas = lax.axis_size("rep")
    domains = lax.axis_size("dom")
    share = COMP_BLOCKS // domains // replicas
    vmem = VMEM_SPEC
    small = pltpu.CompilerParams(vmem_limit_bytes=6 << 20)
    f32 = jnp.float32
    positions = coords.reshape(3 * BLK_DEV, ATOM_BLK)
    listed = block_list.T
    variances = atom_var.reshape(BLK_DEV, ATOM_BLK)
    weights = atom_weight.reshape(BLK_DEV, ATOM_BLK)
    cvar = comp_var.reshape(COMP_BLOCKS, COMP_BLK)
    cweight = comp_weight.reshape(COMP_BLOCKS, COMP_BLK)
    model, over, rows, slots, flag, comps, atoms = call_overlap(
        atoms_live, listed, owner_map, positions, variances, weights, comp_means, cvar, cweight
    )
    crowded = flag[0] > 0
    tie = lax.optimization_barrier
    ratios = [call_ratio(atoms, comps, 0)]
    parts = lax.all_to_all(model.reshape(replicas, ROOM, COMP_BLK), "rep", 0, 0, tiled=True)
    parts, ratios[0] = tie((parts, ratios[0]))
    over_sum = lax.cond(
        crowded,
        lambda v: jnp.sum(lax.all_to_all(v.reshape(replicas, OWNED, COMP_BLK), "rep", 0, 0, tiled=True), axis=0),
        lambda v: jnp.zeros((OWNED, COMP_BLK), f32),
        over,
    )
    over_rep = pl.pallas_call(
        rep_sum_kernel,
        out_shape=jax.ShapeDtypeStruct((OWNED, COMP_BLK), f32),
        in_specs=[SMEM_SPEC, vmem, vmem], out_specs=vmem,
        scratch_shapes=[pltpu.VMEM((ROOM, COMP_BLK), f32), pltpu.VMEM((OWNED + 8, COMP_BLK), f32)],
        compiler_params=small, name="rep_sum",
    )(slots, parts, over_sum)
    over_rep, atoms = tie((over_rep, atoms))
    ratios.append(call_ratio(atoms, comps, 1))
    parts = lax.all_to_all(over_rep.reshape(domains, share, COMP_BLK), "dom", 0, 0, tiled=True)
    parts, ratios[1] = tie((parts, ratios[1]))
    spread, mean = pl.pallas_call(
        adjoint_kernel,
        out_shape=(
            jax.ShapeDtypeStruct((domains, share, COMP_BLK), f32), jax.ShapeDtypeStruct((share, COMP_BLK), f32),
        ),
        in_specs=[vmem] * 3, out_specs=(vmem, vmem), compiler_params=small, name="adjoint",
    )(parts, target.reshape(-1, COMP_BLK), noise_sigma.reshape(-1, COMP_BLK))
    spread, atoms = tie((spread, atoms))
    ratios.append(call_ratio(atoms, comps, 2))
    over_dom = lax.all_to_all(spread, "dom", 0, 0, tiled=True).reshape(domains * share, COMP_BLK)
    over_dom, ratios[2] = tie((over_dom, ratios[2]))
    over_back = lax.cond(
        crowded,
        lambda v: lax.all_to_all(jnp.broadcast_to(v[None], (replicas, OWNED, COMP_BLK)), "rep", 0, 0, tiled=True),
        lambda v: jnp.zeros((replicas, OWNED, COMP_BLK), f32),
        over_dom,
    ).reshape(-1, COMP_BLK)
    spread = pl.pallas_call(
        spread_kernel,
        out_shape=pltpu.HBM((replicas, ROOM + share, COMP_BLK), f32),
        in_specs=[SMEM_SPEC, vmem, vmem], out_specs=HBM_SPEC,
        scratch_shapes=[pltpu.VMEM((ROOM + share, COMP_BLK), f32), pltpu.SemaphoreType.DMA((replicas,))],
        compiler_params=small, name="spread",
    )(slots, over_dom, mean)
    spread, atoms = tie((spread, atoms))
    ratios.append(call_ratio(atoms, comps, 3))
    returned = lax.all_to_all(spread, "rep", 0, 0, tiled=True)
    average = returned[:, ROOM:].reshape(-1)
    returned = returned.reshape(-1, COMP_BLK)

    forces = call_force(atoms_live, rows, positions, weights, comps, returned, over_back, ratios)
    return average, forces.reshape(coords.shape)


def solution(mesh):
    return jax.shard_map(
        shards,
        mesh=mesh,
        in_specs=(
            P("rep", None, "dom"), P("dom"), P("dom"), P("dom"), P("dom", None), P(), P(), P(), P(), P("dom"), P("dom"),
        ),
        out_specs=(P("dom"), P("rep", None, "dom")),
        check_vma=False,
    )
```

```python
import functools
import math

import jax
import jax.numpy as jnp
from jax import lax
from jax.experimental import pallas as pl
from jax.experimental.pallas import tpu as pltpu
from jax.sharding import PartitionSpec as P

ATOM_BLK = 128
COMP_BLK = 128
LISTED = 16
BLK_DEV = 32
COMP_BLOCKS = 2048
REPLICAS = 8
FEATS = 48
ROOM = 96
SHARE = 8
OWNED = 256
PART = 8
DEPTH = 8
ROW_STEPS = (64, 80, 96, 112, 128)

ENERGY_UNIT = 2.494
EXP_SCALE = -0.5 / math.log(2.0)
NORM = (2.0 * math.pi) ** -1.5


def split3(v):
    hi = v.astype(jnp.bfloat16).astype(jnp.float32)
    rest = v - hi
    mid = rest.astype(jnp.bfloat16).astype(jnp.float32)
    return hi, mid, rest - mid


def choose(row, parts, shape, other=0.0):
    out = jnp.full(shape, other, jnp.float32)
    for k, part in enumerate(parts):
        out = jnp.where(row == k, part, out)
    return out


def right_side(comp):
    hi, mid, low = split3(comp)
    return jnp.concatenate([hi, hi, hi, mid, mid, low], axis=0).astype(jnp.bfloat16)


def spread_lanes(atoms, column):
    rows = atoms.shape[0]
    return jnp.broadcast_to(atoms[:, column : column + 1], (rows, 128)).reshape(rows // 8, 8, 128)


def pair_terms(left, spread_var, comp_of):
    for k in range(0, LISTED, 2):
        comps = [comp_of(k), comp_of(k + 1)]
        right = jnp.concatenate([right_side(comp) for comp in comps], axis=1)
        scaled = jnp.dot(left, right, preferred_element_type=jnp.float32).reshape(-1, 8, 256)
        for n in range(2):
            r = lax.rsqrt(spread_var + comps[n][5:6].reshape(1, 1, 128))
            q = r * r
            yield k + n, q, (q * r) * jnp.exp2(scaled[:, :, n * 128 : (n + 1) * 128] * q)


def overlap_kernel(
    live_any, list_any, owner_any, coords_any, var_any, weight_any, means_any, cvar_any, cweight_any,
    model_ref, over_ref, rows_ref, slots_ref, flag_ref, comps_ref, atoms_ref,
    counts_ref, sums_ref, live_ref, list_ref, owner_ref, coords_ref, var_ref, weight_ref, means_ref, cvar_ref, cweight_ref, sems,
):
    pairs = (
        (live_any, live_ref), (list_any, list_ref), (owner_any, owner_ref), (coords_any, coords_ref),
        (var_any, var_ref), (weight_any, weight_ref), (means_any, means_ref), (cvar_any, cvar_ref),
        (cweight_any, cweight_ref),
    )
    copies = [pltpu.make_async_copy(src, dst, sems.at[n]) for n, (src, dst) in enumerate(pairs)]
    for copy in copies:
        copy.start()
    shape = (8, 128)
    row = lax.broadcasted_iota(jnp.int32, shape, 0)
    lane = lax.broadcasted_iota(jnp.int32, (1, 128), 1)
    sums_ref[...] = jnp.zeros_like(sums_ref)
    for r in range(REPLICAS):
        counts_ref[r] = r * ROOM

    def unused(n, _):
        slots_ref[n] = OWNED
        return 0

    lax.fori_loop(0, REPLICAS * ROOM, unused, 0, unroll=8)
    for copy in copies:
        copy.wait()

    def rows_of_block(a, rows):
        x, y, z = (coords_ref[pl.ds(d * BLK_DEV + a, 1), :] for d in range(3))
        norm2 = EXP_SCALE * (x * x + y * y + z * z)
        t = -2.0 * EXP_SCALE
        hi, mid, low = split3(choose(row, (t * x, t * y, t * z, EXP_SCALE, norm2), shape))
        weight = jnp.where(lane < live_ref[a], weight_ref[pl.ds(a, 1), :], 0.0)
        extra = choose(row, (var_ref[pl.ds(a, 1), :], weight), shape)
        feats = jnp.concatenate([hi, mid, low, hi, mid, hi, extra], axis=0)
        atoms_ref[a] = feats
        atoms = feats.T[:rows]
        left = atoms[:, :FEATS].astype(jnp.bfloat16)
        spread_var = spread_lanes(atoms, FEATS)
        spread_weight = spread_lanes(atoms, FEATS + 1)

        def comp_of(k):
            b = list_ref[k, a]
            cols = pl.ds(pl.multiple_of(b * 128, 128), 128)
            cx, cy, cz = (means_ref[d : d + 1, cols] for d in range(3))
            norm = cx * cx + cy * cy + cz * cz
            comp = choose(row, (cx, cy, cz, norm, 1.0, cvar_ref[pl.ds(b, 1), :], cweight_ref[pl.ds(b, 1), :]), shape)
            comps_ref[a, k] = comp
            return comp

        for k, _, t in pair_terms(left, spread_var, comp_of):
            total = jnp.sum(jnp.sum(t * spread_weight, axis=0), axis=0, keepdims=True)
            place = owner_ref[list_ref[k, a]]
            rank = (place >> 3) & 7
            owned = ((place >> 6) << 3) + (place & 7)
            place = counts_ref[rank]
            counts_ref[rank] = place + 1
            fits = place < rank * ROOM + ROOM
            target = jnp.where(fits, place, rank * OWNED + owned + REPLICAS * ROOM)
            slots_ref[target] = owned
            rows_ref[k, a] = target + jnp.where(fits, rank * SHARE, REPLICAS * SHARE)
            sums_ref[pl.ds(target, 1), :] += NORM * total * comps_ref[a, k, 6:7, :]

    def block(a, _):
        step = jnp.clip((live_ref[a] - ROW_STEPS[0] + 15) // 16, 0, len(ROW_STEPS) - 1)
        lax.switch(step, [functools.partial(rows_of_block, a, rows) for rows in ROW_STEPS])
        return 0

    lax.fori_loop(0, BLK_DEV, block, 0)
    crowded = jnp.int32(0)
    for r in range(REPLICAS):
        crowded = jnp.where(counts_ref[r] > (r + 1) * ROOM, 1, crowded)
    flag_ref[0] = crowded
    copies = [
        pltpu.make_async_copy(sums_ref.at[pl.ds(0, REPLICAS * ROOM)], model_ref, sems.at[0]),
        pltpu.make_async_copy(sums_ref.at[pl.ds(REPLICAS * ROOM, COMP_BLOCKS)], over_ref, sems.at[1]),
    ]
    for copy in copies:
        copy.start()
    for copy in copies:
        copy.wait()


def ratio_kernel(first, atoms_ref, comps_ref, ratio_any, ratio_buf, sems):
    blocks = ratio_any.shape[0]

    def store(a):
        return pltpu.make_async_copy(ratio_buf.at[a & 1], ratio_any.at[a], sems.at[a & 1])

    def block(a, _):
        @pl.when(a >= 2)
        def _():
            store(a - 2).wait()

        slot = a & 1
        row = lax.broadcasted_iota(jnp.int32, (8, 128), 0)
        own = jnp.where(row == 5, 1.0, 0.0)
        var = jnp.where(row == 4, jnp.broadcast_to(atoms_ref[first + a, FEATS : FEATS + 1, :], (8, 128)), 0.0)
        hi, mid, low = split3(var)
        sums = jnp.concatenate([hi + own, mid, low, own, jnp.zeros_like(own), own], axis=0)
        right = jnp.concatenate([atoms_ref[first + a, :FEATS, :], sums], axis=1).astype(jnp.bfloat16)
        for k in range(LISTED):
            left = right_side(comps_ref[first + a, k]).T
            both = jnp.dot(left, right, preferred_element_type=jnp.float32).reshape(16, 8, 256)
            r = lax.rsqrt(both[:, :, 128:])
            q = r * r
            ratio = ((q * q) * (r * jnp.exp2(both[:, :, :128] * q))).reshape(128, 128)
            hi = ratio.astype(jnp.bfloat16)
            rows = slice(k * 128, (k + 1) * 128)
            ratio_buf[slot, rows, :128] = hi
            ratio_buf[slot, rows, 128:] = (ratio - hi.astype(jnp.float32)).astype(jnp.bfloat16)
        store(a).start()
        return 0

    lax.fori_loop(0, blocks, block, 0)
    store(blocks - 2).wait()
    store(blocks - 1).wait()


def in_hbm(array):
    return pltpu.with_memory_space_constraint(array, pltpu.HBM)


def rep_sum_kernel(slots_ref, parts_ref, over_ref, out_ref, sum_ref, dense_ref):
    sum_ref[...] = jnp.sum(parts_ref[...], axis=0)
    dense_ref[:OWNED] = over_ref[...]
    first = lax.axis_index("rep") * ROOM
    for n in range(ROOM):
        dense_ref[pl.ds(slots_ref[first + n], 1), :] += sum_ref[n : n + 1, :]
    out_ref[...] = dense_ref[:OWNED]


def adjoint_kernel(parts_ref, target_ref, sigma_ref, spread_ref, mean_ref):
    share = mean_ref.shape[0]
    mean = jnp.sum(parts_ref[...], axis=0) / REPLICAS
    first = pl.ds(pl.multiple_of(lax.axis_index("rep") * share, share), share)
    sigma = sigma_ref[first, :]
    misfit = mean - target_ref[first, :]
    adjoint = misfit / (sigma * sigma + 0.5 * misfit * misfit) / REPLICAS
    mean_ref[...] = mean
    spread_ref[...] = jnp.broadcast_to(adjoint[None], spread_ref.shape)


def spread_kernel(slots_ref, adjoint_ref, mean_ref, out_ref, rows_ref, sems):
    first = lax.axis_index("rep") * ROOM
    for n in range(ROOM):
        rows_ref[n : n + 1, :] = adjoint_ref[pl.ds(jnp.minimum(slots_ref[first + n], OWNED - 1), 1), :]
    rows_ref[ROOM:] = mean_ref[...]
    copies = [pltpu.make_async_copy(rows_ref, out_ref.at[r], sems.at[r]) for r in range(REPLICAS)]
    for copy in copies:
        copy.start()
    for copy in copies:
        copy.wait()


def force_kernel(
    live_ref, rows_ref, coords_ref, weight_ref, comps_ref, adjoint_ref, over_ref, *refs,
):
    parts = BLK_DEV // PART
    ratio_any, (force_ref, ratio_ref, ratio_sems) = refs[:parts], refs[parts:]
    depth = ratio_ref.shape[0]
    shape = (8, 128)
    row = lax.broadcasted_iota(jnp.int32, shape, 0)
    upper = row < 4
    lane = lax.broadcasted_iota(jnp.int32, (1, 128), 1)

    def load(part, n):
        slot = (part * PART + n) % depth
        return pltpu.make_async_copy(ratio_any[part].at[n], ratio_ref.at[slot], ratio_sems.at[slot])

    def ahead(part, n):
        if n >= PART:
            part, n = part + 1, n - PART
        if part < parts:
            load(part, n).start()

    def block(part, n):
        a = part * PART + n
        load(part, n).wait()
        slot = a % depth
        rights = []
        for k in range(LISTED):
            target = rows_ref[k, a]
            beyond = target - REPLICAS * (ROOM + SHARE)
            near = adjoint_ref[pl.ds(jnp.minimum(target, REPLICAS * (ROOM + SHARE) - 1), 1), :]
            far = over_ref[pl.ds(jnp.maximum(beyond, 0), 1), :]
            cx, cy, cz, cw = (comps_ref[a, k, d : d + 1, :] for d in (0, 1, 2, 6))
            pull = (ENERGY_UNIT * NORM) * jnp.where(beyond < 0, near, far) * cw
            hi, mid, low = split3(pull * choose(row & 3, (cx, cy, cz, 1.0), shape))
            rights.append(
                jnp.concatenate([jnp.where(upper, hi, mid), jnp.where(upper, low, 0.0)], axis=0).astype(jnp.bfloat16)
            )
        total = jnp.zeros((16, 256), jnp.float32)
        for k in range(0, LISTED, 2):
            pulls = jnp.concatenate(rights[k : k + 2], axis=1)
            total += jnp.dot(pulls, ratio_ref[slot, k * 128 : (k + 2) * 128, :], preferred_element_type=jnp.float32)
        got = total[:, :128] + total[:, 128:]
        got = got[0:8] + got[8:16]
        got = got[0:4] + got[4:8]
        weight = jnp.where(lane < live_ref[a], weight_ref[pl.ds(a, 1), :], 0.0)
        for d in range(3):
            at = pl.ds(d * BLK_DEV + a, 1)
            force_ref[at, :] = weight * (coords_ref[at, :] * got[3:4] - got[d : d + 1])

    for n in range(depth - 1):
        ahead(0, n)
    for part in range(parts):
        def step(n, _, part=part):
            @pl.when(n + depth - 1 < PART)
            def _():
                load(part, n + depth - 1).start()

            if part + 1 < parts:
                @pl.when(n + depth - 1 >= PART)
                def _():
                    load(part + 1, n + depth - 1 - PART).start()

            block(part, n)
            return 0

        lax.fori_loop(0, PART, step, 0)


SMEM_SPEC = pl.BlockSpec(memory_space=pltpu.SMEM)
VMEM_SPEC = pl.BlockSpec(memory_space=pltpu.VMEM)
HBM_SPEC = pl.BlockSpec(memory_space=pltpu.HBM)


def call_overlap(*arrays):
    f32 = jnp.float32
    vmem, hbm = VMEM_SPEC, HBM_SPEC
    return pl.pallas_call(
        overlap_kernel,
        out_shape=(
            pltpu.HBM((REPLICAS * ROOM, COMP_BLK), f32),
            pltpu.HBM((COMP_BLOCKS, COMP_BLK), f32),
            jax.ShapeDtypeStruct((LISTED, BLK_DEV), jnp.int32),
            jax.ShapeDtypeStruct((REPLICAS * ROOM + COMP_BLOCKS,), jnp.int32),
            jax.ShapeDtypeStruct((1,), jnp.int32),
            jax.ShapeDtypeStruct((BLK_DEV, LISTED, 8, COMP_BLK), f32),
            jax.ShapeDtypeStruct((BLK_DEV, FEATS + 8, ATOM_BLK), f32),
        ),
        in_specs=[hbm] * 9,
        out_specs=(hbm, hbm, SMEM_SPEC, SMEM_SPEC, SMEM_SPEC, vmem, vmem),
        scratch_shapes=[
            pltpu.SMEM((REPLICAS,), jnp.int32),
            pltpu.VMEM((REPLICAS * ROOM + COMP_BLOCKS, COMP_BLK), f32),
            pltpu.SMEM((BLK_DEV,), jnp.int32),
            pltpu.SMEM((LISTED, BLK_DEV), jnp.int32),
            pltpu.SMEM((COMP_BLOCKS,), jnp.int32),
            pltpu.VMEM((3 * BLK_DEV, ATOM_BLK), f32),
            pltpu.VMEM((BLK_DEV, ATOM_BLK), f32),
            pltpu.VMEM((BLK_DEV, ATOM_BLK), f32),
            pltpu.VMEM((3, COMP_BLOCKS * COMP_BLK), f32),
            pltpu.VMEM((COMP_BLOCKS, COMP_BLK), f32),
            pltpu.VMEM((COMP_BLOCKS, COMP_BLK), f32),
            pltpu.SemaphoreType.DMA((9,)),
        ],
        compiler_params=pltpu.CompilerParams(vmem_limit_bytes=20 << 20),
        name="overlap",
    )(*(in_hbm(v) for v in arrays))


def call_ratio(atoms, comps, part):
    f32 = jnp.float32
    return pl.pallas_call(
        functools.partial(ratio_kernel, part * PART),
        out_shape=pltpu.HBM((PART, LISTED * COMP_BLK, 2 * ATOM_BLK), jnp.bfloat16),
        in_specs=[VMEM_SPEC] * 2,
        out_specs=HBM_SPEC,
        scratch_shapes=[
            pltpu.VMEM((2, LISTED * COMP_BLK, 2 * ATOM_BLK), jnp.bfloat16),
            pltpu.SemaphoreType.DMA((2,)),
        ],
        compiler_params=pltpu.CompilerParams(vmem_limit_bytes=12 << 20),
        cost_estimate=pl.CostEstimate(flops=PART << 24, bytes_accessed=PART << 20, transcendentals=PART << 19),
        name="ratio",
    )(atoms, comps)


def call_force(*arrays):
    f32 = jnp.float32
    smem, vmem, hbm = SMEM_SPEC, VMEM_SPEC, HBM_SPEC
    *arrays, ratios = arrays
    return pl.pallas_call(
        force_kernel,
        out_shape=jax.ShapeDtypeStruct((3 * BLK_DEV, ATOM_BLK), f32),
        in_specs=[smem] * 2 + [vmem] * 5 + [hbm] * len(ratios),
        out_specs=vmem,
        scratch_shapes=[
            pltpu.VMEM((DEPTH, LISTED * COMP_BLK, 2 * ATOM_BLK), jnp.bfloat16),
            pltpu.SemaphoreType.DMA((DEPTH,)),
        ],
        compiler_params=pltpu.CompilerParams(vmem_limit_bytes=24 << 20),
        name="force",
    )(*arrays, *(in_hbm(ratio) for ratio in ratios))


def shards(
    coords, atom_var, atom_weight, atoms_live, block_list, owner_map, comp_means, comp_var, comp_weight, target, noise_sigma,
):
    replicas = lax.axis_size("rep")
    domains = lax.axis_size("dom")
    share = COMP_BLOCKS // domains // replicas
    vmem = VMEM_SPEC
    small = pltpu.CompilerParams(vmem_limit_bytes=6 << 20)
    f32 = jnp.float32
    positions = coords.reshape(3 * BLK_DEV, ATOM_BLK)
    listed = block_list.T
    variances = atom_var.reshape(BLK_DEV, ATOM_BLK)
    weights = atom_weight.reshape(BLK_DEV, ATOM_BLK)
    cvar = comp_var.reshape(COMP_BLOCKS, COMP_BLK)
    cweight = comp_weight.reshape(COMP_BLOCKS, COMP_BLK)
    model, over, rows, slots, flag, comps, atoms = call_overlap(
        atoms_live, listed, owner_map, positions, variances, weights, comp_means, cvar, cweight
    )
    crowded = flag[0] > 0
    tie = lax.optimization_barrier
    ratios = [call_ratio(atoms, comps, 0)]
    parts = lax.all_to_all(model.reshape(replicas, ROOM, COMP_BLK), "rep", 0, 0, tiled=True)
    parts, ratios[0] = tie((parts, ratios[0]))
    over_sum = lax.cond(
        crowded,
        lambda v: jnp.sum(lax.all_to_all(v.reshape(replicas, OWNED, COMP_BLK), "rep", 0, 0, tiled=True), axis=0),
        lambda v: jnp.zeros((OWNED, COMP_BLK), f32),
        over,
    )
    over_rep = pl.pallas_call(
        rep_sum_kernel,
        out_shape=jax.ShapeDtypeStruct((OWNED, COMP_BLK), f32),
        in_specs=[SMEM_SPEC, vmem, vmem], out_specs=vmem,
        scratch_shapes=[pltpu.VMEM((ROOM, COMP_BLK), f32), pltpu.VMEM((OWNED + 8, COMP_BLK), f32)],
        compiler_params=small, name="rep_sum",
    )(slots, parts, over_sum)
    over_rep, atoms = tie((over_rep, atoms))
    ratios.append(call_ratio(atoms, comps, 1))
    parts = lax.all_to_all(over_rep.reshape(domains, share, COMP_BLK), "dom", 0, 0, tiled=True)
    parts, ratios[1] = tie((parts, ratios[1]))
    spread, mean = pl.pallas_call(
        adjoint_kernel,
        out_shape=(
            jax.ShapeDtypeStruct((domains, share, COMP_BLK), f32), jax.ShapeDtypeStruct((share, COMP_BLK), f32),
        ),
        in_specs=[vmem] * 3, out_specs=(vmem, vmem), compiler_params=small, name="adjoint",
    )(parts, target.reshape(-1, COMP_BLK), noise_sigma.reshape(-1, COMP_BLK))
    spread, atoms = tie((spread, atoms))
    ratios.append(call_ratio(atoms, comps, 2))
    over_dom = lax.all_to_all(spread, "dom", 0, 0, tiled=True).reshape(domains * share, COMP_BLK)
    over_dom, ratios[2] = tie((over_dom, ratios[2]))
    over_back = lax.cond(
        crowded,
        lambda v: lax.all_to_all(jnp.broadcast_to(v[None], (replicas, OWNED, COMP_BLK)), "rep", 0, 0, tiled=True),
        lambda v: jnp.zeros((replicas, OWNED, COMP_BLK), f32),
        over_dom,
    ).reshape(-1, COMP_BLK)
    spread = pl.pallas_call(
        spread_kernel,
        out_shape=pltpu.HBM((replicas, ROOM + share, COMP_BLK), f32),
        in_specs=[SMEM_SPEC, vmem, vmem], out_specs=HBM_SPEC,
        scratch_shapes=[pltpu.VMEM((ROOM + share, COMP_BLK), f32), pltpu.SemaphoreType.DMA((replicas,))],
        compiler_params=small, name="spread",
    )(slots, over_dom, mean)
    spread, atoms = tie((spread, atoms))
    ratios.append(call_ratio(atoms, comps, 3))
    returned = lax.all_to_all(spread, "rep", 0, 0, tiled=True)
    average = returned[:, ROOM:].reshape(-1)
    returned = returned.reshape(-1, COMP_BLK)

    forces = call_force(atoms_live, rows, positions, weights, comps, returned, over_back, ratios)
    return average, forces.reshape(coords.shape)


def solution(mesh):
    return jax.shard_map(
        shards,
        mesh=mesh,
        in_specs=(
            P("rep", None, "dom"), P("dom"), P("dom"), P("dom"), P("dom", None), P(), P(), P(), P(), P("dom"), P("dom"),
        ),
        out_specs=(P("dom"), P("rep", None, "dom")),
        check_vma=False,
    )
```

```python
import functools
import math

import jax
import jax.numpy as jnp
from jax import lax
from jax.experimental import pallas as pl
from jax.experimental.pallas import tpu as pltpu
from jax.sharding import PartitionSpec as P

ATOM_BLK = 128
COMP_BLK = 128
LISTED = 16
BLK_DEV = 32
COMP_BLOCKS = 2048
REPLICAS = 8
FEATS = 48
ROOM = 96
SHARE = 8
OWNED = 256
PART = 8
DEPTH = 8
ROW_STEPS = (64, 80, 96, 112, 128)

ENERGY_UNIT = 2.494
EXP_SCALE = -0.5 / math.log(2.0)
NORM = (2.0 * math.pi) ** -1.5


def split3(v):
    hi = v.astype(jnp.bfloat16).astype(jnp.float32)
    rest = v - hi
    mid = rest.astype(jnp.bfloat16).astype(jnp.float32)
    return hi, mid, rest - mid


def choose(row, parts, shape, other=0.0):
    out = jnp.full(shape, other, jnp.float32)
    for k, part in enumerate(parts):
        out = jnp.where(row == k, part, out)
    return out


def right_side(comp):
    hi, mid, low = split3(comp)
    return jnp.concatenate([hi, hi, hi, mid, mid, low], axis=0).astype(jnp.bfloat16)


def spread_lanes(atoms, column):
    rows = atoms.shape[0]
    return jnp.broadcast_to(atoms[:, column : column + 1], (rows, 128)).reshape(rows // 8, 8, 128)


def pair_terms(left, spread_var, comp_of):
    for k in range(0, LISTED, 2):
        comps = [comp_of(k), comp_of(k + 1)]
        right = jnp.concatenate([right_side(comp) for comp in comps], axis=1)
        scaled = jnp.dot(left, right, preferred_element_type=jnp.float32).reshape(-1, 8, 256)
        for n in range(2):
            r = lax.rsqrt(spread_var + comps[n][5:6].reshape(1, 1, 128))
            q = r * r
            yield k + n, q, (q * r) * jnp.exp2(scaled[:, :, n * 128 : (n + 1) * 128] * q)


def overlap_kernel(
    live_any, list_any, owner_any, coords_any, var_any, weight_any, means_any, cvar_any, cweight_any,
    model_ref, over_ref, rows_ref, slots_ref, flag_ref, comps_ref, atoms_ref,
    counts_ref, sums_ref, live_ref, list_ref, owner_ref, coords_ref, var_ref, weight_ref, means_ref, cvar_ref, cweight_ref, sems,
):
    pairs = (
        (live_any, live_ref), (list_any, list_ref), (owner_any, owner_ref), (coords_any, coords_ref),
        (var_any, var_ref), (weight_any, weight_ref), (means_any, means_ref), (cvar_any, cvar_ref),
        (cweight_any, cweight_ref),
    )
    copies = [pltpu.make_async_copy(src, dst, sems.at[n]) for n, (src, dst) in enumerate(pairs)]
    for copy in copies:
        copy.start()
    shape = (8, 128)
    row = lax.broadcasted_iota(jnp.int32, shape, 0)
    lane = lax.broadcasted_iota(jnp.int32, (1, 128), 1)
    sums_ref[...] = jnp.zeros_like(sums_ref)
    for r in range(REPLICAS):
        counts_ref[r] = r * ROOM

    def unused(n, _):
        slots_ref[n] = OWNED
        return 0

    lax.fori_loop(0, REPLICAS * ROOM, unused, 0, unroll=8)
    for copy in copies:
        copy.wait()

    def rows_of_block(a, rows):
        x, y, z = (coords_ref[pl.ds(d * BLK_DEV + a, 1), :] for d in range(3))
        norm2 = EXP_SCALE * (x * x + y * y + z * z)
        t = -2.0 * EXP_SCALE
        hi, mid, low = split3(choose(row, (t * x, t * y, t * z, EXP_SCALE, norm2), shape))
        weight = jnp.where(lane < live_ref[a], weight_ref[pl.ds(a, 1), :], 0.0)
        extra = choose(row, (var_ref[pl.ds(a, 1), :], weight), shape)
        feats = jnp.concatenate([hi, mid, low, hi, mid, hi, extra], axis=0)
        atoms_ref[a] = feats
        atoms = feats.T[:rows]
        left = atoms[:, :FEATS].astype(jnp.bfloat16)
        spread_var = spread_lanes(atoms, FEATS)
        spread_weight = spread_lanes(atoms, FEATS + 1)

        def comp_of(k):
            b = list_ref[k, a]
            cols = pl.ds(pl.multiple_of(b * 128, 128), 128)
            cx, cy, cz = (means_ref[d : d + 1, cols] for d in range(3))
            norm = cx * cx + cy * cy + cz * cz
            comp = choose(row, (cx, cy, cz, norm, 1.0, cvar_ref[pl.ds(b, 1), :], cweight_ref[pl.ds(b, 1), :]), shape)
            comps_ref[a, k] = comp
            return comp

        for k, _, t in pair_terms(left, spread_var, comp_of):
            total = jnp.sum(jnp.sum(t * spread_weight, axis=0), axis=0, keepdims=True)
            place = owner_ref[list_ref[k, a]]
            rank = (place >> 3) & 7
            owned = ((place >> 6) << 3) + (place & 7)
            place = counts_ref[rank]
            counts_ref[rank] = place + 1
            fits = place < rank * ROOM + ROOM
            target = jnp.where(fits, place, rank * OWNED + owned + REPLICAS * ROOM)
            slots_ref[target] = owned
            rows_ref[k, a] = target + jnp.where(fits, rank * SHARE, REPLICAS * SHARE)
            sums_ref[pl.ds(target, 1), :] += NORM * total * comps_ref[a, k, 6:7, :]

    def block(a, _):
        step = jnp.clip((live_ref[a] - ROW_STEPS[0] + 15) // 16, 0, len(ROW_STEPS) - 1)
        lax.switch(step, [functools.partial(rows_of_block, a, rows) for rows in ROW_STEPS])
        return 0

    lax.fori_loop(0, BLK_DEV, block, 0)
    crowded = jnp.int32(0)
    for r in range(REPLICAS):
        crowded = jnp.where(counts_ref[r] > (r + 1) * ROOM, 1, crowded)
    flag_ref[0] = crowded
    copies = [
        pltpu.make_async_copy(sums_ref.at[pl.ds(0, REPLICAS * ROOM)], model_ref, sems.at[0]),
        pltpu.make_async_copy(sums_ref.at[pl.ds(REPLICAS * ROOM, COMP_BLOCKS)], over_ref, sems.at[1]),
    ]
    for copy in copies:
        copy.start()
    for copy in copies:
        copy.wait()


def ratio_kernel(first, atoms_ref, comps_ref, ratio_any, ratio_buf, sems):
    blocks = ratio_any.shape[0]

    def store(a):
        return pltpu.make_async_copy(ratio_buf.at[a & 1], ratio_any.at[a], sems.at[a & 1])

    def block(a, _):
        @pl.when(a >= 2)
        def _():
            store(a - 2).wait()

        slot = a & 1
        row = lax.broadcasted_iota(jnp.int32, (8, 128), 0)
        own = jnp.where(row == 5, 1.0, 0.0)
        var = jnp.where(row == 4, jnp.broadcast_to(atoms_ref[first + a, FEATS : FEATS + 1, :], (8, 128)), 0.0)
        hi, mid, low = split3(var)
        sums = jnp.concatenate([hi + own, mid, low, own, jnp.zeros_like(own), own], axis=0)
        right = jnp.concatenate([atoms_ref[first + a, :FEATS, :], sums], axis=1).astype(jnp.bfloat16)
        for k in range(LISTED):
            left = right_side(comps_ref[first + a, k]).T
            both = jnp.dot(left, right, preferred_element_type=jnp.float32).reshape(16, 8, 256)
            r = lax.rsqrt(both[:, :, 128:])
            q = r * r
            ratio = ((q * q) * (r * jnp.exp2(both[:, :, :128] * q))).reshape(128, 128)
            hi = ratio.astype(jnp.bfloat16)
            rows = slice(k * 128, (k + 1) * 128)
            ratio_buf[slot, rows, :128] = hi
            ratio_buf[slot, rows, 128:] = (ratio - hi.astype(jnp.float32)).astype(jnp.bfloat16)
        store(a).start()
        return 0

    lax.fori_loop(0, blocks, block, 0)
    store(blocks - 2).wait()
    store(blocks - 1).wait()


def in_hbm(array):
    return pltpu.with_memory_space_constraint(array, pltpu.HBM)


def rep_sum_kernel(slots_ref, parts_ref, over_ref, out_ref, sum_ref, dense_ref):
    sum_ref[...] = jnp.sum(parts_ref[...], axis=0)
    dense_ref[:OWNED] = over_ref[...]
    first = lax.axis_index("rep") * ROOM
    for n in range(ROOM):
        dense_ref[pl.ds(slots_ref[first + n], 1), :] += sum_ref[n : n + 1, :]
    out_ref[...] = dense_ref[:OWNED]


def adjoint_kernel(parts_ref, target_ref, sigma_ref, spread_ref, mean_ref):
    share = mean_ref.shape[0]
    mean = jnp.sum(parts_ref[...], axis=0) / REPLICAS
    first = pl.ds(pl.multiple_of(lax.axis_index("rep") * share, share), share)
    sigma = sigma_ref[first, :]
    misfit = mean - target_ref[first, :]
    adjoint = misfit / (sigma * sigma + 0.5 * misfit * misfit) / REPLICAS
    mean_ref[...] = mean
    spread_ref[...] = jnp.broadcast_to(adjoint[None], spread_ref.shape)


def spread_kernel(slots_ref, adjoint_ref, mean_ref, out_ref, rows_ref, sems):
    first = lax.axis_index("rep") * ROOM
    for n in range(ROOM):
        rows_ref[n : n + 1, :] = adjoint_ref[pl.ds(jnp.minimum(slots_ref[first + n], OWNED - 1), 1), :]
    rows_ref[ROOM:] = mean_ref[...]
    copies = [pltpu.make_async_copy(rows_ref, out_ref.at[r], sems.at[r]) for r in range(REPLICAS)]
    for copy in copies:
        copy.start()
    for copy in copies:
        copy.wait()


def force_kernel(
    live_ref, rows_ref, coords_ref, weight_ref, comps_ref, adjoint_ref, over_ref, *refs,
):
    parts = BLK_DEV // PART
    ratio_any, (force_ref, ratio_ref, ratio_sems) = refs[:parts], refs[parts:]
    depth = ratio_ref.shape[0]
    shape = (8, 128)
    row = lax.broadcasted_iota(jnp.int32, shape, 0)
    upper = row < 4
    lane = lax.broadcasted_iota(jnp.int32, (1, 128), 1)

    def load(part, n):
        slot = (part * PART + n) % depth
        return pltpu.make_async_copy(ratio_any[part].at[n], ratio_ref.at[slot], ratio_sems.at[slot])

    def ahead(part, n):
        if n >= PART:
            part, n = part + 1, n - PART
        if part < parts:
            load(part, n).start()

    def block(part, n):
        a = part * PART + n
        load(part, n).wait()
        slot = a % depth
        rights = []
        for k in range(LISTED):
            target = rows_ref[k, a]
            beyond = target - REPLICAS * (ROOM + SHARE)
            near = adjoint_ref[pl.ds(jnp.minimum(target, REPLICAS * (ROOM + SHARE) - 1), 1), :]
            far = over_ref[pl.ds(jnp.maximum(beyond, 0), 1), :]
            cx, cy, cz, cw = (comps_ref[a, k, d : d + 1, :] for d in (0, 1, 2, 6))
            pull = (ENERGY_UNIT * NORM) * jnp.where(beyond < 0, near, far) * cw
            hi, mid, low = split3(pull * choose(row & 3, (cx, cy, cz, 1.0), shape))
            rights.append(
                jnp.concatenate([jnp.where(upper, hi, mid), jnp.where(upper, low, 0.0)], axis=0).astype(jnp.bfloat16)
            )
        total = jnp.zeros((16, 256), jnp.float32)
        for k in range(0, LISTED, 2):
            pulls = jnp.concatenate(rights[k : k + 2], axis=1)
            total += jnp.dot(pulls, ratio_ref[slot, k * 128 : (k + 2) * 128, :], preferred_element_type=jnp.float32)
        got = total[:, :128] + total[:, 128:]
        got = got[0:8] + got[8:16]
        got = got[0:4] + got[4:8]
        weight = jnp.where(lane < live_ref[a], weight_ref[pl.ds(a, 1), :], 0.0)
        for d in range(3):
            at = pl.ds(d * BLK_DEV + a, 1)
            force_ref[at, :] = weight * (coords_ref[at, :] * got[3:4] - got[d : d + 1])

    for n in range(depth - 1):
        ahead(0, n)
    for part in range(parts):
        def step(n, _, part=part):
            @pl.when(n + depth - 1 < PART)
            def _():
                load(part, n + depth - 1).start()

            if part + 1 < parts:
                @pl.when(n + depth - 1 >= PART)
                def _():
                    load(part + 1, n + depth - 1 - PART).start()

            block(part, n)
            return 0

        lax.fori_loop(0, PART, step, 0)


SMEM_SPEC = pl.BlockSpec(memory_space=pltpu.SMEM)
VMEM_SPEC = pl.BlockSpec(memory_space=pltpu.VMEM)
HBM_SPEC = pl.BlockSpec(memory_space=pltpu.HBM)


def call_overlap(*arrays):
    f32 = jnp.float32
    vmem, hbm = VMEM_SPEC, HBM_SPEC
    return pl.pallas_call(
        overlap_kernel,
        out_shape=(
            pltpu.HBM((REPLICAS * ROOM, COMP_BLK), f32),
            pltpu.HBM((COMP_BLOCKS, COMP_BLK), f32),
            jax.ShapeDtypeStruct((LISTED, BLK_DEV), jnp.int32),
            jax.ShapeDtypeStruct((REPLICAS * ROOM + COMP_BLOCKS,), jnp.int32),
            jax.ShapeDtypeStruct((1,), jnp.int32),
            jax.ShapeDtypeStruct((BLK_DEV, LISTED, 8, COMP_BLK), f32),
            jax.ShapeDtypeStruct((BLK_DEV, FEATS + 8, ATOM_BLK), f32),
        ),
        in_specs=[hbm] * 9,
        out_specs=(hbm, hbm, SMEM_SPEC, SMEM_SPEC, SMEM_SPEC, vmem, vmem),
        scratch_shapes=[
            pltpu.SMEM((REPLICAS,), jnp.int32),
            pltpu.VMEM((REPLICAS * ROOM + COMP_BLOCKS, COMP_BLK), f32),
            pltpu.SMEM((BLK_DEV,), jnp.int32),
            pltpu.SMEM((LISTED, BLK_DEV), jnp.int32),
            pltpu.SMEM((COMP_BLOCKS,), jnp.int32),
            pltpu.VMEM((3 * BLK_DEV, ATOM_BLK), f32),
            pltpu.VMEM((BLK_DEV, ATOM_BLK), f32),
            pltpu.VMEM((BLK_DEV, ATOM_BLK), f32),
            pltpu.VMEM((3, COMP_BLOCKS * COMP_BLK), f32),
            pltpu.VMEM((COMP_BLOCKS, COMP_BLK), f32),
            pltpu.VMEM((COMP_BLOCKS, COMP_BLK), f32),
            pltpu.SemaphoreType.DMA((9,)),
        ],
        compiler_params=pltpu.CompilerParams(vmem_limit_bytes=20 << 20),
        name="overlap",
    )(*(in_hbm(v) for v in arrays))


def call_ratio(atoms, comps, part):
    f32 = jnp.float32
    return pl.pallas_call(
        functools.partial(ratio_kernel, part * PART),
        out_shape=pltpu.HBM((PART, LISTED * COMP_BLK, 2 * ATOM_BLK), jnp.bfloat16),
        in_specs=[VMEM_SPEC] * 2,
        out_specs=HBM_SPEC,
        scratch_shapes=[
            pltpu.VMEM((2, LISTED * COMP_BLK, 2 * ATOM_BLK), jnp.bfloat16),
            pltpu.SemaphoreType.DMA((2,)),
        ],
        compiler_params=pltpu.CompilerParams(vmem_limit_bytes=12 << 20),
        cost_estimate=pl.CostEstimate(flops=PART << 24, bytes_accessed=PART << 20, transcendentals=PART << 19),
        name="ratio",
    )(atoms, comps)


def call_force(*arrays):
    f32 = jnp.float32
    smem, vmem, hbm = SMEM_SPEC, VMEM_SPEC, HBM_SPEC
    *arrays, ratios = arrays
    return pl.pallas_call(
        force_kernel,
        out_shape=jax.ShapeDtypeStruct((3 * BLK_DEV, ATOM_BLK), f32),
        in_specs=[smem] * 2 + [vmem] * 5 + [hbm] * len(ratios),
        out_specs=vmem,
        scratch_shapes=[
            pltpu.VMEM((DEPTH, LISTED * COMP_BLK, 2 * ATOM_BLK), jnp.bfloat16),
            pltpu.SemaphoreType.DMA((DEPTH,)),
        ],
        compiler_params=pltpu.CompilerParams(vmem_limit_bytes=24 << 20),
        name="force",
    )(*arrays, *(in_hbm(ratio) for ratio in ratios))


def shards(
    coords, atom_var, atom_weight, atoms_live, block_list, owner_map, comp_means, comp_var, comp_weight, target, noise_sigma,
):
    replicas = lax.axis_size("rep")
    domains = lax.axis_size("dom")
    share = COMP_BLOCKS // domains // replicas
    vmem = VMEM_SPEC
    small = pltpu.CompilerParams(vmem_limit_bytes=6 << 20)
    f32 = jnp.float32
    positions = coords.reshape(3 * BLK_DEV, ATOM_BLK)
    listed = block_list.T
    variances = atom_var.reshape(BLK_DEV, ATOM_BLK)
    weights = atom_weight.reshape(BLK_DEV, ATOM_BLK)
    cvar = comp_var.reshape(COMP_BLOCKS, COMP_BLK)
    cweight = comp_weight.reshape(COMP_BLOCKS, COMP_BLK)
    model, over, rows, slots, flag, comps, atoms = call_overlap(
        atoms_live, listed, owner_map, positions, variances, weights, comp_means, cvar, cweight
    )
    crowded = flag[0] > 0
    tie = lax.optimization_barrier
    ratios = [call_ratio(atoms, comps, 0)]
    parts = lax.all_to_all(model.reshape(replicas, ROOM, COMP_BLK), "rep", 0, 0, tiled=True)
    parts, ratios[0] = tie((parts, ratios[0]))
    over_sum = lax.cond(
        crowded,
        lambda v: jnp.sum(lax.all_to_all(v.reshape(replicas, OWNED, COMP_BLK), "rep", 0, 0, tiled=True), axis=0),
        lambda v: jnp.zeros((OWNED, COMP_BLK), f32),
        over,
    )
    over_rep = pl.pallas_call(
        rep_sum_kernel,
        out_shape=jax.ShapeDtypeStruct((OWNED, COMP_BLK), f32),
        in_specs=[SMEM_SPEC, vmem, vmem], out_specs=vmem,
        scratch_shapes=[pltpu.VMEM((ROOM, COMP_BLK), f32), pltpu.VMEM((OWNED + 8, COMP_BLK), f32)],
        compiler_params=small, name="rep_sum",
    )(slots, parts, over_sum)
    over_rep, atoms = tie((over_rep, atoms))
    ratios.append(call_ratio(atoms, comps, 1))
    parts = lax.all_to_all(over_rep.reshape(domains, share, COMP_BLK), "dom", 0, 0, tiled=True)
    parts, ratios[1] = tie((parts, ratios[1]))
    spread, mean = pl.pallas_call(
        adjoint_kernel,
        out_shape=(
            jax.ShapeDtypeStruct((domains, share, COMP_BLK), f32), jax.ShapeDtypeStruct((share, COMP_BLK), f32),
        ),
        in_specs=[vmem] * 3, out_specs=(vmem, vmem), compiler_params=small, name="adjoint",
    )(parts, target.reshape(-1, COMP_BLK), noise_sigma.reshape(-1, COMP_BLK))
    spread, atoms = tie((spread, atoms))
    ratios.append(call_ratio(atoms, comps, 2))
    over_dom = lax.all_to_all(spread, "dom", 0, 0, tiled=True).reshape(domains * share, COMP_BLK)
    over_dom, ratios[2] = tie((over_dom, ratios[2]))
    over_back = lax.cond(
        crowded,
        lambda v, unread: lax.all_to_all(
            jnp.broadcast_to(v[None], (replicas, OWNED, COMP_BLK)), "rep", 0, 0, tiled=True
        ).reshape(unread.shape),
        lambda v, unread: unread,
        over_dom,
        over,
    )
    spread = pl.pallas_call(
        spread_kernel,
        out_shape=pltpu.HBM((replicas, ROOM + share, COMP_BLK), f32),
        in_specs=[SMEM_SPEC, vmem, vmem], out_specs=HBM_SPEC,
        scratch_shapes=[pltpu.VMEM((ROOM + share, COMP_BLK), f32), pltpu.SemaphoreType.DMA((replicas,))],
        compiler_params=small, name="spread",
    )(slots, over_dom, mean)
    spread, atoms = tie((spread, atoms))
    ratios.append(call_ratio(atoms, comps, 3))
    returned = lax.all_to_all(spread, "rep", 0, 0, tiled=True)
    average = returned[:, ROOM:].reshape(-1)
    returned = returned.reshape(-1, COMP_BLK)

    forces = call_force(atoms_live, rows, positions, weights, comps, returned, over_back, ratios)
    return average, forces.reshape(coords.shape)


def solution(mesh):
    return jax.shard_map(
        shards,
        mesh=mesh,
        in_specs=(
            P("rep", None, "dom"), P("dom"), P("dom"), P("dom"), P("dom", None), P(), P(), P(), P(), P("dom"), P("dom"),
        ),
        out_specs=(P("dom"), P("rep", None, "dom")),
        check_vma=False,
    )
```

```python
import functools
import math

import jax
import jax.numpy as jnp
from jax import lax
from jax.experimental import pallas as pl
from jax.experimental.pallas import tpu as pltpu
from jax.sharding import PartitionSpec as P

ATOM_BLK = 128
COMP_BLK = 128
LISTED = 16
BLK_DEV = 32
COMP_BLOCKS = 2048
REPLICAS = 8
FEATS = 48
ROOM = 96
SHARE = 8
OWNED = 256
PART = 8
DEPTH = 8
ROW_STEPS = (64, 80, 96, 112, 128)

ENERGY_UNIT = 2.494
EXP_SCALE = -0.5 / math.log(2.0)
NORM = (2.0 * math.pi) ** -1.5


def split3(v):
    hi = v.astype(jnp.bfloat16).astype(jnp.float32)
    rest = v - hi
    mid = rest.astype(jnp.bfloat16).astype(jnp.float32)
    return hi, mid, rest - mid


def choose(row, parts, shape, other=0.0):
    out = jnp.full(shape, other, jnp.float32)
    for k, part in enumerate(parts):
        out = jnp.where(row == k, part, out)
    return out


def right_side(comp):
    hi, mid, low = split3(comp)
    return jnp.concatenate([hi, hi, hi, mid, mid, low], axis=0).astype(jnp.bfloat16)


def spread_lanes(atoms, column):
    rows = atoms.shape[0]
    return jnp.broadcast_to(atoms[:, column : column + 1], (rows, 128)).reshape(rows // 8, 8, 128)


def pair_terms(left, spread_var, comp_of):
    for k in range(0, LISTED, 2):
        comps = [comp_of(k), comp_of(k + 1)]
        right = jnp.concatenate([right_side(comp) for comp in comps], axis=1)
        scaled = jnp.dot(left, right, preferred_element_type=jnp.float32).reshape(-1, 8, 256)
        for n in range(2):
            r = lax.rsqrt(spread_var + comps[n][5:6].reshape(1, 1, 128))
            q = r * r
            yield k + n, q, (q * r) * jnp.exp2(scaled[:, :, n * 128 : (n + 1) * 128] * q)


def overlap_kernel(
    live_any, list_any, owner_any, coords_any, var_any, weight_any, means_any, cvar_any, cweight_any,
    model_ref, over_ref, rows_ref, slots_ref, flag_ref, comps_ref, atoms_ref,
    counts_ref, sums_ref, live_ref, list_ref, owner_ref, coords_ref, var_ref, weight_ref, means_ref, cvar_ref, cweight_ref, sems,
):
    pairs = (
        (live_any, live_ref), (list_any, list_ref), (owner_any, owner_ref), (coords_any, coords_ref),
        (var_any, var_ref), (weight_any, weight_ref), (means_any, means_ref), (cvar_any, cvar_ref),
        (cweight_any, cweight_ref),
    )
    copies = [pltpu.make_async_copy(src, dst, sems.at[n]) for n, (src, dst) in enumerate(pairs)]
    for copy in copies:
        copy.start()
    shape = (8, 128)
    row = lax.broadcasted_iota(jnp.int32, shape, 0)
    lane = lax.broadcasted_iota(jnp.int32, (1, 128), 1)
    sums_ref[...] = jnp.zeros_like(sums_ref)
    for r in range(REPLICAS):
        counts_ref[r] = r * ROOM

    def unused(n, _):
        slots_ref[n] = OWNED
        return 0

    lax.fori_loop(0, REPLICAS * ROOM, unused, 0, unroll=8)
    for copy in copies:
        copy.wait()

    def rows_of_block(a, rows):
        x, y, z = (coords_ref[pl.ds(d * BLK_DEV + a, 1), :] for d in range(3))
        norm2 = EXP_SCALE * (x * x + y * y + z * z)
        t = -2.0 * EXP_SCALE
        hi, mid, low = split3(choose(row, (t * x, t * y, t * z, EXP_SCALE, norm2), shape))
        weight = jnp.where(lane < live_ref[a], weight_ref[pl.ds(a, 1), :], 0.0)
        extra = choose(row, (var_ref[pl.ds(a, 1), :], weight), shape)
        feats = jnp.concatenate([hi, mid, low, hi, mid, hi, extra], axis=0)
        atoms_ref[a] = feats
        atoms = feats.T[:rows]
        left = atoms[:, :FEATS].astype(jnp.bfloat16)
        spread_var = spread_lanes(atoms, FEATS)
        spread_weight = spread_lanes(atoms, FEATS + 1)

        def comp_of(k):
            b = list_ref[k, a]
            cols = pl.ds(pl.multiple_of(b * 128, 128), 128)
            cx, cy, cz = (means_ref[d : d + 1, cols] for d in range(3))
            norm = cx * cx + cy * cy + cz * cz
            comp = choose(row, (cx, cy, cz, norm, 1.0, cvar_ref[pl.ds(b, 1), :], cweight_ref[pl.ds(b, 1), :]), shape)
            comps_ref[a, k] = comp
            return comp

        for k, _, t in pair_terms(left, spread_var, comp_of):
            total = jnp.sum(jnp.sum(t * spread_weight, axis=0), axis=0, keepdims=True)
            place = owner_ref[list_ref[k, a]]
            rank = (place >> 3) & 7
            owned = ((place >> 6) << 3) + (place & 7)
            place = counts_ref[rank]
            counts_ref[rank] = place + 1
            fits = place < rank * ROOM + ROOM
            target = jnp.where(fits, place, rank * OWNED + owned + REPLICAS * ROOM)
            slots_ref[target] = owned
            rows_ref[k, a] = target + jnp.where(fits, rank * SHARE, REPLICAS * SHARE)
            sums_ref[pl.ds(target, 1), :] += NORM * total * comps_ref[a, k, 6:7, :]

    def block(a, _):
        step = jnp.clip((live_ref[a] - ROW_STEPS[0] + 15) // 16, 0, len(ROW_STEPS) - 1)
        lax.switch(step, [functools.partial(rows_of_block, a, rows) for rows in ROW_STEPS])
        return 0

    lax.fori_loop(0, BLK_DEV, block, 0)
    crowded = jnp.int32(0)
    for r in range(REPLICAS):
        crowded = jnp.where(counts_ref[r] > (r + 1) * ROOM, 1, crowded)
    flag_ref[0] = crowded
    copies = [
        pltpu.make_async_copy(sums_ref.at[pl.ds(0, REPLICAS * ROOM)], model_ref, sems.at[0]),
        pltpu.make_async_copy(sums_ref.at[pl.ds(REPLICAS * ROOM, COMP_BLOCKS)], over_ref, sems.at[1]),
    ]
    for copy in copies:
        copy.start()
    for copy in copies:
        copy.wait()


def ratio_kernel(first, atoms_ref, comps_ref, ratio_any, ratio_buf, sems):
    blocks = ratio_any.shape[0]

    def store(a):
        return pltpu.make_async_copy(ratio_buf.at[a & 1], ratio_any.at[a], sems.at[a & 1])

    def block(a, _):
        @pl.when(a >= 2)
        def _():
            store(a - 2).wait()

        slot = a & 1
        row = lax.broadcasted_iota(jnp.int32, (8, 128), 0)
        own = jnp.where(row == 5, 1.0, 0.0)
        var = jnp.where(row == 4, jnp.broadcast_to(atoms_ref[first + a, FEATS : FEATS + 1, :], (8, 128)), 0.0)
        hi, mid, low = split3(var)
        sums = jnp.concatenate([hi + own, mid, low, own, jnp.zeros_like(own), own], axis=0)
        right = jnp.concatenate([atoms_ref[first + a, :FEATS, :], sums], axis=1).astype(jnp.bfloat16)
        for k in range(LISTED):
            left = right_side(comps_ref[first + a, k]).T
            both = jnp.dot(left, right, preferred_element_type=jnp.float32).reshape(16, 8, 256)
            r = lax.rsqrt(both[:, :, 128:])
            q = r * r
            ratio = ((q * q) * (r * jnp.exp2(both[:, :, :128] * q))).reshape(128, 128)
            hi = ratio.astype(jnp.bfloat16)
            rows = slice(k * 128, (k + 1) * 128)
            ratio_buf[slot, rows, :128] = hi
            ratio_buf[slot, rows, 128:] = (ratio - hi.astype(jnp.float32)).astype(jnp.bfloat16)
        store(a).start()
        return 0

    lax.fori_loop(0, blocks, block, 0)
    store(blocks - 2).wait()
    store(blocks - 1).wait()


def in_hbm(array):
    return pltpu.with_memory_space_constraint(array, pltpu.HBM)


def rep_sum_kernel(flag_ref, slots_ref, parts_ref, over_any, out_ref, sum_ref, dense_ref, over_ref, sem):
    sum_ref[...] = jnp.sum(parts_ref[...], axis=0)
    dense_ref[...] = jnp.zeros_like(dense_ref)

    @pl.when(flag_ref[0] > 0)
    def _():
        copy = pltpu.make_async_copy(over_any, over_ref, sem)
        copy.start()
        copy.wait()
        dense_ref[:OWNED] = jnp.sum(over_ref[...].reshape(REPLICAS, OWNED, COMP_BLK), axis=0)

    first = lax.axis_index("rep") * ROOM
    for n in range(ROOM):
        dense_ref[pl.ds(slots_ref[first + n], 1), :] += sum_ref[n : n + 1, :]
    out_ref[...] = dense_ref[:OWNED]


def adjoint_kernel(parts_ref, target_ref, sigma_ref, spread_ref, mean_ref):
    share = mean_ref.shape[0]
    mean = jnp.sum(parts_ref[...], axis=0) / REPLICAS
    first = pl.ds(pl.multiple_of(lax.axis_index("rep") * share, share), share)
    sigma = sigma_ref[first, :]
    misfit = mean - target_ref[first, :]
    adjoint = misfit / (sigma * sigma + 0.5 * misfit * misfit) / REPLICAS
    mean_ref[...] = mean
    spread_ref[...] = jnp.broadcast_to(adjoint[None], spread_ref.shape)


def spread_kernel(slots_ref, adjoint_ref, mean_ref, out_ref, rows_ref, sems):
    first = lax.axis_index("rep") * ROOM
    for n in range(ROOM):
        rows_ref[n : n + 1, :] = adjoint_ref[pl.ds(jnp.minimum(slots_ref[first + n], OWNED - 1), 1), :]
    rows_ref[ROOM:] = mean_ref[...]
    copies = [pltpu.make_async_copy(rows_ref, out_ref.at[r], sems.at[r]) for r in range(REPLICAS)]
    for copy in copies:
        copy.start()
    for copy in copies:
        copy.wait()


def force_kernel(
    live_ref, rows_ref, coords_ref, weight_ref, comps_ref, adjoint_ref, over_ref, *refs,
):
    parts = BLK_DEV // PART
    ratio_any, (force_ref, average_ref, ratio_ref, ratio_sems) = refs[:parts], refs[parts:]
    depth = ratio_ref.shape[0]
    for r in range(REPLICAS):
        first = r * (ROOM + SHARE) + ROOM
        average_ref[r * SHARE : (r + 1) * SHARE] = adjoint_ref[first : first + SHARE]
    shape = (8, 128)
    row = lax.broadcasted_iota(jnp.int32, shape, 0)
    upper = row < 4
    lane = lax.broadcasted_iota(jnp.int32, (1, 128), 1)

    def load(part, n):
        slot = (part * PART + n) % depth
        return pltpu.make_async_copy(ratio_any[part].at[n], ratio_ref.at[slot], ratio_sems.at[slot])

    def ahead(part, n):
        if n >= PART:
            part, n = part + 1, n - PART
        if part < parts:
            load(part, n).start()

    def block(part, n):
        a = part * PART + n
        load(part, n).wait()
        slot = a % depth
        rights = []
        for k in range(LISTED):
            target = rows_ref[k, a]
            beyond = target - REPLICAS * (ROOM + SHARE)
            near = adjoint_ref[pl.ds(jnp.minimum(target, REPLICAS * (ROOM + SHARE) - 1), 1), :]
            far = over_ref[pl.ds(jnp.maximum(beyond, 0), 1), :]
            cx, cy, cz, cw = (comps_ref[a, k, d : d + 1, :] for d in (0, 1, 2, 6))
            pull = (ENERGY_UNIT * NORM) * jnp.where(beyond < 0, near, far) * cw
            hi, mid, low = split3(pull * choose(row & 3, (cx, cy, cz, 1.0), shape))
            rights.append(
                jnp.concatenate([jnp.where(upper, hi, mid), jnp.where(upper, low, 0.0)], axis=0).astype(jnp.bfloat16)
            )
        total = jnp.zeros((16, 256), jnp.float32)
        for k in range(0, LISTED, 2):
            pulls = jnp.concatenate(rights[k : k + 2], axis=1)
            total += jnp.dot(pulls, ratio_ref[slot, k * 128 : (k + 2) * 128, :], preferred_element_type=jnp.float32)
        got = total[:, :128] + total[:, 128:]
        got = got[0:8] + got[8:16]
        got = got[0:4] + got[4:8]
        weight = jnp.where(lane < live_ref[a], weight_ref[pl.ds(a, 1), :], 0.0)
        for d in range(3):
            at = pl.ds(d * BLK_DEV + a, 1)
            force_ref[at, :] = weight * (coords_ref[at, :] * got[3:4] - got[d : d + 1])

    for n in range(depth - 1):
        ahead(0, n)
    for part in range(parts):
        def step(n, _, part=part):
            @pl.when(n + depth - 1 < PART)
            def _():
                load(part, n + depth - 1).start()

            if part + 1 < parts:
                @pl.when(n + depth - 1 >= PART)
                def _():
                    load(part + 1, n + depth - 1 - PART).start()

            block(part, n)
            return 0

        lax.fori_loop(0, PART, step, 0)


SMEM_SPEC = pl.BlockSpec(memory_space=pltpu.SMEM)
VMEM_SPEC = pl.BlockSpec(memory_space=pltpu.VMEM)
HBM_SPEC = pl.BlockSpec(memory_space=pltpu.HBM)


def call_overlap(*arrays):
    f32 = jnp.float32
    vmem, hbm = VMEM_SPEC, HBM_SPEC
    return pl.pallas_call(
        overlap_kernel,
        out_shape=(
            pltpu.HBM((REPLICAS * ROOM, COMP_BLK), f32),
            pltpu.HBM((COMP_BLOCKS, COMP_BLK), f32),
            jax.ShapeDtypeStruct((LISTED, BLK_DEV), jnp.int32),
            jax.ShapeDtypeStruct((REPLICAS * ROOM + COMP_BLOCKS,), jnp.int32),
            jax.ShapeDtypeStruct((1,), jnp.int32),
            jax.ShapeDtypeStruct((BLK_DEV, LISTED, 8, COMP_BLK), f32),
            jax.ShapeDtypeStruct((BLK_DEV, FEATS + 8, ATOM_BLK), f32),
        ),
        in_specs=[hbm] * 9,
        out_specs=(hbm, hbm, SMEM_SPEC, SMEM_SPEC, SMEM_SPEC, vmem, vmem),
        scratch_shapes=[
            pltpu.SMEM((REPLICAS,), jnp.int32),
            pltpu.VMEM((REPLICAS * ROOM + COMP_BLOCKS, COMP_BLK), f32),
            pltpu.SMEM((BLK_DEV,), jnp.int32),
            pltpu.SMEM((LISTED, BLK_DEV), jnp.int32),
            pltpu.SMEM((COMP_BLOCKS,), jnp.int32),
            pltpu.VMEM((3 * BLK_DEV, ATOM_BLK), f32),
            pltpu.VMEM((BLK_DEV, ATOM_BLK), f32),
            pltpu.VMEM((BLK_DEV, ATOM_BLK), f32),
            pltpu.VMEM((3, COMP_BLOCKS * COMP_BLK), f32),
            pltpu.VMEM((COMP_BLOCKS, COMP_BLK), f32),
            pltpu.VMEM((COMP_BLOCKS, COMP_BLK), f32),
            pltpu.SemaphoreType.DMA((9,)),
        ],
        compiler_params=pltpu.CompilerParams(vmem_limit_bytes=20 << 20),
        name="overlap",
    )(*(in_hbm(v) for v in arrays))


def call_ratio(atoms, comps, part):
    f32 = jnp.float32
    return pl.pallas_call(
        functools.partial(ratio_kernel, part * PART),
        out_shape=pltpu.HBM((PART, LISTED * COMP_BLK, 2 * ATOM_BLK), jnp.bfloat16),
        in_specs=[VMEM_SPEC] * 2,
        out_specs=HBM_SPEC,
        scratch_shapes=[
            pltpu.VMEM((2, LISTED * COMP_BLK, 2 * ATOM_BLK), jnp.bfloat16),
            pltpu.SemaphoreType.DMA((2,)),
        ],
        compiler_params=pltpu.CompilerParams(vmem_limit_bytes=12 << 20),
        cost_estimate=pl.CostEstimate(flops=PART << 24, bytes_accessed=PART << 20, transcendentals=PART << 19),
        name="ratio",
    )(atoms, comps)


def call_force(*arrays):
    f32 = jnp.float32
    smem, vmem, hbm = SMEM_SPEC, VMEM_SPEC, HBM_SPEC
    *arrays, ratios = arrays
    return pl.pallas_call(
        force_kernel,
        out_shape=(
            jax.ShapeDtypeStruct((3 * BLK_DEV, ATOM_BLK), f32),
            jax.ShapeDtypeStruct((REPLICAS * SHARE, COMP_BLK), f32),
        ),
        in_specs=[smem] * 2 + [vmem] * 5 + [hbm] * len(ratios),
        out_specs=(vmem, vmem),
        scratch_shapes=[
            pltpu.VMEM((DEPTH, LISTED * COMP_BLK, 2 * ATOM_BLK), jnp.bfloat16),
            pltpu.SemaphoreType.DMA((DEPTH,)),
        ],
        compiler_params=pltpu.CompilerParams(vmem_limit_bytes=24 << 20),
        name="force",
    )(*arrays, *(in_hbm(ratio) for ratio in ratios))


def shards(
    coords, atom_var, atom_weight, atoms_live, block_list, owner_map, comp_means, comp_var, comp_weight, target, noise_sigma,
):
    replicas = lax.axis_size("rep")
    domains = lax.axis_size("dom")
    share = COMP_BLOCKS // domains // replicas
    vmem = VMEM_SPEC
    small = pltpu.CompilerParams(vmem_limit_bytes=6 << 20)
    f32 = jnp.float32
    positions = coords.reshape(3 * BLK_DEV, ATOM_BLK)
    listed = block_list.T
    variances = atom_var.reshape(BLK_DEV, ATOM_BLK)
    weights = atom_weight.reshape(BLK_DEV, ATOM_BLK)
    cvar = comp_var.reshape(COMP_BLOCKS, COMP_BLK)
    cweight = comp_weight.reshape(COMP_BLOCKS, COMP_BLK)
    model, over, rows, slots, flag, comps, atoms = call_overlap(
        atoms_live, listed, owner_map, positions, variances, weights, comp_means, cvar, cweight
    )
    crowded = flag[0] > 0
    tie = lax.optimization_barrier
    ratios = [call_ratio(atoms, comps, 0)]
    parts = lax.all_to_all(model.reshape(replicas, ROOM, COMP_BLK), "rep", 0, 0, tiled=True)
    parts, ratios[0] = tie((parts, ratios[0]))
    over_sum = lax.cond(
        crowded,
        lambda v: lax.all_to_all(v.reshape(replicas, OWNED, COMP_BLK), "rep", 0, 0, tiled=True).reshape(v.shape),
        lambda v: v,
        over,
    )
    over_rep = pl.pallas_call(
        rep_sum_kernel,
        out_shape=jax.ShapeDtypeStruct((OWNED, COMP_BLK), f32),
        in_specs=[SMEM_SPEC, SMEM_SPEC, vmem, HBM_SPEC], out_specs=vmem,
        scratch_shapes=[
            pltpu.VMEM((ROOM, COMP_BLK), f32),
            pltpu.VMEM((OWNED + 8, COMP_BLK), f32),
            pltpu.VMEM((COMP_BLOCKS, COMP_BLK), f32),
            pltpu.SemaphoreType.DMA,
        ],
        compiler_params=small, name="rep_sum",
    )(flag, slots, parts, in_hbm(over_sum))
    over_rep, atoms = tie((over_rep, atoms))
    ratios.append(call_ratio(atoms, comps, 1))
    parts = lax.all_to_all(over_rep.reshape(domains, share, COMP_BLK), "dom", 0, 0, tiled=True)
    parts, ratios[1] = tie((parts, ratios[1]))
    spread, mean = pl.pallas_call(
        adjoint_kernel,
        out_shape=(
            jax.ShapeDtypeStruct((domains, share, COMP_BLK), f32), jax.ShapeDtypeStruct((share, COMP_BLK), f32),
        ),
        in_specs=[vmem] * 3, out_specs=(vmem, vmem), compiler_params=small, name="adjoint",
    )(parts, target.reshape(-1, COMP_BLK), noise_sigma.reshape(-1, COMP_BLK))
    spread, atoms = tie((spread, atoms))
    ratios.append(call_ratio(atoms, comps, 2))
    over_dom = lax.all_to_all(spread, "dom", 0, 0, tiled=True).reshape(domains * share, COMP_BLK)
    over_dom, ratios[2] = tie((over_dom, ratios[2]))
    over_back = lax.cond(
        crowded,
        lambda v, unread: lax.all_to_all(
            jnp.broadcast_to(v[None], (replicas, OWNED, COMP_BLK)), "rep", 0, 0, tiled=True
        ).reshape(unread.shape),
        lambda v, unread: unread,
        over_dom,
        over,
    )
    spread = pl.pallas_call(
        spread_kernel,
        out_shape=pltpu.HBM((replicas, ROOM + share, COMP_BLK), f32),
        in_specs=[SMEM_SPEC, vmem, vmem], out_specs=HBM_SPEC,
        scratch_shapes=[pltpu.VMEM((ROOM + share, COMP_BLK), f32), pltpu.SemaphoreType.DMA((replicas,))],
        compiler_params=small, name="spread",
    )(slots, over_dom, mean)
    spread, atoms = tie((spread, atoms))
    ratios.append(call_ratio(atoms, comps, 3))
    returned = lax.all_to_all(spread, "rep", 0, 0, tiled=True)
    returned = returned.reshape(-1, COMP_BLK)

    forces, average = call_force(atoms_live, rows, positions, weights, comps, returned, over_back, ratios)
    return average.reshape(-1), forces.reshape(coords.shape)


def solution(mesh):
    return jax.shard_map(
        shards,
        mesh=mesh,
        in_specs=(
            P("rep", None, "dom"), P("dom"), P("dom"), P("dom"), P("dom", None), P(), P(), P(), P(), P("dom"), P("dom"),
        ),
        out_specs=(P("dom"), P("rep", None, "dom")),
        check_vma=False,
    )
```

```python
import functools
import math

import jax
import jax.numpy as jnp
from jax import lax
from jax.experimental import pallas as pl
from jax.experimental.pallas import tpu as pltpu
from jax.sharding import PartitionSpec as P

ATOM_BLK = 128
COMP_BLK = 128
LISTED = 16
BLK_DEV = 32
COMP_BLOCKS = 2048
REPLICAS = 8
FEATS = 48
ROOM = 96
SHARE = 8
OWNED = 256
PART = 8
DEPTH = 8
ROW_STEPS = (64, 80, 96, 112, 128)

ENERGY_UNIT = 2.494
EXP_SCALE = -0.5 / math.log(2.0)
NORM = (2.0 * math.pi) ** -1.5


def split3(v):
    hi = v.astype(jnp.bfloat16).astype(jnp.float32)
    rest = v - hi
    mid = rest.astype(jnp.bfloat16).astype(jnp.float32)
    return hi, mid, rest - mid


def choose(row, parts, shape, other=0.0):
    out = jnp.full(shape, other, jnp.float32)
    for k, part in enumerate(parts):
        out = jnp.where(row == k, part, out)
    return out


def right_side(comp):
    hi, mid, low = split3(comp)
    return jnp.concatenate([hi, hi, hi, mid, mid, low], axis=0).astype(jnp.bfloat16)


def spread_lanes(atoms, column):
    rows = atoms.shape[0]
    return jnp.broadcast_to(atoms[:, column : column + 1], (rows, 128)).reshape(rows // 8, 8, 128)


def pair_terms(left, spread_var, comp_of):
    for k in range(0, LISTED, 2):
        comps = [comp_of(k), comp_of(k + 1)]
        right = jnp.concatenate([right_side(comp) for comp in comps], axis=1)
        scaled = jnp.dot(left, right, preferred_element_type=jnp.float32).reshape(-1, 8, 256)
        for n in range(2):
            r = lax.rsqrt(spread_var + comps[n][5:6].reshape(1, 1, 128))
            q = r * r
            yield k + n, q, (q * r) * jnp.exp2(scaled[:, :, n * 128 : (n + 1) * 128] * q)


def overlap_kernel(
    live_any, list_any, owner_any, coords_any, var_any, weight_any, means_any, cvar_any, cweight_any,
    model_ref, over_ref, rows_ref, slots_ref, flag_ref, comps_ref, atoms_ref,
    counts_ref, sums_ref, live_ref, list_ref, owner_ref, coords_ref, var_ref, weight_ref, means_ref, cvar_ref, cweight_ref, sems,
):
    pairs = (
        (live_any, live_ref), (list_any, list_ref), (owner_any, owner_ref), (coords_any, coords_ref),
        (var_any, var_ref), (weight_any, weight_ref), (means_any, means_ref), (cvar_any, cvar_ref),
        (cweight_any, cweight_ref),
    )
    copies = [pltpu.make_async_copy(src, dst, sems.at[n]) for n, (src, dst) in enumerate(pairs)]
    for copy in copies:
        copy.start()
    shape = (8, 128)
    row = lax.broadcasted_iota(jnp.int32, shape, 0)
    lane = lax.broadcasted_iota(jnp.int32, (1, 128), 1)
    sums_ref[...] = jnp.zeros_like(sums_ref)
    for r in range(REPLICAS):
        counts_ref[r] = r * ROOM

    def unused(n, _):
        slots_ref[n] = OWNED
        return 0

    lax.fori_loop(0, REPLICAS * ROOM, unused, 0, unroll=8)
    for copy in copies:
        copy.wait()

    def rows_of_block(a, rows):
        x, y, z = (coords_ref[pl.ds(d * BLK_DEV + a, 1), :] for d in range(3))
        norm2 = EXP_SCALE * (x * x + y * y + z * z)
        t = -2.0 * EXP_SCALE
        hi, mid, low = split3(choose(row, (t * x, t * y, t * z, EXP_SCALE, norm2), shape))
        weight = jnp.where(lane < live_ref[a], weight_ref[pl.ds(a, 1), :], 0.0)
        extra = choose(row, (var_ref[pl.ds(a, 1), :], weight), shape)
        feats = jnp.concatenate([hi, mid, low, hi, mid, hi, extra], axis=0)
        atoms_ref[a] = feats
        atoms = feats.T[:rows]
        left = atoms[:, :FEATS].astype(jnp.bfloat16)
        spread_var = spread_lanes(atoms, FEATS)
        spread_weight = spread_lanes(atoms, FEATS + 1)

        def comp_of(k):
            b = list_ref[k, a]
            cols = pl.ds(pl.multiple_of(b * 128, 128), 128)
            cx, cy, cz = (means_ref[d : d + 1, cols] for d in range(3))
            norm = cx * cx + cy * cy + cz * cz
            comp = choose(row, (cx, cy, cz, norm, 1.0, cvar_ref[pl.ds(b, 1), :], cweight_ref[pl.ds(b, 1), :]), shape)
            comps_ref[a, k] = comp
            return comp

        for k, _, t in pair_terms(left, spread_var, comp_of):
            total = jnp.sum(jnp.sum(t * spread_weight, axis=0), axis=0, keepdims=True)
            place = owner_ref[list_ref[k, a]]
            rank = (place >> 3) & 7
            owned = ((place >> 6) << 3) + (place & 7)
            place = counts_ref[rank]
            counts_ref[rank] = place + 1
            fits = place < rank * ROOM + ROOM
            target = jnp.where(fits, place, rank * OWNED + owned + REPLICAS * ROOM)
            slots_ref[target] = owned
            rows_ref[k, a] = target + jnp.where(fits, rank * SHARE, REPLICAS * SHARE)
            sums_ref[pl.ds(target, 1), :] += NORM * total * comps_ref[a, k, 6:7, :]

    def block(a, _):
        step = jnp.clip((live_ref[a] - ROW_STEPS[0] + 15) // 16, 0, len(ROW_STEPS) - 1)
        lax.switch(step, [functools.partial(rows_of_block, a, rows) for rows in ROW_STEPS])
        return 0

    lax.fori_loop(0, BLK_DEV, block, 0)
    crowded = jnp.int32(0)
    for r in range(REPLICAS):
        crowded = jnp.where(counts_ref[r] > (r + 1) * ROOM, 1, crowded)
    flag_ref[0] = crowded
    copies = [
        pltpu.make_async_copy(sums_ref.at[pl.ds(0, REPLICAS * ROOM)], model_ref, sems.at[0]),
        pltpu.make_async_copy(sums_ref.at[pl.ds(REPLICAS * ROOM, COMP_BLOCKS)], over_ref, sems.at[1]),
    ]
    for copy in copies:
        copy.start()
    for copy in copies:
        copy.wait()


def ratio_kernel(first, atoms_ref, comps_ref, ratio_any, ratio_buf, sems):
    blocks = ratio_any.shape[0]

    def store(a):
        return pltpu.make_async_copy(ratio_buf.at[a & 1], ratio_any.at[a], sems.at[a & 1])

    def block(a, _):
        @pl.when(a >= 2)
        def _():
            store(a - 2).wait()

        slot = a & 1
        row = lax.broadcasted_iota(jnp.int32, (8, 128), 0)
        own = jnp.where(row == 5, 1.0, 0.0)
        var = jnp.where(row == 4, jnp.broadcast_to(atoms_ref[first + a, FEATS : FEATS + 1, :], (8, 128)), 0.0)
        hi, mid, low = split3(var)
        sums = jnp.concatenate([hi + own, mid, low, own, jnp.zeros_like(own), own], axis=0)
        right = jnp.concatenate([atoms_ref[first + a, :FEATS, :], sums], axis=1).astype(jnp.bfloat16)
        for k in range(LISTED):
            left = right_side(comps_ref[first + a, k]).T
            both = jnp.dot(left, right, preferred_element_type=jnp.float32).reshape(16, 8, 256)
            r = lax.rsqrt(both[:, :, 128:])
            q = r * r
            ratio = ((q * q) * (r * jnp.exp2(both[:, :, :128] * q))).reshape(128, 128)
            hi = ratio.astype(jnp.bfloat16)
            rows = slice(k * 128, (k + 1) * 128)
            ratio_buf[slot, rows, :128] = hi
            ratio_buf[slot, rows, 128:] = (ratio - hi.astype(jnp.float32)).astype(jnp.bfloat16)
        store(a).start()
        return 0

    lax.fori_loop(0, blocks, block, 0)
    store(blocks - 2).wait()
    store(blocks - 1).wait()


def in_hbm(array):
    return pltpu.with_memory_space_constraint(array, pltpu.HBM)


def rep_sum_kernel(slots_ref, parts_ref, over_ref, out_ref, sum_ref, dense_ref):
    sum_ref[...] = jnp.sum(parts_ref[...], axis=0)
    dense_ref[:OWNED] = over_ref[...]
    first = lax.axis_index("rep") * ROOM
    for n in range(ROOM):
        dense_ref[pl.ds(slots_ref[first + n], 1), :] += sum_ref[n : n + 1, :]
    out_ref[...] = dense_ref[:OWNED]


def adjoint_kernel(parts_ref, target_ref, sigma_ref, spread_ref, mean_ref):
    share = mean_ref.shape[0]
    mean = jnp.sum(parts_ref[...], axis=0) / REPLICAS
    first = pl.ds(pl.multiple_of(lax.axis_index("rep") * share, share), share)
    sigma = sigma_ref[first, :]
    misfit = mean - target_ref[first, :]
    adjoint = misfit / (sigma * sigma + 0.5 * misfit * misfit) / REPLICAS
    mean_ref[...] = mean
    spread_ref[...] = jnp.broadcast_to(adjoint[None], spread_ref.shape)


def spread_kernel(slots_ref, adjoint_ref, mean_ref, out_ref, rows_ref, sems):
    first = lax.axis_index("rep") * ROOM
    for n in range(ROOM):
        rows_ref[n : n + 1, :] = adjoint_ref[pl.ds(jnp.minimum(slots_ref[first + n], OWNED - 1), 1), :]
    rows_ref[ROOM:] = mean_ref[...]
    copies = [pltpu.make_async_copy(rows_ref, out_ref.at[r], sems.at[r]) for r in range(REPLICAS)]
    for copy in copies:
        copy.start()
    for copy in copies:
        copy.wait()


def force_kernel(
    live_ref, rows_ref, coords_ref, weight_ref, comps_ref, adjoint_ref, over_ref, *refs,
):
    parts = BLK_DEV // PART
    ratio_any, (force_ref, average_ref, ratio_ref, ratio_sems) = refs[:parts], refs[parts:]
    depth = ratio_ref.shape[0]
    for r in range(REPLICAS):
        first = r * (ROOM + SHARE) + ROOM
        average_ref[r * SHARE : (r + 1) * SHARE] = adjoint_ref[first : first + SHARE]
    shape = (8, 128)
    row = lax.broadcasted_iota(jnp.int32, shape, 0)
    upper = row < 4
    lane = lax.broadcasted_iota(jnp.int32, (1, 128), 1)

    def load(part, n):
        slot = (part * PART + n) % depth
        return pltpu.make_async_copy(ratio_any[part].at[n], ratio_ref.at[slot], ratio_sems.at[slot])

    def ahead(part, n):
        if n >= PART:
            part, n = part + 1, n - PART
        if part < parts:
            load(part, n).start()

    def block(part, n):
        a = part * PART + n
        load(part, n).wait()
        slot = a % depth
        rights = []
        for k in range(LISTED):
            target = rows_ref[k, a]
            beyond = target - REPLICAS * (ROOM + SHARE)
            near = adjoint_ref[pl.ds(jnp.minimum(target, REPLICAS * (ROOM + SHARE) - 1), 1), :]
            far = over_ref[pl.ds(jnp.maximum(beyond, 0), 1), :]
            cx, cy, cz, cw = (comps_ref[a, k, d : d + 1, :] for d in (0, 1, 2, 6))
            pull = (ENERGY_UNIT * NORM) * jnp.where(beyond < 0, near, far) * cw
            hi, mid, low = split3(pull * choose(row & 3, (cx, cy, cz, 1.0), shape))
            rights.append(
                jnp.concatenate([jnp.where(upper, hi, mid), jnp.where(upper, low, 0.0)], axis=0).astype(jnp.bfloat16)
            )
        total = jnp.zeros((16, 256), jnp.float32)
        for k in range(0, LISTED, 2):
            pulls = jnp.concatenate(rights[k : k + 2], axis=1)
            total += jnp.dot(pulls, ratio_ref[slot, k * 128 : (k + 2) * 128, :], preferred_element_type=jnp.float32)
        got = total[:, :128] + total[:, 128:]
        got = got[0:8] + got[8:16]
        got = got[0:4] + got[4:8]
        weight = jnp.where(lane < live_ref[a], weight_ref[pl.ds(a, 1), :], 0.0)
        for d in range(3):
            at = pl.ds(d * BLK_DEV + a, 1)
            force_ref[at, :] = weight * (coords_ref[at, :] * got[3:4] - got[d : d + 1])

    for n in range(depth - 1):
        ahead(0, n)
    for part in range(parts):
        def step(n, _, part=part):
            @pl.when(n + depth - 1 < PART)
            def _():
                load(part, n + depth - 1).start()

            if part + 1 < parts:
                @pl.when(n + depth - 1 >= PART)
                def _():
                    load(part + 1, n + depth - 1 - PART).start()

            block(part, n)
            return 0

        lax.fori_loop(0, PART, step, 0)


SMEM_SPEC = pl.BlockSpec(memory_space=pltpu.SMEM)
VMEM_SPEC = pl.BlockSpec(memory_space=pltpu.VMEM)
HBM_SPEC = pl.BlockSpec(memory_space=pltpu.HBM)


def call_overlap(*arrays):
    f32 = jnp.float32
    vmem, hbm = VMEM_SPEC, HBM_SPEC
    return pl.pallas_call(
        overlap_kernel,
        out_shape=(
            pltpu.HBM((REPLICAS * ROOM, COMP_BLK), f32),
            pltpu.HBM((COMP_BLOCKS, COMP_BLK), f32),
            jax.ShapeDtypeStruct((LISTED, BLK_DEV), jnp.int32),
            jax.ShapeDtypeStruct((REPLICAS * ROOM + COMP_BLOCKS,), jnp.int32),
            jax.ShapeDtypeStruct((1,), jnp.int32),
            jax.ShapeDtypeStruct((BLK_DEV, LISTED, 8, COMP_BLK), f32),
            jax.ShapeDtypeStruct((BLK_DEV, FEATS + 8, ATOM_BLK), f32),
        ),
        in_specs=[hbm] * 9,
        out_specs=(hbm, hbm, SMEM_SPEC, SMEM_SPEC, SMEM_SPEC, vmem, vmem),
        scratch_shapes=[
            pltpu.SMEM((REPLICAS,), jnp.int32),
            pltpu.VMEM((REPLICAS * ROOM + COMP_BLOCKS, COMP_BLK), f32),
            pltpu.SMEM((BLK_DEV,), jnp.int32),
            pltpu.SMEM((LISTED, BLK_DEV), jnp.int32),
            pltpu.SMEM((COMP_BLOCKS,), jnp.int32),
            pltpu.VMEM((3 * BLK_DEV, ATOM_BLK), f32),
            pltpu.VMEM((BLK_DEV, ATOM_BLK), f32),
            pltpu.VMEM((BLK_DEV, ATOM_BLK), f32),
            pltpu.VMEM((3, COMP_BLOCKS * COMP_BLK), f32),
            pltpu.VMEM((COMP_BLOCKS, COMP_BLK), f32),
            pltpu.VMEM((COMP_BLOCKS, COMP_BLK), f32),
            pltpu.SemaphoreType.DMA((9,)),
        ],
        compiler_params=pltpu.CompilerParams(vmem_limit_bytes=20 << 20),
        name="overlap",
    )(*(in_hbm(v) for v in arrays))


def call_ratio(atoms, comps, part):
    f32 = jnp.float32
    return pl.pallas_call(
        functools.partial(ratio_kernel, part * PART),
        out_shape=pltpu.HBM((PART, LISTED * COMP_BLK, 2 * ATOM_BLK), jnp.bfloat16),
        in_specs=[VMEM_SPEC] * 2,
        out_specs=HBM_SPEC,
        scratch_shapes=[
            pltpu.VMEM((2, LISTED * COMP_BLK, 2 * ATOM_BLK), jnp.bfloat16),
            pltpu.SemaphoreType.DMA((2,)),
        ],
        compiler_params=pltpu.CompilerParams(vmem_limit_bytes=12 << 20),
        cost_estimate=pl.CostEstimate(flops=PART << 24, bytes_accessed=PART << 20, transcendentals=PART << 19),
        name="ratio",
    )(atoms, comps)


def call_force(*arrays):
    f32 = jnp.float32
    smem, vmem, hbm = SMEM_SPEC, VMEM_SPEC, HBM_SPEC
    *arrays, ratios = arrays
    return pl.pallas_call(
        force_kernel,
        out_shape=(
            jax.ShapeDtypeStruct((3 * BLK_DEV, ATOM_BLK), f32),
            jax.ShapeDtypeStruct((REPLICAS * SHARE, COMP_BLK), f32),
        ),
        in_specs=[smem] * 2 + [vmem] * 5 + [hbm] * len(ratios),
        out_specs=(vmem, vmem),
        scratch_shapes=[
            pltpu.VMEM((DEPTH, LISTED * COMP_BLK, 2 * ATOM_BLK), jnp.bfloat16),
            pltpu.SemaphoreType.DMA((DEPTH,)),
        ],
        compiler_params=pltpu.CompilerParams(vmem_limit_bytes=24 << 20),
        name="force",
    )(*arrays, *(in_hbm(ratio) for ratio in ratios))


def shards(
    coords, atom_var, atom_weight, atoms_live, block_list, owner_map, comp_means, comp_var, comp_weight, target, noise_sigma,
):
    replicas = lax.axis_size("rep")
    domains = lax.axis_size("dom")
    share = COMP_BLOCKS // domains // replicas
    vmem = VMEM_SPEC
    small = pltpu.CompilerParams(vmem_limit_bytes=6 << 20)
    f32 = jnp.float32
    positions = coords.reshape(3 * BLK_DEV, ATOM_BLK)
    listed = block_list.T
    variances = atom_var.reshape(BLK_DEV, ATOM_BLK)
    weights = atom_weight.reshape(BLK_DEV, ATOM_BLK)
    cvar = comp_var.reshape(COMP_BLOCKS, COMP_BLK)
    cweight = comp_weight.reshape(COMP_BLOCKS, COMP_BLK)
    model, over, rows, slots, flag, comps, atoms = call_overlap(
        atoms_live, listed, owner_map, positions, variances, weights, comp_means, cvar, cweight
    )
    crowded = flag[0] > 0
    tie = lax.optimization_barrier
    ratios = [call_ratio(atoms, comps, 0)]
    parts = lax.all_to_all(model.reshape(replicas, ROOM, COMP_BLK), "rep", 0, 0, tiled=True)
    parts, ratios[0] = tie((parts, ratios[0]))
    over_sum = lax.cond(
        crowded,
        lambda v: jnp.sum(lax.all_to_all(v.reshape(replicas, OWNED, COMP_BLK), "rep", 0, 0, tiled=True), axis=0),
        lambda v: jnp.zeros((OWNED, COMP_BLK), f32),
        over,
    )
    over_rep = pl.pallas_call(
        rep_sum_kernel,
        out_shape=jax.ShapeDtypeStruct((OWNED, COMP_BLK), f32),
        in_specs=[SMEM_SPEC, vmem, vmem], out_specs=vmem,
        scratch_shapes=[pltpu.VMEM((ROOM, COMP_BLK), f32), pltpu.VMEM((OWNED + 8, COMP_BLK), f32)],
        compiler_params=small, name="rep_sum",
    )(slots, parts, over_sum)
    over_rep, atoms = tie((over_rep, atoms))
    ratios.append(call_ratio(atoms, comps, 1))
    parts = lax.all_to_all(over_rep.reshape(domains, share, COMP_BLK), "dom", 0, 0, tiled=True)
    parts, ratios[1] = tie((parts, ratios[1]))
    spread, mean = pl.pallas_call(
        adjoint_kernel,
        out_shape=(
            jax.ShapeDtypeStruct((domains, share, COMP_BLK), f32), jax.ShapeDtypeStruct((share, COMP_BLK), f32),
        ),
        in_specs=[vmem] * 3, out_specs=(vmem, vmem), compiler_params=small, name="adjoint",
    )(parts, target.reshape(-1, COMP_BLK), noise_sigma.reshape(-1, COMP_BLK))
    spread, atoms = tie((spread, atoms))
    ratios.append(call_ratio(atoms, comps, 2))
    over_dom = lax.all_to_all(spread, "dom", 0, 0, tiled=True).reshape(domains * share, COMP_BLK)
    over_dom, ratios[2] = tie((over_dom, ratios[2]))
    over_back = lax.cond(
        crowded,
        lambda v, unread: lax.all_to_all(
            jnp.broadcast_to(v[None], (replicas, OWNED, COMP_BLK)), "rep", 0, 0, tiled=True
        ).reshape(unread.shape),
        lambda v, unread: unread,
        over_dom,
        over,
    )
    spread = pl.pallas_call(
        spread_kernel,
        out_shape=pltpu.HBM((replicas, ROOM + share, COMP_BLK), f32),
        in_specs=[SMEM_SPEC, vmem, vmem], out_specs=HBM_SPEC,
        scratch_shapes=[pltpu.VMEM((ROOM + share, COMP_BLK), f32), pltpu.SemaphoreType.DMA((replicas,))],
        compiler_params=small, name="spread",
    )(slots, over_dom, mean)
    spread, atoms = tie((spread, atoms))
    ratios.append(call_ratio(atoms, comps, 3))
    returned = lax.all_to_all(spread, "rep", 0, 0, tiled=True)
    returned = returned.reshape(-1, COMP_BLK)

    forces, average = call_force(atoms_live, rows, positions, weights, comps, returned, over_back, ratios)
    return average.reshape(-1), forces.reshape(coords.shape)


def solution(mesh):
    return jax.shard_map(
        shards,
        mesh=mesh,
        in_specs=(
            P("rep", None, "dom"), P("dom"), P("dom"), P("dom"), P("dom", None), P(), P(), P(), P(), P("dom"), P("dom"),
        ),
        out_specs=(P("dom"), P("rep", None, "dom")),
        check_vma=False,
    )
```
